256 devices in a mesh: az: 16 (over x, y_lo, core), rad: 16 (over z, y_hi).
Axes of the slice: x: 4, y: 4 (y_hi: 2, y_lo: 2; y = y_hi * 2 + y_lo), z: 8, core: 2. Of those that a mesh axis runs over, the one named last changes fastest.
Arguments:
- density: float32 [16, 128, 4096], P(None, 'rad', 'az'), may hold values from 0.5 to 2
- velocity: float32 [3, 16, 128, 4096], P(None, None, 'rad', 'az'), may hold values from -1 to 1
- energy: float32 [16, 128, 4096], P(None, 'rad', 'az'), may hold values from 0.5 to 2
- shifts: int32 [128], P('rad'), may hold values from 0 to 4095
- fraction: float32 [128], P('rad'), may hold values from 0 to 1
Outputs:
- density_out: float32 [16, 128, 4096], P(None, 'rad', 'az')
- velocity_out: float32 [3, 16, 128, 4096], P(None, None, 'rad', 'az')
- energy_out: float32 [16, 128, 4096], P(None, 'rad', 'az')
The draws below stay inside these ranges and needn't reach their ends.
All inputs are finite; a program needn't handle non-finite values.
Results may differ from the reference program's by a relative error of at most 0.0003.
Values sent between devices are 32-bit elements; how exact they have to be, the bound alone decides.
A program may use at most 128 MiB of HBM per device.

```python
import math
import jax
import jax.numpy as jnp
from jax import lax

NTH = 16
STEPS = 2
NR = 128
NPHI = 4096


def place_ends(drawn, rng, low, largest):
    longest = drawn.shape.index(max(drawn.shape))
    spots = []
    for shift in (0, 1):
        where = [jax.random.randint(jax.random.fold_in(rng, axis), (), 0, length) for axis, length in enumerate(drawn.shape)]
        where[longest] = (where[longest] + shift) % drawn.shape[longest]
        spots.append(tuple(where))
    return drawn.at[spots[0]].set(low).at[spots[1]].set(largest)


def shard_levels(rng, shape, shards, least, high):
    def one(position, shards_of):
        steps = jax.random.uniform(jax.random.fold_in(jax.random.fold_in(rng, 6), position), (shards_of,), jnp.float32, least / len(shards), high / len(shards))
        return jnp.repeat(jnp.exp(steps), shape[position] // shards_of).reshape((-1,) + (1,) * (len(shape) - position - 1))

    level = one(*shards[0])
    for cut in shards[1:]:
        level = level * one(*cut)
    return level


def setup_inputs(seed: int = 0) -> dict:
    seeds = jax.random.split(jax.random.key(seed), 6)
    return {
        "density": jnp.clip(jnp.exp(math.log(2.0) - 1.3862944 * jax.random.uniform(seeds[0], (NTH, NR, NPHI), jnp.float32) ** shard_levels(seeds[0], (NTH, NR, NPHI), ((1, 16), (2, 16)), -0.2, 0.2)), 0.5, 2.0),
        "velocity": jnp.clip(jax.random.uniform(seeds[1], (3, NTH, NR, NPHI), jnp.float32, -1.0, 1.0) * shard_levels(seeds[1], (3, NTH, NR, NPHI), ((2, 16), (3, 16)), -0.4, 0.0), -1.0, 1.0),
        "energy": jnp.clip(jnp.exp(math.log(2.0) - 1.3862944 * jax.random.uniform(seeds[2], (NTH, NR, NPHI), jnp.float32) ** shard_levels(seeds[2], (NTH, NR, NPHI), ((1, 16), (2, 16)), -0.2, 0.2)), 0.5, 2.0),
        "shifts": place_ends(jax.random.randint(seeds[3], (NR,), 0, NPHI), jax.random.fold_in(seeds[3], 1), 0, NPHI - 1).astype(jnp.int32),
        "fraction": jnp.clip(1.0 * jax.random.uniform(seeds[4], (NR,), jnp.float32) ** shard_levels(seeds[4], (NR,), ((0, 16),), -0.2, 0.2), 0.0, 1.0),
    }


step_interval = 0.05
press_factor = 0.4


def with_rims(field_stack):
    wrapped = jnp.concatenate([field_stack[..., -1:], field_stack, field_stack[..., :1]], axis=3)
    return jnp.pad(wrapped, ((0, 0), (0, 0), (1, 1), (0, 0)))


def inner_cells(values):
    return values[..., 1:-1, 1:-1]


def azimuth_difference(values):
    return 0.5 * (values[..., 1:-1, 2:] - values[..., 1:-1, :-2])


def rad_diff(values):
    return 0.5 * (values[..., 2:, 1:-1] - values[..., :-2, 1:-1])


def theta_diff(values):
    padded = jnp.pad(values, ((1, 1), (0, 0), (0, 0)))
    return inner_cells(0.5 * (padded[2:] - padded[:-2]))


def source_update(bordered_field):
    gas_pressure = press_factor * bordered_field[4]
    gas_density = inner_cells(bordered_field[0])
    floored_density = jnp.where(gas_density > 0, gas_density, 1.0)
    azimuth_velocity = inner_cells(bordered_field[1]) - (step_interval * azimuth_difference(gas_pressure)) / floored_density
    radial_velocity = inner_cells(bordered_field[2]) - (step_interval * rad_diff(gas_pressure)) / floored_density
    polar_velocity = inner_cells(bordered_field[3]) - (step_interval * theta_diff(gas_pressure)) / floored_density
    compress = azimuth_difference(bordered_field[1]) + rad_diff(bordered_field[2]) + theta_diff(bordered_field[3])
    heating_term = inner_cells(bordered_field[4]) - step_interval * inner_cells(gas_pressure) * compress
    return jnp.stack([gas_density, azimuth_velocity, radial_velocity, polar_velocity, heating_term])


def face_fluxes(quantity, speed, axis_pos):
    count = quantity.shape[axis_pos]
    low_q = lax.slice_in_dim(quantity, 0, count - 1, axis=axis_pos)
    high_q = lax.slice_in_dim(quantity, 1, count, axis=axis_pos)
    low_u = lax.slice_in_dim(speed, 0, count - 1, axis=axis_pos)
    high_u = lax.slice_in_dim(speed, 1, count, axis=axis_pos)
    face_speed = 0.5 * (high_u + low_u)
    flux = step_interval * face_speed * jnp.where(face_speed > 0, low_q, high_q)
    faces = flux.shape[axis_pos]
    return lax.slice_in_dim(flux, 1, faces, axis=axis_pos) - lax.slice_in_dim(flux, 0, faces - 1, axis=axis_pos)


def transport_update(bordered_field):
    along_rows = bordered_field[:, :, 1:-1, :]
    div_phi = face_fluxes(along_rows, along_rows[1:2], 3)
    along_cols = bordered_field[:, :, :, 1:-1]
    div_rad = face_fluxes(along_cols, along_cols[2:3], 2)
    core = bordered_field[:, :, 1:-1, 1:-1]
    padded = jnp.pad(core, ((0, 0), (1, 1), (0, 0), (0, 0)))
    div_theta = face_fluxes(padded, padded[3:4], 1)
    return core - (div_phi + div_rad + div_theta)


def orbital_shift(moved, shifts, fraction):
    total = moved.shape[3]
    base = jnp.arange(total, dtype=jnp.int32)
    first_idx = (base[None, :] - shifts[:, None]) % total
    second_idx = (base[None, :] - shifts[:, None] - 1) % total
    first = jnp.take_along_axis(moved, jnp.broadcast_to(first_idx[None, None], moved.shape).astype(jnp.int32), axis=3)
    second = jnp.take_along_axis(moved, jnp.broadcast_to(second_idx[None, None], moved.shape).astype(jnp.int32), axis=3)
    weight = fraction[None, None, :, None]
    return (1.0 - weight) * first + weight * second


def reference(density, velocity, energy, shifts, fraction):
    state = jnp.concatenate([density[None], velocity, energy[None]], axis=0)
    for rounds in range(STEPS):
        fresh = source_update(with_rims(state))
        moved = transport_update(with_rims(fresh))
        state = orbital_shift(moved, shifts, fraction)
    return state[0], state[1:4], state[4]
```

```python
import jax
import jax.numpy as jnp
from jax import lax
from jax.experimental import pallas as pl
from jax.experimental.pallas import tpu as pltpu
from jax.sharding import PartitionSpec as P

MESH = pl.DeviceIdType.MESH
AZ = 16
QUADS = 32
CHUNKS = 32
STEPS = 2

VT, DE, EN, VR, VP = range(5)
F_VT, F_EN, F_VR, F_VP = range(4)


def owner(pair, half):
    return (pair // 2) * 4 + half * 2 + pair % 2


def prev_cell(x, lane):
    x1 = pltpu.roll(x, 1, 1)
    return jnp.where(lane == 0, pltpu.roll(x1, 1, 0), x1)


def next_cell(x, lane):
    x1 = pltpu.roll(x, 127, 1)
    return jnp.where(lane == 127, pltpu.roll(x1, CHUNKS - 1, 0), x1)


def kernel(
    den_ref, vel_ref, ene_ref, shift_ref, frac_ref,
    den_out, vel_out, ene_out,
    stage, rows, s0, s1, f0, f1, blended, ostage, back,
    a_send, a_recv, h_send, h_recv, b_send, b_recv, l_sem,
):
    a = lax.axis_index("az")
    rho = lax.axis_index("rad")
    half = (a // 2) % 2
    pair = (a // 4) * 2 + a % 2
    quad = 2 * rho + half
    states, fresh = (s0, s1), (f0, f1)

    for buf in (s0, s1, f0, f1):
        @pl.when(pair == 0)
        def _():
            buf[:, 0] = jnp.zeros_like(buf[:, 0])

        @pl.when(pair == 7)
        def _():
            buf[:, 3] = jnp.zeros_like(buf[:, 3])

        @pl.when(quad == 0)
        def _():
            buf[:, :, 0] = jnp.zeros_like(buf[:, :, 0])

        @pl.when(quad == QUADS - 1)
        def _():
            buf[:, :, 5] = jnp.zeros_like(buf[:, :, 5])

    barrier = pltpu.get_barrier_semaphore()
    for k in range(1, AZ):
        pl.semaphore_signal(barrier, inc=1, device_id={"az": (a + k) % AZ, "rad": rho}, device_id_type=MESH)
    cross = (quad + 2 * half - 1 + QUADS) % QUADS
    pl.semaphore_signal(
        barrier, inc=1, device_id={"az": owner(pair, cross % 2), "rad": cross // 2}, device_id_type=MESH
    )

    def regroup(tp, _):
        for h in range(2):
            dest = owner(tp, h)
            for f, src in (
                (VT, vel_ref.at[2]), (DE, den_ref), (EN, ene_ref), (VR, vel_ref.at[1]), (VP, vel_ref.at[0])
            ):
                for c in range(2):
                    for t in range(2):
                        stage[dest, f, pl.ds(c * 8 + t * 4, 4), :] = src[
                            2 * tp + t, pl.ds(4 * h, 4), pl.ds(128 * c, 128)
                        ]
        return 0

    lax.fori_loop(0, 8, regroup, 0)
    pl.semaphore_wait(barrier, AZ)

    def to_rows(k):
        dest = (a + k) % AZ
        return pltpu.make_async_remote_copy(
            src_ref=stage.at[dest],
            dst_ref=rows.at[:, pl.ds(a * 16, 16), :],
            send_sem=a_send.at[k],
            recv_sem=a_recv.at[k],
            device_id={"az": dest, "rad": rho},
            device_id_type=MESH,
        )

    for k in range(1, AZ):
        to_rows(k).start()
    own = pltpu.make_async_copy(stage.at[a], rows.at[:, pl.ds(a * 16, 16), :], l_sem.at[0])
    own.start()
    own.wait()
    for k in range(1, AZ):
        to_rows(k).wait_recv()

    def unpack(i, _):
        t, r = i // 4, i % 4
        for f in range(5):
            s0[f, t + 1, r + 1] = rows[f, pl.ds(i, CHUNKS, stride=8), :]
        return 0

    lax.fori_loop(0, 8, unpack, 0)

    lane = lax.broadcasted_iota(jnp.int32, (CHUNKS, 128), 1)
    lane8 = lax.broadcasted_iota(jnp.int32, (8, 128), 1)

    t_up, t_dn = (pair + 1) % 8, (pair + 7) % 8
    r_up, r_dn = (quad + 1) % QUADS, (quad + QUADS - 1) % QUADS
    has_tup, has_tdn = pair < 7, pair > 0
    has_rup, has_rdn = quad < QUADS - 1, quad > 0
    id_tup = {"az": owner(t_up, half), "rad": rho}
    id_tdn = {"az": owner(t_dn, half), "rad": rho}
    id_rup = {"az": owner(pair, r_up % 2), "rad": r_up // 2}
    id_rdn = {"az": owner(pair, r_dn % 2), "rad": r_dn // 2}

    def halo(buf, t_fields, r_fields, slot):
        def one(src, dst, ident, d):
            return pltpu.make_async_remote_copy(
                src_ref=src, dst_ref=dst, send_sem=h_send.at[slot, d], recv_sem=h_recv.at[slot, d],
                device_id=ident, device_id_type=MESH,
            )

        inner = pl.ds(1, 4)
        return (
            (one(buf.at[t_fields, 2, inner], buf.at[t_fields, 0, inner], id_tup, 0), has_tup, has_tdn),
            (one(buf.at[t_fields, 1, inner], buf.at[t_fields, 3, inner], id_tdn, 1), has_tdn, has_tup),
            (one(buf.at[r_fields, pl.ds(1, 2), 4], buf.at[r_fields, pl.ds(1, 2), 0], id_rup, 2), has_rup, has_rdn),
            (one(buf.at[r_fields, pl.ds(1, 2), 1], buf.at[r_fields, pl.ds(1, 2), 5], id_rdn, 3), has_rdn, has_rup),
        )

    def each(copies, what):
        for copy, sends, gets in copies:
            @pl.when(gets if what == "wait_recv" else sends)
            def _():
                getattr(copy, what)()

    pending = []
    for step in range(STEPS):
        s, f = states[step], fresh[step]
        first = halo(s, pl.ds(0, 3), pl.ds(1, 3), 2 * step)
        each(first, "start")
        each(first, "wait_recv")

        def source(i, _):
            t, r = i // 4 + 1, i % 4 + 1
            e = s[EN, t, r]
            vp = s[VP, t, r]
            den = s[DE, t, r]
            k = 0.01 / jnp.where(den > 0, den, 1.0)
            f[F_VP, t, r] = vp - k * (next_cell(e, lane) - prev_cell(e, lane))
            f[F_VR, t, r] = s[VR, t, r] - k * (s[EN, t, r + 1] - s[EN, t, r - 1])
            f[F_VT, t, r] = s[VT, t, r] - k * (s[EN, t + 1, r] - s[EN, t - 1, r])
            div = (
                (next_cell(vp, lane) - prev_cell(vp, lane))
                + (s[VR, t, r + 1] - s[VR, t, r - 1])
                + (s[VT, t + 1, r] - s[VT, t - 1, r])
            )
            f[F_EN, t, r] = e - 0.01 * e * div
            return 0

        lax.fori_loop(0, 8, source, 0)
        second = halo(f, pl.ds(0, 4), pl.ds(0, 4), 2 * step + 1)
        each(second, "start")
        each(second, "wait_recv")
        pending += [first, second]

        def transport(i, _):
            t, r = i // 4 + 1, i % 4 + 1
            w = frac_ref[half * 4 + i % 4]
            vp = f[F_VP, t, r]
            vr = f[F_VR, t, r]
            vt = f[F_VT, t, r]
            p_lo = vp + prev_cell(vp, lane)
            r_lo = vr + f[F_VR, t, r - 1]
            r_hi = vr + f[F_VR, t, r + 1]
            t_lo = vt + f[F_VT, t - 1, r]
            t_hi = vt + f[F_VT, t + 1, r]
            for field, buf, slot in (
                (VT, f, F_VT), (DE, s, DE), (EN, f, F_EN), (VR, f, F_VR), (VP, f, F_VP)
            ):
                q = buf[slot, t, r]
                along = p_lo * jnp.where(p_lo > 0, prev_cell(q, lane), q)
                out = next_cell(along, lane) - along
                out += r_hi * jnp.where(r_hi > 0, q, buf[slot, t, r + 1])
                out -= r_lo * jnp.where(r_lo > 0, buf[slot, t, r - 1], q)
                out += t_hi * jnp.where(t_hi > 0, q, buf[slot, t + 1, r])
                out -= t_lo * jnp.where(t_lo > 0, buf[slot, t - 1, r], q)
                moved = q - 0.025 * out
                b = (1.0 - w) * moved + w * prev_cell(moved, lane)
                blended[step, field, i, pl.ds(0, CHUNKS), :] = b
                blended[step, field, i, pl.ds(CHUNKS, 8), :] = b[:8]
            return 0

        lax.fori_loop(0, 8, transport, 0)

        def rotate(i, _):
            t, r = i // 4 + 1, i % 4 + 1
            ahead = (AZ * 256 - shift_ref[half * 4 + i % 4]) % (AZ * 256)
            whole, part = ahead // 128, ahead % 128
            back_by = (128 - part) % 128
            for field in range(5):
                for m in range(4):
                    x = blended[step, field, i, pl.ds((whole + 8 * m) % CHUNKS, 8), :]
                    y = blended[step, field, i, pl.ds((whole + 8 * m + 1) % CHUNKS, 8), :]
                    out = jnp.where(
                        lane8 < 128 - part, pltpu.roll(x, back_by, 1), pltpu.roll(y, back_by, 1)
                    )
                    if step == 0:
                        s1[field, t, r, pl.ds(8 * m, 8), :] = out
                    else:
                        ostage[field, pl.ds(64 * m + i, 8, stride=8), :] = out
            return 0

        lax.fori_loop(0, 8, rotate, 0)

    def to_blocks(k):
        dest = (a + k) % AZ
        return pltpu.make_async_remote_copy(
            src_ref=ostage.at[:, pl.ds(dest * 16, 16), :],
            dst_ref=back.at[a],
            send_sem=b_send.at[k],
            recv_sem=b_recv.at[k],
            device_id={"az": dest, "rad": rho},
            device_id_type=MESH,
        )

    for k in range(1, AZ):
        to_blocks(k).start()
    own = pltpu.make_async_copy(ostage.at[:, pl.ds(a * 16, 16), :], back.at[a], l_sem.at[1])
    own.start()
    own.wait()
    for k in range(1, AZ):
        to_blocks(k).wait_recv()

    def ungroup(tp, _):
        for h in range(2):
            src = owner(tp, h)
            for f, dst in (
                (VT, vel_out.at[2]), (DE, den_out), (EN, ene_out), (VR, vel_out.at[1]), (VP, vel_out.at[0])
            ):
                for c in range(2):
                    for t in range(2):
                        dst[2 * tp + t, pl.ds(4 * h, 4), pl.ds(128 * c, 128)] = back[
                            src, f, pl.ds(c * 8 + t * 4, 4), :
                        ]
        return 0

    lax.fori_loop(0, 8, ungroup, 0)

    for copies in pending:
        each(copies, "wait_send")
    for k in range(1, AZ):
        to_rows(k).wait_send()
        to_blocks(k).wait_send()


def shards(density, velocity, energy, shifts, fraction):
    vmem = pl.BlockSpec(memory_space=pltpu.VMEM)
    smem = pl.BlockSpec(memory_space=pltpu.SMEM)
    f32 = jnp.float32
    return pl.pallas_call(
        kernel,
        out_shape=tuple(jax.ShapeDtypeStruct(v.shape, f32) for v in (density, velocity, energy)),
        in_specs=[vmem, vmem, vmem, smem, smem],
        out_specs=(vmem, vmem, vmem),
        scratch_shapes=[
            pltpu.VMEM((AZ, 5, 16, 128), f32),
            pltpu.VMEM((5, 256, 128), f32),
            pltpu.VMEM((5, 4, 6, CHUNKS, 128), f32),
            pltpu.VMEM((5, 4, 6, CHUNKS, 128), f32),
            pltpu.VMEM((4, 4, 6, CHUNKS, 128), f32),
            pltpu.VMEM((4, 4, 6, CHUNKS, 128), f32),
            pltpu.VMEM((STEPS, 5, 8, CHUNKS + 8, 128), f32),
            pltpu.VMEM((5, 256, 128), f32),
            pltpu.VMEM((AZ, 5, 16, 128), f32),
            pltpu.SemaphoreType.DMA((AZ,)),
            pltpu.SemaphoreType.DMA((AZ,)),
            pltpu.SemaphoreType.DMA((2 * STEPS, 4)),
            pltpu.SemaphoreType.DMA((2 * STEPS, 4)),
            pltpu.SemaphoreType.DMA((AZ,)),
            pltpu.SemaphoreType.DMA((AZ,)),
            pltpu.SemaphoreType.DMA((2,)),
        ],
        compiler_params=pltpu.CompilerParams(
            collective_id=0, has_side_effects=True, vmem_limit_bytes=40 * 1024 * 1024
        ),
    )(density, velocity, energy, shifts, fraction)


def solution(mesh):
    placed = (
        P(None, "rad", "az"),
        P(None, None, "rad", "az"),
        P(None, "rad", "az"),
        P("rad"),
        P("rad"),
    )
    return jax.shard_map(
        shards,
        mesh=mesh,
        in_specs=placed,
        out_specs=(P(None, "rad", "az"), P(None, None, "rad", "az"), P(None, "rad", "az")),
        check_vma=False,
    )
```

```python
import jax
import jax.numpy as jnp
from jax import lax
from jax.experimental import pallas as pl
from jax.experimental.pallas import tpu as pltpu
from jax.sharding import PartitionSpec as P

MESH = pl.DeviceIdType.MESH
AZ = 16
QUADS = 32
CHUNKS = 32
CELLS = 4096
STEPS = 2

VT, EN, VR, DE, VP = range(5)
EARLY, LATE = (VT, EN, VR), (DE, VP)
GROUPS = (EARLY, LATE)
SPANS = (pl.ds(0, 3), pl.ds(3, 2))
S_VP = 3


def owner(pair, half):
    return lax.div(pair, 2) * 4 + half * 2 + lax.rem(pair, 2)


def prev_cell(x, lane):
    x1 = pltpu.roll(x, 1, 1)
    return jnp.where(lane == 0, pltpu.roll(x1, 1, 0), x1)


def next_cell(x, lane):
    x1 = pltpu.roll(x, 127, 1)
    return jnp.where(lane == 127, pltpu.roll(x1, CHUNKS - 1, 0), x1)


def kernel(
    den_hbm, vel_hbm, ene_hbm, shift_hbm, frac_hbm,
    back,
    den_ref, vel_ref, ene_ref, shift_ref, frac_ref,
    stage, rows, s0, s1, f0, f1, speed, flux, blended, ostage,
    a_send, a_recv, h_send, h_recv, b_send, b_recv, l_sem, i_sem,
):
    a = lax.axis_index("az")
    rho = lax.axis_index("rad")
    x, half, core = lax.div(a, 4), lax.rem(lax.div(a, 2), 2), lax.rem(a, 2)
    pair = 2 * x + core
    quad = 2 * rho + half
    states, fresh = (s0, s1), (f0, f1)

    loads = [
        pltpu.make_async_copy(src, dst, i_sem.at[n])
        for n, (src, dst) in enumerate((
            (ene_hbm, ene_ref), (vel_hbm, vel_ref), (den_hbm, den_ref), (shift_hbm, shift_ref), (frac_hbm, frac_ref)
        ))
    ]
    for copy in loads:
        copy.start()

    peers = []
    for k in range(AZ):
        dx, dy, dc = k // 4, (k // 2) % 2, k % 2
        peers.append(lax.rem(x + dx, 4) * 4 + lax.rem(half + dy, 2) * 2 + lax.rem(core + dc, 2))

    barrier = pltpu.get_barrier_semaphore()
    for k in range(1, AZ):
        pl.semaphore_signal(barrier, inc=1, device_id={"az": peers[k], "rad": rho}, device_id_type=MESH)
    cross = lax.rem(quad + 2 * half - 1 + QUADS, QUADS)
    pl.semaphore_signal(
        barrier, inc=1, device_id={"az": owner(pair, lax.rem(cross, 2)), "rad": lax.div(cross, 2)}, device_id_type=MESH
    )

    inner_t, inner_r = pl.ds(1, 2), pl.ds(1, 4)
    for buf, span in ((s0, pl.ds(0, 3)), (s1, pl.ds(0, 3)), (f0, pl.ds(0, 5)), (f1, pl.ds(0, 5))):
        def clear(where):
            buf[where] = jnp.zeros_like(buf[where])

        pl.when(pair == 0)(lambda: clear((span, 0, inner_r)))
        pl.when(pair == 7)(lambda: clear((span, 3, inner_r)))
        pl.when(quad == 0)(lambda: clear((span, inner_t, 0)))
        pl.when(quad == QUADS - 1)(lambda: clear((span, inner_t, 5)))

    sources = {VT: vel_ref.at[2], EN: ene_ref, VR: vel_ref.at[1], DE: den_ref, VP: vel_ref.at[0]}

    def regroup(fields):
        def one(tp, _):
            for h in range(2):
                dest = owner(tp, h)
                for f in fields:
                    for c in range(2):
                        for t in range(2):
                            stage[dest, f, pl.ds(c * 8 + t * 4, 4), :] = sources[f][
                                2 * tp + t, pl.ds(4 * h, 4), pl.ds(128 * c, 128)
                            ]
            return 0

        lax.fori_loop(0, 8, one, 0)

    def to_rows(k, g):
        dest = peers[k]
        return pltpu.make_async_remote_copy(
            src_ref=stage.at[dest, SPANS[g]],
            dst_ref=rows.at[SPANS[g], pl.ds(pl.multiple_of(a * 16, 16), 16), :],
            send_sem=a_send.at[g, k],
            recv_sem=a_recv.at[g, k],
            device_id={"az": dest, "rad": rho},
            device_id_type=MESH,
        )

    def own_rows(g):
        return pltpu.make_async_copy(
            stage.at[a, SPANS[g]], rows.at[SPANS[g], pl.ds(pl.multiple_of(a * 16, 16), 16), :], l_sem.at[g]
        )

    for copy in loads:
        copy.wait()
    regroup(EARLY)
    pl.semaphore_wait(barrier, AZ)
    for k in range(1, AZ):
        to_rows(k, 0).start()
    own_rows(0).start()
    regroup(LATE)
    for k in range(1, AZ):
        to_rows(k, 1).start()
    own_rows(1).start()

    lane = lax.broadcasted_iota(jnp.int32, (CHUNKS, 128), 1)
    lane8 = lax.broadcasted_iota(jnp.int32, (8, 128), 1)

    t_up, t_dn = lax.rem(pair + 1, 8), lax.rem(pair + 7, 8)
    r_up, r_dn = lax.rem(quad + 1, QUADS), lax.rem(quad + QUADS - 1, QUADS)
    has_tup, has_tdn = pair < 7, pair > 0
    has_rup, has_rdn = quad < QUADS - 1, quad > 0
    id_tup = {"az": owner(t_up, half), "rad": rho}
    id_tdn = {"az": owner(t_dn, half), "rad": rho}
    id_rup = {"az": owner(pair, lax.rem(r_up, 2)), "rad": lax.div(r_up, 2)}
    id_rdn = {"az": owner(pair, lax.rem(r_dn, 2)), "rad": lax.div(r_dn, 2)}

    def halo(buf, t_fields, r_fields, slot):
        def one(src, dst, ident, d):
            return pltpu.make_async_remote_copy(
                src_ref=src, dst_ref=dst, send_sem=h_send.at[slot, d], recv_sem=h_recv.at[slot, d],
                device_id=ident, device_id_type=MESH,
            )

        return (
            (one(buf.at[t_fields, 2, inner_r], buf.at[t_fields, 0, inner_r], id_tup, 0), has_tup, has_tdn),
            (one(buf.at[t_fields, 1, inner_r], buf.at[t_fields, 3, inner_r], id_tdn, 1), has_tdn, has_tup),
            (one(buf.at[r_fields, inner_t, 4], buf.at[r_fields, inner_t, 0], id_rup, 2), has_rup, has_rdn),
            (one(buf.at[r_fields, inner_t, 1], buf.at[r_fields, inner_t, 5], id_rdn, 3), has_rdn, has_rup),
        )

    def each(copies, what):
        for copy, sends, gets in copies:
            @pl.when(gets if what == "wait_recv" else sends)
            def _():
                getattr(copy, what)()

    def eight(body):
        def one(i, _):
            body(i, lax.div(i, 4) + 1, lax.rem(i, 4) + 1)
            return 0

        lax.fori_loop(0, 8, one, 0)

    def unpack(fields):
        def one(i, t, r):
            for q in fields:
                value = rows[q, pl.ds(i, CHUNKS, stride=8), :]
                if q == DE:
                    f0[DE, t, r] = value
                else:
                    s0[S_VP if q == VP else q, t, r] = value

        eight(one)

    def to_blocks(k, g):
        dest = peers[k]
        return pltpu.make_async_remote_copy(
            src_ref=ostage.at[SPANS[g], pl.ds(pl.multiple_of(dest * 16, 16), 16), :],
            dst_ref=back.at[a, SPANS[g]],
            send_sem=b_send.at[g, k],
            recv_sem=b_recv.at[g, k],
            device_id={"az": dest, "rad": rho},
            device_id_type=MESH,
        )

    def own_blocks(g):
        return pltpu.make_async_copy(
            ostage.at[SPANS[g], pl.ds(pl.multiple_of(a * 16, 16), 16), :], back.at[a, SPANS[g]], l_sem.at[2 + g]
        )

    plans = [
        (
            halo(states[step], pl.ds(0, 2), pl.ds(1, 2), 3 * step),
            halo(fresh[step], SPANS[1], SPANS[1], 3 * step + 1),
            halo(fresh[step], SPANS[0], SPANS[0], 3 * step + 2),
        )
        for step in range(STEPS)
    ]

    def along_azimuth(f, i, t, r, fields):
        p_lo = speed[i]
        for q in fields:
            v = f[q, t, r]
            low = p_lo * jnp.where(p_lo > 0, prev_cell(v, lane), v)
            flux[q, i] = next_cell(low, lane) - low

    def face(f, u, below, above):
        s = f[(u,) + below] + f[(u,) + above]
        up = s > 0
        return lambda q: s * jnp.where(up, f[(q,) + below], f[(q,) + above])

    for step in range(STEPS):
        s, f = states[step], fresh[step]
        first, late, early = plans[step]

        if step == 0:
            for k in range(1, AZ):
                to_rows(k, 0).wait_recv()
            own_rows(0).wait()
            unpack(EARLY)
            each(first, "start")
            for k in range(1, AZ):
                to_rows(k, 1).wait_recv()
            own_rows(1).wait()
            unpack(LATE)

        def source_azimuth(i, t, r):
            den = f[DE, t, r]
            k = 0.01 / jnp.where(den > 0, den, 1.0)
            e = s[EN, t, r]
            vp = s[S_VP, t, r]
            new = vp - k * (next_cell(e, lane) - prev_cell(e, lane))
            f[VP, t, r] = new
            flux[VT, i] = k
            flux[EN, i] = next_cell(vp, lane) - prev_cell(vp, lane)
            speed[i] = new + prev_cell(new, lane)

        eight(source_azimuth)
        each(late, "start")

        def azimuth_late(i, t, r):
            along_azimuth(f, i, t, r, LATE)

        eight(azimuth_late)
        each(first, "wait_recv")

        def source_rest(i, t, r):
            k = flux[VT, i]
            e = s[EN, t, r]
            f[VR, t, r] = s[VR, t, r] - k * (s[EN, t, r + 1] - s[EN, t, r - 1])
            f[VT, t, r] = s[VT, t, r] - k * (s[EN, t + 1, r] - s[EN, t - 1, r])
            div = (
                flux[EN, i]
                + (s[VR, t, r + 1] - s[VR, t, r - 1])
                + (s[VT, t + 1, r] - s[VT, t - 1, r])
            )
            f[EN, t, r] = e - 0.01 * e * div

        eight(source_rest)
        each(early, "start")

        def azimuth_early(i, t, r):
            along_azimuth(f, i, t, r, EARLY)

        eight(azimuth_early)

        def inner_radius(n, _):
            t, r = lax.div(n, 3), lax.rem(n, 3)
            one = face(f, VR, (t + 1, r + 1), (t + 1, r + 2))
            for q in range(5):
                v = one(q)
                flux[q, 4 * t + r] += v
                flux[q, 4 * t + r + 1] -= v
            return 0

        lax.fori_loop(0, 6, inner_radius, 0)

        def inner_theta(r, _):
            one = face(f, VT, (1, r + 1), (2, r + 1))
            for q in range(5):
                v = one(q)
                flux[q, r] += v
                flux[q, 4 + r] -= v
            return 0

        lax.fori_loop(0, 4, inner_theta, 0)

        each(late, "wait_recv")
        each(early, "wait_recv")

        for g, fields in enumerate(GROUPS):
            def outer_radius(t, _):
                low = face(f, VR, (t + 1, 0), (t + 1, 1))
                high = face(f, VR, (t + 1, 4), (t + 1, 5))
                for q in fields:
                    flux[q, 4 * t] -= low(q)
                    flux[q, 4 * t + 3] += high(q)
                return 0

            lax.fori_loop(0, 2, outer_radius, 0)

            def outer_theta(r, _):
                low = face(f, VT, (0, r + 1), (1, r + 1))
                high = face(f, VT, (2, r + 1), (3, r + 1))
                for q in fields:
                    flux[q, r] -= low(q)
                    flux[q, 4 + r] += high(q)
                return 0

            lax.fori_loop(0, 4, outer_theta, 0)

            def blend(i, t, r):
                w = frac_ref[half * 4 + r - 1]
                for q in fields:
                    moved = f[q, t, r] - 0.025 * flux[q, i]
                    b = (1.0 - w) * moved + w * prev_cell(moved, lane)
                    blended[q, i, pl.ds(0, CHUNKS), :] = b
                    blended[q, i, pl.ds(CHUNKS, 8), :] = b[:8]

            eight(blend)

            def rotate(i, t, r):
                ahead = lax.rem(CELLS - shift_ref[half * 4 + r - 1], CELLS)
                whole, part = lax.div(ahead, 128), lax.rem(ahead, 128)
                back_by = lax.rem(128 - part, 128)
                for q in fields:
                    for m in range(4):
                        near = blended[q, i, pl.ds(lax.rem(whole + 8 * m, CHUNKS), 8), :]
                        far = blended[q, i, pl.ds(lax.rem(whole + 8 * m + 1, CHUNKS), 8), :]
                        out = jnp.where(
                            lane8 < 128 - part, pltpu.roll(near, back_by, 1), pltpu.roll(far, back_by, 1)
                        )
                        if step == STEPS - 1:
                            ostage[q, pl.ds(64 * m + i, 8, stride=8), :] = out
                        elif q == DE:
                            f1[DE, t, r, pl.ds(8 * m, 8), :] = out
                        else:
                            s1[S_VP if q == VP else q, t, r, pl.ds(8 * m, 8), :] = out

            eight(rotate)
            if step == STEPS - 1:
                for k in range(1, AZ):
                    to_blocks(k, g).start()
                own_blocks(g).start()
            elif g == 0:
                each(plans[step + 1][0], "start")

    for step in range(STEPS):
        for copies in plans[step]:
            each(copies, "wait_send")
    for g in range(2):
        for k in range(1, AZ):
            to_rows(k, g).wait_send()
            to_blocks(k, g).wait_send()
    for g in range(2):
        own_blocks(g).wait()
        for k in range(1, AZ):
            to_blocks(k, g).wait_recv()


def write_out(back, den_hbm, vel_hbm, ene_hbm, blocks, den_out, vel_out, ene_out, in_sem, out_sem):
    targets = {
        VT: (vel_out.at[2], vel_hbm.at[2]), EN: (ene_out, ene_hbm), VR: (vel_out.at[1], vel_hbm.at[1]),
        DE: (den_out, den_hbm), VP: (vel_out.at[0], vel_hbm.at[0]),
    }
    reads = [pltpu.make_async_copy(back.at[:, q], blocks.at[:, q], in_sem.at[q]) for q in range(5)]
    for copy in reads:
        copy.start()
    writes = []
    for q in range(5):
        reads[q].wait()
        dst = targets[q][0]

        def one(tp, _):
            for h in range(2):
                src = owner(tp, h)
                for c in range(2):
                    for t in range(2):
                        dst[2 * tp + t, pl.ds(4 * h, 4), pl.ds(128 * c, 128)] = blocks[
                            src, q, pl.ds(c * 8 + t * 4, 4), :
                        ]
            return 0

        lax.fori_loop(0, 8, one, 0)
        writes.append(pltpu.make_async_copy(*targets[q], out_sem.at[q]))
        writes[-1].start()
    for copy in writes:
        copy.wait()


def shards(density, velocity, energy, shifts, fraction):
    hbm = pl.BlockSpec(memory_space=pl.ANY)
    f32 = jnp.float32
    limit = 60 * 1024 * 1024
    block = (AZ, 5, 16, 128)
    dma = pltpu.SemaphoreType.DMA
    fields = [pltpu.VMEM(v.shape, f32) for v in (density, velocity, energy)]
    back = pl.pallas_call(
        kernel,
        out_shape=jax.ShapeDtypeStruct(block, f32),
        in_specs=[hbm] * 5,
        out_specs=hbm,
        scratch_shapes=fields + [
            pltpu.SMEM(shifts.shape, jnp.int32),
            pltpu.SMEM(fraction.shape, f32),
            pltpu.VMEM(block, f32),
            pltpu.VMEM((5, 256, 128), f32),
            pltpu.VMEM((4, 4, 6, CHUNKS, 128), f32),
            pltpu.VMEM((4, 4, 6, CHUNKS, 128), f32),
            pltpu.VMEM((5, 4, 6, CHUNKS, 128), f32),
            pltpu.VMEM((5, 4, 6, CHUNKS, 128), f32),
            pltpu.VMEM((8, CHUNKS, 128), f32),
            pltpu.VMEM((5, 8, CHUNKS, 128), f32),
            pltpu.VMEM((5, 8, CHUNKS + 8, 128), f32),
            pltpu.VMEM((5, 256, 128), f32),
            dma((2, AZ)),
            dma((2, AZ)),
            dma((3 * STEPS, 4)),
            dma((3 * STEPS, 4)),
            dma((2, AZ)),
            dma((2, AZ)),
            dma((4,)),
            dma((5,)),
        ],
        compiler_params=pltpu.CompilerParams(collective_id=0, has_side_effects=True, vmem_limit_bytes=limit),
    )(density, velocity, energy, shifts, fraction)
    return pl.pallas_call(
        write_out,
        out_shape=tuple(jax.ShapeDtypeStruct(v.shape, f32) for v in (density, velocity, energy)),
        in_specs=[hbm],
        out_specs=(hbm,) * 3,
        scratch_shapes=[pltpu.VMEM(block, f32)] + fields + [dma((5,)), dma((5,))],
        compiler_params=pltpu.CompilerParams(vmem_limit_bytes=limit),
    )(back)


def solution(mesh):
    placed = (
        P(None, "rad", "az"),
        P(None, None, "rad", "az"),
        P(None, "rad", "az"),
        P("rad"),
        P("rad"),
    )
    return jax.shard_map(
        shards,
        mesh=mesh,
        in_specs=placed,
        out_specs=(P(None, "rad", "az"), P(None, None, "rad", "az"), P(None, "rad", "az")),
        check_vma=False,
    )
```

```python
import jax
import jax.numpy as jnp
from jax import lax
from jax.experimental import pallas as pl
from jax.experimental.pallas import tpu as pltpu
from jax.sharding import PartitionSpec as P

MESH = pl.DeviceIdType.MESH
AZ = 16
QUADS = 32
CHUNKS = 32
CELLS = 4096
STEPS = 2

VT, EN, VR, DE, VP = range(5)
EARLY, LATE = (VT, EN, VR), (DE, VP)
GROUPS = (EARLY, LATE)
SPANS = (pl.ds(0, 3), pl.ds(3, 2))
S_VP = 3
UNROLL = 8
ORDER = (8, 4, 12, 2, 9, 5, 13, 3, 10, 6, 14, 1, 11, 7, 15)


def owner(pair, half):
    return lax.div(pair, 2) * 4 + half * 2 + lax.rem(pair, 2)


def prev_cell(x, lane):
    x1 = pltpu.roll(x, 1, 1)
    return jnp.where(lane == 0, pltpu.roll(x1, 1, 0), x1)


def next_cell(x, lane):
    x1 = pltpu.roll(x, 127, 1)
    return jnp.where(lane == 127, pltpu.roll(x1, CHUNKS - 1, 0), x1)


def kernel(
    den_hbm, vel_hbm, ene_hbm, shift_hbm, frac_hbm,
    back,
    den_ref, vel_ref, ene_ref, shift_ref, frac_ref,
    stage, rows, s0, s1, f0, f1, speed, flux, blended, ostage,
    a_send, a_recv, h_send, h_recv, b_send, b_recv, l_sem, i_sem,
):
    a = lax.axis_index("az")
    rho = lax.axis_index("rad")
    x, half, core = lax.div(a, 4), lax.rem(lax.div(a, 2), 2), lax.rem(a, 2)
    pair = 2 * x + core
    quad = 2 * rho + half
    states, fresh = (s0, s1), (f0, f1)

    loads = [
        pltpu.make_async_copy(src, dst, i_sem.at[n])
        for n, (src, dst) in enumerate((
            (ene_hbm, ene_ref), (vel_hbm, vel_ref), (den_hbm, den_ref), (shift_hbm, shift_ref), (frac_hbm, frac_ref)
        ))
    ]
    for copy in loads:
        copy.start()

    peers = []
    for k in range(AZ):
        dx, dy, dc = k // 4, (k // 2) % 2, k % 2
        peers.append(lax.rem(x + dx, 4) * 4 + lax.rem(half + dy, 2) * 2 + lax.rem(core + dc, 2))

    barrier = pltpu.get_barrier_semaphore()
    for k in range(1, AZ):
        pl.semaphore_signal(barrier, inc=1, device_id={"az": peers[k], "rad": rho}, device_id_type=MESH)
    cross = lax.rem(quad + 2 * half - 1 + QUADS, QUADS)
    pl.semaphore_signal(
        barrier, inc=1, device_id={"az": owner(pair, lax.rem(cross, 2)), "rad": lax.div(cross, 2)}, device_id_type=MESH
    )

    inner_t, inner_r = pl.ds(1, 2), pl.ds(1, 4)
    for buf, span in ((s0, pl.ds(0, 3)), (s1, pl.ds(0, 3)), (f0, pl.ds(0, 5)), (f1, pl.ds(0, 5))):
        def clear(where):
            buf[where] = jnp.zeros_like(buf[where])

        pl.when(pair == 0)(lambda: clear((span, 0, inner_r)))
        pl.when(pair == 7)(lambda: clear((span, 3, inner_r)))
        pl.when(quad == 0)(lambda: clear((span, inner_t, 0)))
        pl.when(quad == QUADS - 1)(lambda: clear((span, inner_t, 5)))

    sources = {VT: vel_ref.at[2], EN: ene_ref, VR: vel_ref.at[1], DE: den_ref, VP: vel_ref.at[0]}

    def regroup(fields):
        def one(tp, _):
            for h in range(2):
                dest = owner(tp, h)
                for f in fields:
                    for c in range(2):
                        for t in range(2):
                            stage[dest, f, pl.ds(c * 8 + t * 4, 4), :] = sources[f][
                                2 * tp + t, pl.ds(4 * h, 4), pl.ds(128 * c, 128)
                            ]
            return 0

        lax.fori_loop(0, 8, one, 0)

    def to_rows(k, g):
        dest = peers[k]
        return pltpu.make_async_remote_copy(
            src_ref=stage.at[dest, SPANS[g]],
            dst_ref=rows.at[SPANS[g], pl.ds(pl.multiple_of(a * 16, 16), 16), :],
            send_sem=a_send.at[g, k],
            recv_sem=a_recv.at[g, k],
            device_id={"az": dest, "rad": rho},
            device_id_type=MESH,
        )

    def own_rows(g):
        return pltpu.make_async_copy(
            stage.at[a, SPANS[g]], rows.at[SPANS[g], pl.ds(pl.multiple_of(a * 16, 16), 16), :], l_sem.at[g]
        )

    for copy in loads:
        copy.wait()
    regroup(EARLY)
    pl.semaphore_wait(barrier, AZ)
    for k in ORDER:
        to_rows(k, 0).start()
    own_rows(0).start()
    regroup(LATE)
    for k in ORDER:
        to_rows(k, 1).start()
    own_rows(1).start()

    lane = lax.broadcasted_iota(jnp.int32, (CHUNKS, 128), 1)
    lane8 = lax.broadcasted_iota(jnp.int32, (8, 128), 1)

    t_up, t_dn = lax.rem(pair + 1, 8), lax.rem(pair + 7, 8)
    r_up, r_dn = lax.rem(quad + 1, QUADS), lax.rem(quad + QUADS - 1, QUADS)
    has_tup, has_tdn = pair < 7, pair > 0
    has_rup, has_rdn = quad < QUADS - 1, quad > 0
    id_tup = {"az": owner(t_up, half), "rad": rho}
    id_tdn = {"az": owner(t_dn, half), "rad": rho}
    id_rup = {"az": owner(pair, lax.rem(r_up, 2)), "rad": lax.div(r_up, 2)}
    id_rdn = {"az": owner(pair, lax.rem(r_dn, 2)), "rad": lax.div(r_dn, 2)}

    def halo(buf, t_fields, r_fields, slot):
        def one(src, dst, ident, d):
            return pltpu.make_async_remote_copy(
                src_ref=src, dst_ref=dst, send_sem=h_send.at[slot, d], recv_sem=h_recv.at[slot, d],
                device_id=ident, device_id_type=MESH,
            )

        return (
            (one(buf.at[t_fields, 2, inner_r], buf.at[t_fields, 0, inner_r], id_tup, 0), has_tup, has_tdn),
            (one(buf.at[t_fields, 1, inner_r], buf.at[t_fields, 3, inner_r], id_tdn, 1), has_tdn, has_tup),
            (one(buf.at[r_fields, inner_t, 4], buf.at[r_fields, inner_t, 0], id_rup, 2), has_rup, has_rdn),
            (one(buf.at[r_fields, inner_t, 1], buf.at[r_fields, inner_t, 5], id_rdn, 3), has_rdn, has_rup),
        )

    def each(copies, what):
        for copy, sends, gets in copies:
            @pl.when(gets if what == "wait_recv" else sends)
            def _():
                getattr(copy, what)()

    def eight(body, unroll=1):
        def one(i, _):
            body(i, lax.div(i, 4) + 1, lax.rem(i, 4) + 1)
            return 0

        lax.fori_loop(0, 8, one, 0, unroll=unroll)

    def unpack(fields):
        def one(i, t, r):
            for q in fields:
                value = rows[q, pl.ds(i, CHUNKS, stride=8), :]
                if q == DE:
                    f0[DE, t, r] = value
                else:
                    s0[S_VP if q == VP else q, t, r] = value

        eight(one)

    def to_blocks(k, g):
        dest = peers[k]
        return pltpu.make_async_remote_copy(
            src_ref=ostage.at[SPANS[g], pl.ds(pl.multiple_of(dest * 16, 16), 16), :],
            dst_ref=back.at[a, SPANS[g]],
            send_sem=b_send.at[g, k],
            recv_sem=b_recv.at[g, k],
            device_id={"az": dest, "rad": rho},
            device_id_type=MESH,
        )

    def own_blocks(g):
        return pltpu.make_async_copy(
            ostage.at[SPANS[g], pl.ds(pl.multiple_of(a * 16, 16), 16), :], back.at[a, SPANS[g]], l_sem.at[2 + g]
        )

    plans = [
        (
            halo(states[step], pl.ds(0, 2), pl.ds(1, 2), 3 * step),
            halo(fresh[step], SPANS[1], SPANS[1], 3 * step + 1),
            halo(fresh[step], SPANS[0], SPANS[0], 3 * step + 2),
        )
        for step in range(STEPS)
    ]

    def along_azimuth(f, i, t, r, fields):
        p_lo = speed[i]
        for q in fields:
            v = f[q, t, r]
            low = p_lo * jnp.where(p_lo > 0, prev_cell(v, lane), v)
            flux[q, i] = next_cell(low, lane) - low

    def face(f, u, below, above):
        s = f[(u,) + below] + f[(u,) + above]
        up = s > 0
        return lambda q: s * jnp.where(up, f[(q,) + below], f[(q,) + above])

    for step in range(STEPS):
        s, f = states[step], fresh[step]
        first, late, early = plans[step]

        if step == 0:
            for k in range(1, AZ):
                to_rows(k, 0).wait_recv()
            own_rows(0).wait()
            unpack(EARLY)
            each(first, "start")
            for k in range(1, AZ):
                to_rows(k, 1).wait_recv()
            own_rows(1).wait()
            unpack(LATE)

        def source_azimuth(i, t, r):
            den = f[DE, t, r]
            k = 0.01 / jnp.where(den > 0, den, 1.0)
            e = s[EN, t, r]
            vp = s[S_VP, t, r]
            new = vp - k * (next_cell(e, lane) - prev_cell(e, lane))
            f[VP, t, r] = new
            flux[VT, i] = k
            flux[EN, i] = next_cell(vp, lane) - prev_cell(vp, lane)
            speed[i] = new + prev_cell(new, lane)

        eight(source_azimuth, UNROLL)
        each(late, "start")

        def azimuth_late(i, t, r):
            along_azimuth(f, i, t, r, LATE)

        eight(azimuth_late)
        each(first, "wait_recv")

        def source_rest(i, t, r):
            k = flux[VT, i]
            e = s[EN, t, r]
            f[VR, t, r] = s[VR, t, r] - k * (s[EN, t, r + 1] - s[EN, t, r - 1])
            f[VT, t, r] = s[VT, t, r] - k * (s[EN, t + 1, r] - s[EN, t - 1, r])
            div = (
                flux[EN, i]
                + (s[VR, t, r + 1] - s[VR, t, r - 1])
                + (s[VT, t + 1, r] - s[VT, t - 1, r])
            )
            f[EN, t, r] = e - 0.01 * e * div

        eight(source_rest, UNROLL)
        each(early, "start")

        def azimuth_early(i, t, r):
            along_azimuth(f, i, t, r, EARLY)

        eight(azimuth_early)

        def inner_radius(n, _):
            t, r = lax.div(n, 3), lax.rem(n, 3)
            one = face(f, VR, (t + 1, r + 1), (t + 1, r + 2))
            for q in range(5):
                v = one(q)
                flux[q, 4 * t + r] += v
                flux[q, 4 * t + r + 1] -= v
            return 0

        lax.fori_loop(0, 6, inner_radius, 0)

        def inner_theta(r, _):
            one = face(f, VT, (1, r + 1), (2, r + 1))
            for q in range(5):
                v = one(q)
                flux[q, r] += v
                flux[q, 4 + r] -= v
            return 0

        lax.fori_loop(0, 4, inner_theta, 0)

        each(late, "wait_recv")
        each(early, "wait_recv")

        for g in ((0, 1) if step < STEPS - 1 else (1, 0)):
            fields = GROUPS[g]

            def outer_radius(t, _):
                low = face(f, VR, (t + 1, 0), (t + 1, 1))
                high = face(f, VR, (t + 1, 4), (t + 1, 5))
                for q in fields:
                    flux[q, 4 * t] -= low(q)
                    flux[q, 4 * t + 3] += high(q)
                return 0

            lax.fori_loop(0, 2, outer_radius, 0)

            def outer_theta(r, _):
                low = face(f, VT, (0, r + 1), (1, r + 1))
                high = face(f, VT, (2, r + 1), (3, r + 1))
                for q in fields:
                    flux[q, r] -= low(q)
                    flux[q, 4 + r] += high(q)
                return 0

            lax.fori_loop(0, 4, outer_theta, 0)

            def finish(i, t, r):
                for q in fields:
                    moved = f[q, t, r] - 0.025 * flux[q, i]
                    blended[q, i, pl.ds(0, CHUNKS), :] = moved
                    blended[q, i, pl.ds(CHUNKS, 8), :] = moved[:8]

            eight(finish, UNROLL)

            def rotate(i, t, r):
                w = frac_ref[half * 4 + r - 1]
                shift = shift_ref[half * 4 + r - 1]
                views = []
                for back_cells in (0, 1):
                    ahead = lax.rem(2 * CELLS - shift - back_cells, CELLS)
                    views.append((lax.div(ahead, 128), lax.rem(ahead, 128)))
                for q in fields:
                    for m in range(4):
                        parts = []
                        for whole, part in views:
                            near = blended[q, i, pl.ds(lax.rem(whole + 8 * m, CHUNKS), 8), :]
                            far = blended[q, i, pl.ds(lax.rem(whole + 8 * m + 1, CHUNKS), 8), :]
                            parts.append(pltpu.roll(jnp.where(lane8 < part, far, near), lax.rem(128 - part, 128), 1))
                        out = (1.0 - w) * parts[0] + w * parts[1]
                        if step == STEPS - 1:
                            ostage[q, pl.ds(64 * m + i, 8, stride=8), :] = out
                        elif q == DE:
                            f1[DE, t, r, pl.ds(8 * m, 8), :] = out
                        else:
                            s1[S_VP if q == VP else q, t, r, pl.ds(8 * m, 8), :] = out

            eight(rotate, UNROLL)
            if step == STEPS - 1:
                for k in ORDER:
                    to_blocks(k, g).start()
                own_blocks(g).start()
            elif g == 0:
                each(plans[step + 1][0], "start")

    for step in range(STEPS):
        for copies in plans[step]:
            each(copies, "wait_send")
    for g in range(2):
        for k in range(1, AZ):
            to_rows(k, g).wait_send()
            to_blocks(k, g).wait_send()
    for g in range(2):
        own_blocks(g).wait()
        for k in range(1, AZ):
            to_blocks(k, g).wait_recv()


def write_out(back, den_hbm, vel_hbm, ene_hbm, blocks, den_out, vel_out, ene_out, in_sem, out_sem):
    targets = {
        VT: (vel_out.at[2], vel_hbm.at[2]), EN: (ene_out, ene_hbm), VR: (vel_out.at[1], vel_hbm.at[1]),
        DE: (den_out, den_hbm), VP: (vel_out.at[0], vel_hbm.at[0]),
    }
    reads = [pltpu.make_async_copy(back.at[:, q], blocks.at[:, q], in_sem.at[q]) for q in range(5)]
    for copy in reads:
        copy.start()
    writes = []
    for q in range(5):
        reads[q].wait()
        dst = targets[q][0]

        def one(tp, _):
            for h in range(2):
                src = owner(tp, h)
                for c in range(2):
                    for t in range(2):
                        dst[2 * tp + t, pl.ds(4 * h, 4), pl.ds(128 * c, 128)] = blocks[
                            src, q, pl.ds(c * 8 + t * 4, 4), :
                        ]
            return 0

        lax.fori_loop(0, 8, one, 0)
        writes.append(pltpu.make_async_copy(*targets[q], out_sem.at[q]))
        writes[-1].start()
    for copy in writes:
        copy.wait()


def shards(density, velocity, energy, shifts, fraction):
    hbm = pl.BlockSpec(memory_space=pl.ANY)
    f32 = jnp.float32
    limit = 60 * 1024 * 1024
    block = (AZ, 5, 16, 128)
    dma = pltpu.SemaphoreType.DMA
    fields = [pltpu.VMEM(v.shape, f32) for v in (density, velocity, energy)]
    back = pl.pallas_call(
        kernel,
        out_shape=jax.ShapeDtypeStruct(block, f32),
        in_specs=[hbm] * 5,
        out_specs=hbm,
        scratch_shapes=fields + [
            pltpu.SMEM(shifts.shape, jnp.int32),
            pltpu.SMEM(fraction.shape, f32),
            pltpu.VMEM(block, f32),
            pltpu.VMEM((5, 256, 128), f32),
            pltpu.VMEM((4, 4, 6, CHUNKS, 128), f32),
            pltpu.VMEM((4, 4, 6, CHUNKS, 128), f32),
            pltpu.VMEM((5, 4, 6, CHUNKS, 128), f32),
            pltpu.VMEM((5, 4, 6, CHUNKS, 128), f32),
            pltpu.VMEM((8, CHUNKS, 128), f32),
            pltpu.VMEM((5, 8, CHUNKS, 128), f32),
            pltpu.VMEM((5, 8, CHUNKS + 8, 128), f32),
            pltpu.VMEM((5, 256, 128), f32),
            dma((2, AZ)),
            dma((2, AZ)),
            dma((3 * STEPS, 4)),
            dma((3 * STEPS, 4)),
            dma((2, AZ)),
            dma((2, AZ)),
            dma((4,)),
            dma((5,)),
        ],
        compiler_params=pltpu.CompilerParams(collective_id=0, has_side_effects=True, vmem_limit_bytes=limit),
    )(density, velocity, energy, shifts, fraction)
    return pl.pallas_call(
        write_out,
        out_shape=tuple(jax.ShapeDtypeStruct(v.shape, f32) for v in (density, velocity, energy)),
        in_specs=[hbm],
        out_specs=(hbm,) * 3,
        scratch_shapes=[pltpu.VMEM(block, f32)] + fields + [dma((5,)), dma((5,))],
        compiler_params=pltpu.CompilerParams(vmem_limit_bytes=limit),
    )(back)


def solution(mesh):
    placed = (
        P(None, "rad", "az"),
        P(None, None, "rad", "az"),
        P(None, "rad", "az"),
        P("rad"),
        P("rad"),
    )
    return jax.shard_map(
        shards,
        mesh=mesh,
        in_specs=placed,
        out_specs=(P(None, "rad", "az"), P(None, None, "rad", "az"), P(None, "rad", "az")),
        check_vma=False,
    )
```

```python
import jax
import jax.numpy as jnp
from jax import lax
from jax.experimental import pallas as pl
from jax.experimental.pallas import tpu as pltpu
from jax.sharding import PartitionSpec as P

MESH = pl.DeviceIdType.MESH
AZ = 16
QUADS = 32
CHUNKS = 32
CELLS = 4096
STEPS = 2

EN, VT, VR, DE, VP = range(5)
EARLY, LATE = (EN, VT, VR), (DE, VP)
GROUPS = (EARLY, LATE)
SPANS = (pl.ds(0, 3), pl.ds(3, 2))
S_VP = 3
UNROLL = 8
ORDER = (8, 4, 12, 2, 9, 5, 13, 3, 10, 6, 14, 1, 11, 7, 15)


def owner(pair, half):
    return lax.div(pair, 2) * 4 + half * 2 + lax.rem(pair, 2)


def prev_cell(x, lane):
    x1 = pltpu.roll(x, 1, 1)
    return jnp.where(lane == 0, pltpu.roll(x1, 1, 0), x1)


def next_cell(x, lane):
    x1 = pltpu.roll(x, 127, 1)
    return jnp.where(lane == 127, pltpu.roll(x1, CHUNKS - 1, 0), x1)


def kernel(
    den_hbm, vel_hbm, ene_hbm, shift_hbm, frac_hbm,
    back,
    den_ref, vel_ref, ene_ref, shift_ref, frac_ref,
    stage, rows, s0, s1, f0, f1, speed, flux, blended, ostage,
    a_send, a_recv, h_send, h_recv, b_send, b_recv, l_sem, i_sem,
):
    a = lax.axis_index("az")
    rho = lax.axis_index("rad")
    x, half, core = lax.div(a, 4), lax.rem(lax.div(a, 2), 2), lax.rem(a, 2)
    pair = 2 * x + core
    quad = 2 * rho + half
    states, fresh = (s0, s1), (f0, f1)

    loads = [
        pltpu.make_async_copy(src, dst, i_sem.at[n])
        for n, (src, dst) in enumerate((
            (ene_hbm, ene_ref), (vel_hbm, vel_ref), (den_hbm, den_ref), (shift_hbm, shift_ref), (frac_hbm, frac_ref)
        ))
    ]
    for copy in loads:
        copy.start()

    peers = []
    for k in range(AZ):
        dx, dy, dc = k // 4, (k // 2) % 2, k % 2
        peers.append(lax.rem(x + dx, 4) * 4 + lax.rem(half + dy, 2) * 2 + lax.rem(core + dc, 2))

    barrier = pltpu.get_barrier_semaphore()
    for k in range(1, AZ):
        pl.semaphore_signal(barrier, inc=1, device_id={"az": peers[k], "rad": rho}, device_id_type=MESH)
    cross = lax.rem(quad + 2 * half - 1 + QUADS, QUADS)
    has_cross = jnp.logical_and(quad > 0, quad < QUADS - 1)

    @pl.when(has_cross)
    def _():
        pl.semaphore_signal(
            barrier, inc=1, device_id={"az": owner(pair, lax.rem(cross, 2)), "rad": lax.div(cross, 2)},
            device_id_type=MESH,
        )

    inner_t, inner_r = pl.ds(1, 2), pl.ds(1, 4)
    for buf, span in ((s0, pl.ds(0, 3)), (s1, pl.ds(0, 3)), (f0, pl.ds(0, 5)), (f1, pl.ds(0, 5))):
        def clear(where):
            buf[where] = jnp.zeros_like(buf[where])

        pl.when(pair == 0)(lambda: clear((span, 0, inner_r)))
        pl.when(pair == 7)(lambda: clear((span, 3, inner_r)))
        pl.when(quad == 0)(lambda: clear((span, inner_t, 0)))
        pl.when(quad == QUADS - 1)(lambda: clear((span, inner_t, 5)))

    sources = {VT: vel_ref.at[2], EN: ene_ref, VR: vel_ref.at[1], DE: den_ref, VP: vel_ref.at[0]}

    def regroup(fields):
        def one(tp, _):
            for h in range(2):
                dest = owner(tp, h)
                for f in fields:
                    for c in range(2):
                        for t in range(2):
                            stage[dest, f, pl.ds(c * 8 + t * 4, 4), :] = sources[f][
                                2 * tp + t, pl.ds(4 * h, 4), pl.ds(128 * c, 128)
                            ]
            return 0

        lax.fori_loop(0, 8, one, 0)

    def to_rows(k, g):
        dest = peers[k]
        return pltpu.make_async_remote_copy(
            src_ref=stage.at[dest, SPANS[g]],
            dst_ref=rows.at[SPANS[g], pl.ds(pl.multiple_of(a * 16, 16), 16), :],
            send_sem=a_send.at[g, k],
            recv_sem=a_recv.at[g, k],
            device_id={"az": dest, "rad": rho},
            device_id_type=MESH,
        )

    def own_rows(g):
        return pltpu.make_async_copy(
            stage.at[a, SPANS[g]], rows.at[SPANS[g], pl.ds(pl.multiple_of(a * 16, 16), 16), :], l_sem.at[g]
        )

    for copy in loads:
        copy.wait()
    regroup(EARLY)
    pl.semaphore_wait(barrier, AZ - 1 + has_cross.astype(jnp.int32))
    for k in ORDER:
        to_rows(k, 0).start()
    own_rows(0).start()
    regroup(LATE)
    for k in ORDER:
        to_rows(k, 1).start()
    own_rows(1).start()

    lane = lax.broadcasted_iota(jnp.int32, (CHUNKS, 128), 1)
    lane8 = lax.broadcasted_iota(jnp.int32, (8, 128), 1)

    t_up, t_dn = lax.rem(pair + 1, 8), lax.rem(pair + 7, 8)
    r_up, r_dn = lax.rem(quad + 1, QUADS), lax.rem(quad + QUADS - 1, QUADS)
    has_tup, has_tdn = pair < 7, pair > 0
    has_rup, has_rdn = quad < QUADS - 1, quad > 0
    id_tup = {"az": owner(t_up, half), "rad": rho}
    id_tdn = {"az": owner(t_dn, half), "rad": rho}
    id_rup = {"az": owner(pair, lax.rem(r_up, 2)), "rad": lax.div(r_up, 2)}
    id_rdn = {"az": owner(pair, lax.rem(r_dn, 2)), "rad": lax.div(r_dn, 2)}

    def halo(buf, t_fields, r_fields, slot):
        def one(src, dst, ident, d):
            return pltpu.make_async_remote_copy(
                src_ref=src, dst_ref=dst, send_sem=h_send.at[slot, d], recv_sem=h_recv.at[slot, d],
                device_id=ident, device_id_type=MESH,
            )

        return (
            (one(buf.at[t_fields, 2, inner_r], buf.at[t_fields, 0, inner_r], id_tup, 0), has_tup, has_tdn),
            (one(buf.at[t_fields, 1, inner_r], buf.at[t_fields, 3, inner_r], id_tdn, 1), has_tdn, has_tup),
            (one(buf.at[r_fields, inner_t, 4], buf.at[r_fields, inner_t, 0], id_rup, 2), has_rup, has_rdn),
            (one(buf.at[r_fields, inner_t, 1], buf.at[r_fields, inner_t, 5], id_rdn, 3), has_rdn, has_rup),
        )

    def each(copies, what):
        for copy, sends, gets in copies:
            @pl.when(gets if what == "wait_recv" else sends)
            def _():
                getattr(copy, what)()

    def eight(body, unroll=1):
        def one(i, _):
            body(i, lax.div(i, 4) + 1, lax.rem(i, 4) + 1)
            return 0

        lax.fori_loop(0, 8, one, 0, unroll=unroll)

    def unpack(fields):
        def one(i, t, r):
            for q in fields:
                value = rows[q, pl.ds(i, CHUNKS, stride=8), :]
                if q == DE:
                    f0[DE, t, r] = value
                else:
                    s0[S_VP if q == VP else q, t, r] = value

        eight(one)

    def to_blocks(k, g):
        dest = peers[k]
        return pltpu.make_async_remote_copy(
            src_ref=ostage.at[SPANS[g], pl.ds(pl.multiple_of(dest * 16, 16), 16), :],
            dst_ref=back.at[a, SPANS[g]],
            send_sem=b_send.at[g, k],
            recv_sem=b_recv.at[g, k],
            device_id={"az": dest, "rad": rho},
            device_id_type=MESH,
        )

    def own_blocks(g):
        return pltpu.make_async_copy(
            ostage.at[SPANS[g], pl.ds(pl.multiple_of(a * 16, 16), 16), :], back.at[a, SPANS[g]], l_sem.at[2 + g]
        )

    plans = []
    for step in range(STEPS):
        s, f = states[step], fresh[step]
        plans.append((
            halo(s, EN, EN, 5 * step),
            halo(s, VT, VR, 5 * step + 1),
            halo(f, SPANS[1], SPANS[1], 5 * step + 2),
            halo(f, EN, EN, 5 * step + 3),
            halo(f, pl.ds(1, 2), pl.ds(1, 2), 5 * step + 4),
        ))

    def along_azimuth(f, i, t, r, fields):
        p_lo = speed[i]
        for q in fields:
            v = f[q, t, r]
            low = p_lo * jnp.where(p_lo > 0, prev_cell(v, lane), v)
            flux[q, i] = next_cell(low, lane) - low

    def face(f, u, below, above):
        s = f[(u,) + below] + f[(u,) + above]
        up = s > 0
        return lambda q: s * jnp.where(up, f[(q,) + below], f[(q,) + above])

    for step in range(STEPS):
        s, f = states[step], fresh[step]
        old_en, old_v, late, new_en, new_v = plans[step]

        if step == 0:
            for k in range(1, AZ):
                to_rows(k, 0).wait_recv()
            own_rows(0).wait()
            unpack(EARLY)
            each(old_v, "start")
            each(old_en, "start")
            for k in range(1, AZ):
                to_rows(k, 1).wait_recv()
            own_rows(1).wait()
            unpack(LATE)

        def source_azimuth(i, t, r):
            den = f[DE, t, r]
            k = 0.01 / jnp.where(den > 0, den, 1.0)
            e = s[EN, t, r]
            vp = s[S_VP, t, r]
            new = vp - k * (next_cell(e, lane) - prev_cell(e, lane))
            f[VP, t, r] = new
            flux[VT, i] = k
            flux[EN, i] = next_cell(vp, lane) - prev_cell(vp, lane)
            speed[i] = new + prev_cell(new, lane)

        eight(source_azimuth, UNROLL)
        each(late, "start")

        def azimuth_late(i, t, r):
            along_azimuth(f, i, t, r, LATE)

        eight(azimuth_late)

        def source_speeds(i, t, r):
            k = flux[VT, i]
            f[VR, t, r] = s[VR, t, r] - k * (s[EN, t, r + 1] - s[EN, t, r - 1])
            f[VT, t, r] = s[VT, t, r] - k * (s[EN, t + 1, r] - s[EN, t - 1, r])

        def source_energy(i, t, r):
            e = s[EN, t, r]
            div = (
                flux[EN, i]
                + (s[VR, t, r + 1] - s[VR, t, r - 1])
                + (s[VT, t + 1, r] - s[VT, t - 1, r])
            )
            f[EN, t, r] = e - 0.01 * e * div

        turns = [(old_v, source_energy, new_en), (old_en, source_speeds, new_v)]
        for needs, body, sends in turns if step == 0 else turns[::-1]:
            each(needs, "wait_recv")
            eight(body, UNROLL)
            each(sends, "start")

        def azimuth_early(i, t, r):
            along_azimuth(f, i, t, r, EARLY)

        eight(azimuth_early)

        def inner_radius(n, _):
            t, r = lax.div(n, 3), lax.rem(n, 3)
            one = face(f, VR, (t + 1, r + 1), (t + 1, r + 2))
            for q in range(5):
                v = one(q)
                flux[q, 4 * t + r] += v
                flux[q, 4 * t + r + 1] -= v
            return 0

        lax.fori_loop(0, 6, inner_radius, 0)

        def inner_theta(r, _):
            one = face(f, VT, (1, r + 1), (2, r + 1))
            for q in range(5):
                v = one(q)
                flux[q, r] += v
                flux[q, 4 + r] -= v
            return 0

        lax.fori_loop(0, 4, inner_theta, 0)

        each(late, "wait_recv")
        each(new_v, "wait_recv")

        last = step == STEPS - 1
        for g, fields in ((1, LATE), (0, EARLY)) if last else ((0, (EN,)), (0, (VT, VR)), (1, LATE)):
            if EN in fields:
                each(new_en, "wait_recv")

            def outer_radius(t, _):
                low = face(f, VR, (t + 1, 0), (t + 1, 1))
                high = face(f, VR, (t + 1, 4), (t + 1, 5))
                for q in fields:
                    flux[q, 4 * t] -= low(q)
                    flux[q, 4 * t + 3] += high(q)
                return 0

            lax.fori_loop(0, 2, outer_radius, 0)

            def outer_theta(r, _):
                low = face(f, VT, (0, r + 1), (1, r + 1))
                high = face(f, VT, (2, r + 1), (3, r + 1))
                for q in fields:
                    flux[q, r] -= low(q)
                    flux[q, 4 + r] += high(q)
                return 0

            lax.fori_loop(0, 4, outer_theta, 0)

            def finish(i, t, r):
                for q in fields:
                    moved = f[q, t, r] - 0.025 * flux[q, i]
                    blended[q, i, pl.ds(0, CHUNKS), :] = moved
                    blended[q, i, pl.ds(CHUNKS, 8), :] = moved[:8]

            eight(finish, UNROLL)

            def rotate(i, t, r):
                w = frac_ref[half * 4 + r - 1]
                shift = shift_ref[half * 4 + r - 1]
                views = []
                for back_cells in (0, 1):
                    ahead = lax.rem(2 * CELLS - shift - back_cells, CELLS)
                    views.append((lax.div(ahead, 128), lax.rem(ahead, 128)))
                for q in fields:
                    for m in range(4):
                        parts = []
                        for whole, part in views:
                            near = blended[q, i, pl.ds(lax.rem(whole + 8 * m, CHUNKS), 8), :]
                            far = blended[q, i, pl.ds(lax.rem(whole + 8 * m + 1, CHUNKS), 8), :]
                            parts.append(pltpu.roll(jnp.where(lane8 < part, far, near), lax.rem(128 - part, 128), 1))
                        out = (1.0 - w) * parts[0] + w * parts[1]
                        if last:
                            ostage[q, pl.ds(64 * m + i, 8, stride=8), :] = out
                        elif q == DE:
                            f1[DE, t, r, pl.ds(8 * m, 8), :] = out
                        else:
                            s1[S_VP if q == VP else q, t, r, pl.ds(8 * m, 8), :] = out

            eight(rotate, UNROLL)
            if last:
                for k in ORDER:
                    to_blocks(k, g).start()
                own_blocks(g).start()
            elif EN in fields:
                each(plans[step + 1][0], "start")
            elif VT in fields:
                each(plans[step + 1][1], "start")

    for step in range(STEPS):
        for copies in plans[step]:
            each(copies, "wait_send")
    for g in range(2):
        for k in range(1, AZ):
            to_rows(k, g).wait_send()
            to_blocks(k, g).wait_send()
    for g in range(2):
        own_blocks(g).wait()
        for k in range(1, AZ):
            to_blocks(k, g).wait_recv()


def write_out(back, den_hbm, vel_hbm, ene_hbm, blocks, den_out, vel_out, ene_out, in_sem, out_sem):
    targets = {
        VT: (vel_out.at[2], vel_hbm.at[2]), EN: (ene_out, ene_hbm), VR: (vel_out.at[1], vel_hbm.at[1]),
        DE: (den_out, den_hbm), VP: (vel_out.at[0], vel_hbm.at[0]),
    }
    reads = [pltpu.make_async_copy(back.at[:, q], blocks.at[:, q], in_sem.at[q]) for q in range(5)]
    for copy in reads:
        copy.start()
    writes = []
    for q in range(5):
        reads[q].wait()
        dst = targets[q][0]

        def one(tp, _):
            for h in range(2):
                src = owner(tp, h)
                for c in range(2):
                    for t in range(2):
                        dst[2 * tp + t, pl.ds(4 * h, 4), pl.ds(128 * c, 128)] = blocks[
                            src, q, pl.ds(c * 8 + t * 4, 4), :
                        ]
            return 0

        lax.fori_loop(0, 8, one, 0, unroll=8)
        writes.append(pltpu.make_async_copy(*targets[q], out_sem.at[q]))
        writes[-1].start()
    for copy in writes:
        copy.wait()


def shards(density, velocity, energy, shifts, fraction):
    hbm = pl.BlockSpec(memory_space=pl.ANY)
    f32 = jnp.float32
    limit = 60 * 1024 * 1024
    block = (AZ, 5, 16, 128)
    dma = pltpu.SemaphoreType.DMA
    fields = [pltpu.VMEM(v.shape, f32) for v in (density, velocity, energy)]
    back = pl.pallas_call(
        kernel,
        out_shape=jax.ShapeDtypeStruct(block, f32),
        in_specs=[hbm] * 5,
        out_specs=hbm,
        scratch_shapes=fields + [
            pltpu.SMEM(shifts.shape, jnp.int32),
            pltpu.SMEM(fraction.shape, f32),
            pltpu.VMEM(block, f32),
            pltpu.VMEM((5, 256, 128), f32),
            pltpu.VMEM((4, 4, 6, CHUNKS, 128), f32),
            pltpu.VMEM((4, 4, 6, CHUNKS, 128), f32),
            pltpu.VMEM((5, 4, 6, CHUNKS, 128), f32),
            pltpu.VMEM((5, 4, 6, CHUNKS, 128), f32),
            pltpu.VMEM((8, CHUNKS, 128), f32),
            pltpu.VMEM((5, 8, CHUNKS, 128), f32),
            pltpu.VMEM((5, 8, CHUNKS + 8, 128), f32),
            pltpu.VMEM((5, 256, 128), f32),
            dma((2, AZ)),
            dma((2, AZ)),
            dma((5 * STEPS, 4)),
            dma((5 * STEPS, 4)),
            dma((2, AZ)),
            dma((2, AZ)),
            dma((4,)),
            dma((5,)),
        ],
        compiler_params=pltpu.CompilerParams(collective_id=0, has_side_effects=True, vmem_limit_bytes=limit),
    )(density, velocity, energy, shifts, fraction)
    return pl.pallas_call(
        write_out,
        out_shape=tuple(jax.ShapeDtypeStruct(v.shape, f32) for v in (density, velocity, energy)),
        in_specs=[hbm],
        out_specs=(hbm,) * 3,
        scratch_shapes=[pltpu.VMEM(block, f32)] + fields + [dma((5,)), dma((5,))],
        compiler_params=pltpu.CompilerParams(vmem_limit_bytes=limit),
    )(back)


def solution(mesh):
    placed = (
        P(None, "rad", "az"),
        P(None, None, "rad", "az"),
        P(None, "rad", "az"),
        P("rad"),
        P("rad"),
    )
    return jax.shard_map(
        shards,
        mesh=mesh,
        in_specs=placed,
        out_specs=(P(None, "rad", "az"), P(None, None, "rad", "az"), P(None, "rad", "az")),
        check_vma=False,
    )
```

```python
import jax
import jax.numpy as jnp
from jax import lax
from jax.experimental import pallas as pl
from jax.experimental.pallas import tpu as pltpu
from jax.sharding import PartitionSpec as P

MESH = pl.DeviceIdType.MESH
AZ = 16
QUADS = 32
CHUNKS = 32
CELLS = 4096
STEPS = 2

EN, VT, VR, DE, VP = range(5)
EARLY, LATE = (EN, VT, VR), (DE, VP)
GROUPS = (EARLY, LATE)
SPANS = (pl.ds(0, 3), pl.ds(3, 2))
S_VP = 3
UNROLL = 8
ORDER = (8, 4, 12, 2, 9, 5, 13, 3, 10, 6, 14, 1, 11, 7, 15)


def owner(pair, half):
    return lax.div(pair, 2) * 4 + half * 2 + lax.rem(pair, 2)


def prev_cell(x, lane):
    x1 = pltpu.roll(x, 1, 1)
    return jnp.where(lane == 0, pltpu.roll(x1, 1, 0), x1)


def next_cell(x, lane):
    x1 = pltpu.roll(x, 127, 1)
    return jnp.where(lane == 127, pltpu.roll(x1, CHUNKS - 1, 0), x1)


def kernel(
    den_hbm, vel_hbm, ene_hbm, shift_hbm, frac_hbm,
    back,
    den_ref, vel_ref, ene_ref, shift_ref, frac_ref,
    stage, rows, s0, s1, f0, f1, speed, flux, blended, ostage,
    a_send, a_recv, h_send, h_recv, b_send, b_recv, l_sem, i_sem,
):
    a = lax.axis_index("az")
    rho = lax.axis_index("rad")
    x, half, core = lax.div(a, 4), lax.rem(lax.div(a, 2), 2), lax.rem(a, 2)
    pair = 2 * x + core
    quad = 2 * rho + half
    states, fresh = (s0, s1), (f0, f1)

    loads = [
        pltpu.make_async_copy(src, dst, i_sem.at[n])
        for n, (src, dst) in enumerate((
            (ene_hbm, ene_ref), (vel_hbm, vel_ref), (den_hbm, den_ref), (shift_hbm, shift_ref), (frac_hbm, frac_ref)
        ))
    ]
    for copy in loads[:3]:
        copy.start()

    peers = []
    for k in range(AZ):
        dx, dy, dc = k // 4, (k // 2) % 2, k % 2
        peers.append(lax.rem(x + dx, 4) * 4 + lax.rem(half + dy, 2) * 2 + lax.rem(core + dc, 2))

    barrier = pltpu.get_barrier_semaphore()
    for k in range(1, AZ):
        pl.semaphore_signal(barrier, inc=1, device_id={"az": peers[k], "rad": rho}, device_id_type=MESH)
    cross = lax.rem(quad + 2 * half - 1 + QUADS, QUADS)
    has_cross = jnp.logical_and(quad > 0, quad < QUADS - 1)

    @pl.when(has_cross)
    def _():
        pl.semaphore_signal(
            barrier, inc=1, device_id={"az": owner(pair, lax.rem(cross, 2)), "rad": lax.div(cross, 2)},
            device_id_type=MESH,
        )

    for copy in loads[3:]:
        copy.start()

    inner_t, inner_r = pl.ds(1, 2), pl.ds(1, 4)
    for buf, span in ((s0, pl.ds(0, 3)), (s1, pl.ds(0, 3)), (f0, pl.ds(0, 5)), (f1, pl.ds(0, 5))):
        def clear(where):
            buf[where] = jnp.zeros_like(buf[where])

        pl.when(pair == 0)(lambda: clear((span, 0, inner_r)))
        pl.when(pair == 7)(lambda: clear((span, 3, inner_r)))
        pl.when(quad == 0)(lambda: clear((span, inner_t, 0)))
        pl.when(quad == QUADS - 1)(lambda: clear((span, inner_t, 5)))

    sources = {VT: vel_ref.at[2], EN: ene_ref, VR: vel_ref.at[1], DE: den_ref, VP: vel_ref.at[0]}

    def regroup(fields):
        def one(tp, _):
            for h in range(2):
                dest = owner(tp, h)
                for f in fields:
                    for c in range(2):
                        for t in range(2):
                            stage[dest, f, pl.ds(c * 8 + t * 4, 4), :] = sources[f][
                                2 * tp + t, pl.ds(4 * h, 4), pl.ds(128 * c, 128)
                            ]
            return 0

        lax.fori_loop(0, 8, one, 0)

    def to_rows(k, g):
        dest = peers[k]
        return pltpu.make_async_remote_copy(
            src_ref=stage.at[dest, SPANS[g]],
            dst_ref=rows.at[SPANS[g], pl.ds(pl.multiple_of(a * 16, 16), 16), :],
            send_sem=a_send.at[g, k],
            recv_sem=a_recv.at[g, k],
            device_id={"az": dest, "rad": rho},
            device_id_type=MESH,
        )

    def own_rows(g):
        return pltpu.make_async_copy(
            stage.at[a, SPANS[g]], rows.at[SPANS[g], pl.ds(pl.multiple_of(a * 16, 16), 16), :], l_sem.at[g]
        )

    for copy in loads[:2]:
        copy.wait()
    regroup(EARLY)
    pl.semaphore_wait(barrier, AZ - 1 + has_cross.astype(jnp.int32))
    for k in ORDER:
        to_rows(k, 0).start()
    own_rows(0).start()
    for copy in loads[2:]:
        copy.wait()
    regroup(LATE)
    for k in ORDER:
        to_rows(k, 1).start()
    own_rows(1).start()

    lane = lax.broadcasted_iota(jnp.int32, (CHUNKS, 128), 1)
    lane8 = lax.broadcasted_iota(jnp.int32, (8, 128), 1)

    t_up, t_dn = lax.rem(pair + 1, 8), lax.rem(pair + 7, 8)
    r_up, r_dn = lax.rem(quad + 1, QUADS), lax.rem(quad + QUADS - 1, QUADS)
    has_tup, has_tdn = pair < 7, pair > 0
    has_rup, has_rdn = quad < QUADS - 1, quad > 0
    id_tup = {"az": owner(t_up, half), "rad": rho}
    id_tdn = {"az": owner(t_dn, half), "rad": rho}
    id_rup = {"az": owner(pair, lax.rem(r_up, 2)), "rad": lax.div(r_up, 2)}
    id_rdn = {"az": owner(pair, lax.rem(r_dn, 2)), "rad": lax.div(r_dn, 2)}

    def halo(buf, t_fields, r_fields, slot):
        def one(src, dst, ident, d):
            return pltpu.make_async_remote_copy(
                src_ref=src, dst_ref=dst, send_sem=h_send.at[slot, d], recv_sem=h_recv.at[slot, d],
                device_id=ident, device_id_type=MESH,
            )

        return (
            (one(buf.at[r_fields, inner_t, 4], buf.at[r_fields, inner_t, 0], id_rup, 2), has_rup, has_rdn),
            (one(buf.at[r_fields, inner_t, 1], buf.at[r_fields, inner_t, 5], id_rdn, 3), has_rdn, has_rup),
            (one(buf.at[t_fields, 2, inner_r], buf.at[t_fields, 0, inner_r], id_tup, 0), has_tup, has_tdn),
            (one(buf.at[t_fields, 1, inner_r], buf.at[t_fields, 3, inner_r], id_tdn, 1), has_tdn, has_tup),
        )

    def each(copies, what):
        for copy, sends, gets in copies:
            @pl.when(gets if what == "wait_recv" else sends)
            def _():
                getattr(copy, what)()

    def eight(body, unroll=1):
        def one(i, _):
            body(i, lax.div(i, 4) + 1, lax.rem(i, 4) + 1)
            return 0

        lax.fori_loop(0, 8, one, 0, unroll=unroll)

    def unpack(fields):
        def one(i, t, r):
            for q in fields:
                value = rows[q, pl.ds(i, CHUNKS, stride=8), :]
                if q == DE:
                    f0[DE, t, r] = value
                else:
                    s0[S_VP if q == VP else q, t, r] = value

        eight(one)

    def to_blocks(k, g):
        dest = peers[k]
        return pltpu.make_async_remote_copy(
            src_ref=ostage.at[SPANS[g], pl.ds(pl.multiple_of(dest * 16, 16), 16), :],
            dst_ref=back.at[a, SPANS[g]],
            send_sem=b_send.at[g, k],
            recv_sem=b_recv.at[g, k],
            device_id={"az": dest, "rad": rho},
            device_id_type=MESH,
        )

    def own_blocks(g):
        return pltpu.make_async_copy(
            ostage.at[SPANS[g], pl.ds(pl.multiple_of(a * 16, 16), 16), :], back.at[a, SPANS[g]], l_sem.at[2 + g]
        )

    plans = []
    for step in range(STEPS):
        s, f = states[step], fresh[step]
        plans.append((
            halo(s, EN, EN, 6 * step),
            halo(s, VT, VR, 6 * step + 1),
            halo(f, SPANS[1], SPANS[1], 6 * step + 2),
            halo(f, EN, EN, 6 * step + 3),
            halo(f, VT, VR, 6 * step + 4),
            halo(f, VR, VT, 6 * step + 5),
        ))

    def along_azimuth(f, i, t, r, fields):
        p_lo = speed[i]
        for q in fields:
            v = f[q, t, r]
            low = p_lo * jnp.where(p_lo > 0, prev_cell(v, lane), v)
            flux[q, i] = next_cell(low, lane) - low

    def face(f, u, below, above):
        s = f[(u,) + below] + f[(u,) + above]
        up = s > 0
        return lambda q: s * jnp.where(up, f[(q,) + below], f[(q,) + above])

    for step in range(STEPS):
        s, f = states[step], fresh[step]
        old_en, old_v, late, new_en, new_v, rest = plans[step]

        if step == 0:
            for k in range(1, AZ):
                to_rows(k, 0).wait_recv()
            own_rows(0).wait()
            unpack(EARLY)
            each(old_v, "start")
            each(old_en, "start")
            for k in range(1, AZ):
                to_rows(k, 1).wait_recv()
            own_rows(1).wait()
            unpack(LATE)

        def source_azimuth(i, t, r):
            den = f[DE, t, r]
            k = 0.01 / jnp.where(den > 0, den, 1.0)
            e = s[EN, t, r]
            vp = s[S_VP, t, r]
            new = vp - k * (next_cell(e, lane) - prev_cell(e, lane))
            f[VP, t, r] = new
            flux[VT, i] = k
            flux[EN, i] = next_cell(vp, lane) - prev_cell(vp, lane)
            speed[i] = new + prev_cell(new, lane)

        eight(source_azimuth, UNROLL)
        each(late, "start")

        def azimuth_late(i, t, r):
            along_azimuth(f, i, t, r, LATE)

        eight(azimuth_late)

        def source_speeds(i, t, r):
            k = flux[VT, i]
            f[VR, t, r] = s[VR, t, r] - k * (s[EN, t, r + 1] - s[EN, t, r - 1])
            f[VT, t, r] = s[VT, t, r] - k * (s[EN, t + 1, r] - s[EN, t - 1, r])

        def source_energy(i, t, r):
            e = s[EN, t, r]
            div = (
                flux[EN, i]
                + (s[VR, t, r + 1] - s[VR, t, r - 1])
                + (s[VT, t + 1, r] - s[VT, t - 1, r])
            )
            f[EN, t, r] = e - 0.01 * e * div

        turns = [(old_v, source_energy, new_en), (old_en, source_speeds, new_v)]
        for needs, body, sends in turns if step == 0 else turns[::-1]:
            each(needs, "wait_recv")
            eight(body, UNROLL)
            each(sends, "start")
        each(rest, "start")

        def azimuth_early(i, t, r):
            along_azimuth(f, i, t, r, EARLY)

        eight(azimuth_early)

        def inner_radius(n, _):
            t, r = lax.div(n, 3), lax.rem(n, 3)
            one = face(f, VR, (t + 1, r + 1), (t + 1, r + 2))
            for q in range(5):
                v = one(q)
                flux[q, 4 * t + r] += v
                flux[q, 4 * t + r + 1] -= v
            return 0

        lax.fori_loop(0, 6, inner_radius, 0)

        def inner_theta(r, _):
            one = face(f, VT, (1, r + 1), (2, r + 1))
            for q in range(5):
                v = one(q)
                flux[q, r] += v
                flux[q, 4 + r] -= v
            return 0

        lax.fori_loop(0, 4, inner_theta, 0)

        each(new_v, "wait_recv")

        last = step == STEPS - 1
        for g, fields in ((1, LATE), (0, EARLY)) if last else ((0, (EN,)), (0, (VT, VR)), (1, LATE)):
            if EN in fields:
                each(new_en, "wait_recv")
            if VT in fields:
                each(rest, "wait_recv")
            if DE in fields:
                each(late, "wait_recv")

            def outer_radius(t, _):
                low = face(f, VR, (t + 1, 0), (t + 1, 1))
                high = face(f, VR, (t + 1, 4), (t + 1, 5))
                for q in fields:
                    flux[q, 4 * t] -= low(q)
                    flux[q, 4 * t + 3] += high(q)
                return 0

            lax.fori_loop(0, 2, outer_radius, 0)

            def outer_theta(r, _):
                low = face(f, VT, (0, r + 1), (1, r + 1))
                high = face(f, VT, (2, r + 1), (3, r + 1))
                for q in fields:
                    flux[q, r] -= low(q)
                    flux[q, 4 + r] += high(q)
                return 0

            lax.fori_loop(0, 4, outer_theta, 0)

            def finish(i, t, r):
                for q in fields:
                    moved = f[q, t, r] - 0.025 * flux[q, i]
                    blended[q, i, pl.ds(0, CHUNKS), :] = moved
                    blended[q, i, pl.ds(CHUNKS, CHUNKS), :] = moved

            eight(finish, UNROLL)

            def rotate(i, t, r):
                w = frac_ref[half * 4 + r - 1]
                shift = shift_ref[half * 4 + r - 1]
                views = []
                for back_cells in (0, 1):
                    ahead = lax.rem(2 * CELLS - shift - back_cells, CELLS)
                    views.append((lax.div(ahead, 128), lax.rem(ahead, 128)))
                for q in fields:
                    for m in range(4):
                        parts = []
                        for whole, part in views:
                            near = blended[q, i, pl.ds(whole + 8 * m, 8), :]
                            far = blended[q, i, pl.ds(whole + 8 * m + 1, 8), :]
                            parts.append(pltpu.roll(jnp.where(lane8 < part, far, near), lax.rem(128 - part, 128), 1))
                        out = (1.0 - w) * parts[0] + w * parts[1]
                        if last:
                            ostage[q, pl.ds(64 * m + i, 8, stride=8), :] = out
                        elif q == DE:
                            f1[DE, t, r, pl.ds(8 * m, 8), :] = out
                        else:
                            s1[S_VP if q == VP else q, t, r, pl.ds(8 * m, 8), :] = out

            eight(rotate, UNROLL)
            if last:
                for k in ORDER:
                    to_blocks(k, g).start()
                own_blocks(g).start()
            elif EN in fields:
                each(plans[step + 1][0], "start")
            elif VT in fields:
                each(plans[step + 1][1], "start")

    for step in range(STEPS):
        for copies in plans[step]:
            each(copies, "wait_send")
    for g in range(2):
        for k in range(1, AZ):
            to_rows(k, g).wait_send()
            to_blocks(k, g).wait_send()
    for g in range(2):
        own_blocks(g).wait()
        for k in range(1, AZ):
            to_blocks(k, g).wait_recv()


def write_out(back, den_hbm, vel_hbm, ene_hbm, blocks, den_out, vel_out, ene_out, in_sem, out_sem):
    targets = {
        VT: (vel_out.at[2], vel_hbm.at[2]), EN: (ene_out, ene_hbm), VR: (vel_out.at[1], vel_hbm.at[1]),
        DE: (den_out, den_hbm), VP: (vel_out.at[0], vel_hbm.at[0]),
    }
    reads = [pltpu.make_async_copy(back.at[:, q], blocks.at[:, q], in_sem.at[q]) for q in range(5)]
    for copy in reads:
        copy.start()
    writes = []
    for q in range(5):
        reads[q].wait()
        dst = targets[q][0]

        def one(tp, _):
            for h in range(2):
                src = owner(tp, h)
                for c in range(2):
                    for t in range(2):
                        dst[2 * tp + t, pl.ds(4 * h, 4), pl.ds(128 * c, 128)] = blocks[
                            src, q, pl.ds(c * 8 + t * 4, 4), :
                        ]
            return 0

        lax.fori_loop(0, 8, one, 0, unroll=8)
        writes.append(pltpu.make_async_copy(*targets[q], out_sem.at[q]))
        writes[-1].start()
    for copy in writes:
        copy.wait()


def shards(density, velocity, energy, shifts, fraction):
    hbm = pl.BlockSpec(memory_space=pl.ANY)
    f32 = jnp.float32
    limit = 60 * 1024 * 1024
    block = (AZ, 5, 16, 128)
    dma = pltpu.SemaphoreType.DMA
    fields = [pltpu.VMEM(v.shape, f32) for v in (density, velocity, energy)]
    back = pl.pallas_call(
        kernel,
        out_shape=jax.ShapeDtypeStruct(block, f32),
        in_specs=[hbm] * 5,
        out_specs=hbm,
        scratch_shapes=fields + [
            pltpu.SMEM(shifts.shape, jnp.int32),
            pltpu.SMEM(fraction.shape, f32),
            pltpu.VMEM(block, f32),
            pltpu.VMEM((5, 256, 128), f32),
            pltpu.VMEM((4, 4, 6, CHUNKS, 128), f32),
            pltpu.VMEM((4, 4, 6, CHUNKS, 128), f32),
            pltpu.VMEM((5, 4, 6, CHUNKS, 128), f32),
            pltpu.VMEM((5, 4, 6, CHUNKS, 128), f32),
            pltpu.VMEM((8, CHUNKS, 128), f32),
            pltpu.VMEM((5, 8, CHUNKS, 128), f32),
            pltpu.VMEM((5, 8, 2 * CHUNKS, 128), f32),
            pltpu.VMEM((5, 256, 128), f32),
            dma((2, AZ)),
            dma((2, AZ)),
            dma((6 * STEPS, 4)),
            dma((6 * STEPS, 4)),
            dma((2, AZ)),
            dma((2, AZ)),
            dma((4,)),
            dma((5,)),
        ],
        compiler_params=pltpu.CompilerParams(collective_id=0, has_side_effects=True, vmem_limit_bytes=limit),
    )(density, velocity, energy, shifts, fraction)
    return pl.pallas_call(
        write_out,
        out_shape=tuple(jax.ShapeDtypeStruct(v.shape, f32) for v in (density, velocity, energy)),
        in_specs=[hbm],
        out_specs=(hbm,) * 3,
        scratch_shapes=[pltpu.VMEM(block, f32)] + fields + [dma((5,)), dma((5,))],
        compiler_params=pltpu.CompilerParams(vmem_limit_bytes=limit),
    )(back)


def solution(mesh):
    placed = (
        P(None, "rad", "az"),
        P(None, None, "rad", "az"),
        P(None, "rad", "az"),
        P("rad"),
        P("rad"),
    )
    return jax.shard_map(
        shards,
        mesh=mesh,
        in_specs=placed,
        out_specs=(P(None, "rad", "az"), P(None, None, "rad", "az"), P(None, "rad", "az")),
        check_vma=False,
    )
```

```python
import jax
import jax.numpy as jnp
from jax import lax
from jax.experimental import pallas as pl
from jax.experimental.pallas import tpu as pltpu
from jax.sharding import PartitionSpec as P

MESH = pl.DeviceIdType.MESH
AZ = 16
QUADS = 32
CHUNKS = 32
CELLS = 4096
STEPS = 2

EN, VT, VR, DE, VP = range(5)
EARLY, LATE = (EN, VT, VR), (DE, VP)
GROUPS = (EARLY, LATE)
SPANS = (pl.ds(0, 3), pl.ds(3, 2))
S_VP = 3
UNROLL = 8
ORDER = (10, 8, 6, 4, 14, 12, 2, 11, 9, 7, 5, 15, 13, 3, 1)


def owner(pair, half):
    return lax.div(pair, 2) * 4 + (1 - half) * 2 + lax.rem(pair, 2)


def prev_cell(x, lane):
    x1 = pltpu.roll(x, 1, 1)
    return jnp.where(lane == 0, pltpu.roll(x1, 1, 0), x1)


def next_cell(x, lane):
    x1 = pltpu.roll(x, 127, 1)
    return jnp.where(lane == 127, pltpu.roll(x1, CHUNKS - 1, 0), x1)


def kernel(
    den_hbm, vel_hbm, ene_hbm, shift_hbm, frac_hbm,
    back,
    den_ref, vel_ref, ene_ref, shift_ref, frac_ref,
    stage, rows, s0, s1, f0, f1, speed, flux, blended, ostage,
    a_send, a_recv, h_send, h_recv, b_send, b_recv, l_sem, i_sem,
):
    a = lax.axis_index("az")
    rho = lax.axis_index("rad")
    x, y, core = lax.div(a, 4), lax.rem(lax.div(a, 2), 2), lax.rem(a, 2)
    half = 1 - y
    pair = 2 * x + core
    quad = 2 * rho + half
    states, fresh = (s0, s1), (f0, f1)

    loads = [
        pltpu.make_async_copy(src, dst, i_sem.at[n])
        for n, (src, dst) in enumerate((
            (ene_hbm, ene_ref), (vel_hbm, vel_ref), (den_hbm, den_ref), (shift_hbm, shift_ref), (frac_hbm, frac_ref)
        ))
    ]
    for copy in loads[:3]:
        copy.start()

    peers = []
    for k in range(AZ):
        dx, dy, dc = k // 4, (k // 2) % 2, k % 2
        peers.append(lax.rem(x + dx, 4) * 4 + lax.rem(y + dy, 2) * 2 + lax.rem(core + dc, 2))

    barrier = pltpu.get_barrier_semaphore()
    for k in range(1, AZ):
        pl.semaphore_signal(barrier, inc=1, device_id={"az": peers[k], "rad": rho}, device_id_type=MESH)
    cross = lax.rem(quad + 2 * half - 1 + QUADS, QUADS)
    has_cross = jnp.logical_and(quad > 0, quad < QUADS - 1)

    @pl.when(has_cross)
    def _():
        pl.semaphore_signal(
            barrier, inc=1, device_id={"az": owner(pair, lax.rem(cross, 2)), "rad": lax.div(cross, 2)},
            device_id_type=MESH,
        )

    for copy in loads[3:]:
        copy.start()

    inner_t, inner_r = pl.ds(1, 2), pl.ds(1, 4)
    for buf, span in ((s0, pl.ds(0, 3)), (s1, pl.ds(0, 3)), (f0, pl.ds(0, 5)), (f1, pl.ds(0, 5))):
        def clear(where):
            buf[where] = jnp.zeros_like(buf[where])

        pl.when(pair == 0)(lambda: clear((span, 0, inner_r)))
        pl.when(pair == 7)(lambda: clear((span, 3, inner_r)))
        pl.when(quad == 0)(lambda: clear((span, inner_t, 0)))
        pl.when(quad == QUADS - 1)(lambda: clear((span, inner_t, 5)))

    sources = {VT: vel_ref.at[2], EN: ene_ref, VR: vel_ref.at[1], DE: den_ref, VP: vel_ref.at[0]}

    def regroup(fields):
        def one(tp, _):
            for h in range(2):
                dest = owner(tp, h)
                for f in fields:
                    for c in range(2):
                        for t in range(2):
                            stage[dest, f, pl.ds(c * 8 + t * 4, 4), :] = sources[f][
                                2 * tp + t, pl.ds(4 * h, 4), pl.ds(128 * c, 128)
                            ]
            return 0

        lax.fori_loop(0, 8, one, 0)

    def to_rows(k, g):
        dest = peers[k]
        return pltpu.make_async_remote_copy(
            src_ref=stage.at[dest, SPANS[g]],
            dst_ref=rows.at[SPANS[g], pl.ds(pl.multiple_of(a * 16, 16), 16), :],
            send_sem=a_send.at[g, k],
            recv_sem=a_recv.at[g, k],
            device_id={"az": dest, "rad": rho},
            device_id_type=MESH,
        )

    def own_rows(g):
        return pltpu.make_async_copy(
            stage.at[a, SPANS[g]], rows.at[SPANS[g], pl.ds(pl.multiple_of(a * 16, 16), 16), :], l_sem.at[g]
        )

    for copy in loads[:2]:
        copy.wait()
    regroup(EARLY)
    pl.semaphore_wait(barrier, AZ - 1 + has_cross.astype(jnp.int32))
    for k in ORDER:
        to_rows(k, 0).start()
    own_rows(0).start()
    for copy in loads[2:]:
        copy.wait()
    regroup(LATE)
    for k in ORDER:
        to_rows(k, 1).start()
    own_rows(1).start()

    lane = lax.broadcasted_iota(jnp.int32, (CHUNKS, 128), 1)
    lane8 = lax.broadcasted_iota(jnp.int32, (8, 128), 1)

    t_up, t_dn = lax.rem(pair + 1, 8), lax.rem(pair + 7, 8)
    r_up, r_dn = lax.rem(quad + 1, QUADS), lax.rem(quad + QUADS - 1, QUADS)
    has_tup, has_tdn = pair < 7, pair > 0
    has_rup, has_rdn = quad < QUADS - 1, quad > 0
    id_tup = {"az": owner(t_up, half), "rad": rho}
    id_tdn = {"az": owner(t_dn, half), "rad": rho}
    id_rup = {"az": owner(pair, lax.rem(r_up, 2)), "rad": lax.div(r_up, 2)}
    id_rdn = {"az": owner(pair, lax.rem(r_dn, 2)), "rad": lax.div(r_dn, 2)}

    def halo(buf, t_fields, r_fields, slot):
        def one(src, dst, ident, d):
            return pltpu.make_async_remote_copy(
                src_ref=src, dst_ref=dst, send_sem=h_send.at[slot, d], recv_sem=h_recv.at[slot, d],
                device_id=ident, device_id_type=MESH,
            )

        return (
            (one(buf.at[r_fields, inner_t, 4], buf.at[r_fields, inner_t, 0], id_rup, 2), has_rup, has_rdn),
            (one(buf.at[r_fields, inner_t, 1], buf.at[r_fields, inner_t, 5], id_rdn, 3), has_rdn, has_rup),
            (one(buf.at[t_fields, 2, inner_r], buf.at[t_fields, 0, inner_r], id_tup, 0), has_tup, has_tdn),
            (one(buf.at[t_fields, 1, inner_r], buf.at[t_fields, 3, inner_r], id_tdn, 1), has_tdn, has_tup),
        )

    def each(copies, what):
        for copy, sends, gets in copies:
            @pl.when(gets if what == "wait_recv" else sends)
            def _():
                getattr(copy, what)()

    def eight(body, unroll=1):
        def one(i, _):
            body(i, lax.div(i, 4) + 1, lax.rem(i, 4) + 1)
            return 0

        lax.fori_loop(0, 8, one, 0, unroll=unroll)

    def unpack(fields):
        def one(i, t, r):
            for q in fields:
                value = rows[q, pl.ds(i, CHUNKS, stride=8), :]
                if q == DE:
                    f0[DE, t, r] = value
                else:
                    s0[S_VP if q == VP else q, t, r] = value

        eight(one)

    def to_blocks(k, g):
        dest = peers[k]
        return pltpu.make_async_remote_copy(
            src_ref=ostage.at[SPANS[g], pl.ds(pl.multiple_of(dest * 16, 16), 16), :],
            dst_ref=back.at[a, SPANS[g]],
            send_sem=b_send.at[g, k],
            recv_sem=b_recv.at[g, k],
            device_id={"az": dest, "rad": rho},
            device_id_type=MESH,
        )

    def own_blocks(g):
        return pltpu.make_async_copy(
            ostage.at[SPANS[g], pl.ds(pl.multiple_of(a * 16, 16), 16), :], back.at[a, SPANS[g]], l_sem.at[2 + g]
        )

    plans = []
    for step in range(STEPS):
        s, f = states[step], fresh[step]
        plans.append((
            halo(s, EN, EN, 6 * step),
            halo(s, VT, VR, 6 * step + 1),
            halo(f, SPANS[1], SPANS[1], 6 * step + 2),
            halo(f, EN, EN, 6 * step + 3),
            halo(f, VT, VR, 6 * step + 4),
            halo(f, VR, VT, 6 * step + 5),
        ))

    def along_azimuth(f, i, t, r, fields):
        p_lo = speed[i]
        for q in fields:
            v = f[q, t, r]
            low = p_lo * jnp.where(p_lo > 0, prev_cell(v, lane), v)
            flux[q, i] = next_cell(low, lane) - low

    def face(f, u, below, above):
        s = f[(u,) + below] + f[(u,) + above]
        up = s > 0
        return lambda q: s * jnp.where(up, f[(q,) + below], f[(q,) + above])

    for step in range(STEPS):
        s, f = states[step], fresh[step]
        old_en, old_v, late, new_en, new_v, rest = plans[step]

        if step == 0:
            for k in range(1, AZ):
                to_rows(k, 0).wait_recv()
            own_rows(0).wait()
            unpack(EARLY)
            each(old_v, "start")
            each(old_en, "start")
            for k in range(1, AZ):
                to_rows(k, 1).wait_recv()
            own_rows(1).wait()
            unpack(LATE)

        def source_azimuth(i, t, r):
            den = f[DE, t, r]
            k = 0.01 / jnp.where(den > 0, den, 1.0)
            e = s[EN, t, r]
            vp = s[S_VP, t, r]
            new = vp - k * (next_cell(e, lane) - prev_cell(e, lane))
            f[VP, t, r] = new
            flux[VT, i] = k
            flux[EN, i] = next_cell(vp, lane) - prev_cell(vp, lane)
            speed[i] = new + prev_cell(new, lane)

        eight(source_azimuth, UNROLL)
        each(late, "start")

        def azimuth_late(i, t, r):
            along_azimuth(f, i, t, r, LATE)

        eight(azimuth_late)

        def source_speeds(i, t, r):
            k = flux[VT, i]
            f[VR, t, r] = s[VR, t, r] - k * (s[EN, t, r + 1] - s[EN, t, r - 1])
            f[VT, t, r] = s[VT, t, r] - k * (s[EN, t + 1, r] - s[EN, t - 1, r])

        def source_energy(i, t, r):
            e = s[EN, t, r]
            div = (
                flux[EN, i]
                + (s[VR, t, r + 1] - s[VR, t, r - 1])
                + (s[VT, t + 1, r] - s[VT, t - 1, r])
            )
            f[EN, t, r] = e - 0.01 * e * div

        turns = [(old_v, source_energy, new_en), (old_en, source_speeds, new_v)]
        for needs, body, sends in turns if step == 0 else turns[::-1]:
            each(needs, "wait_recv")
            eight(body, UNROLL)
            each(sends, "start")
        each(rest, "start")

        def azimuth_early(i, t, r):
            along_azimuth(f, i, t, r, EARLY)

        eight(azimuth_early)

        def inner_radius(n, _):
            t, r = lax.div(n, 3), lax.rem(n, 3)
            one = face(f, VR, (t + 1, r + 1), (t + 1, r + 2))
            for q in range(5):
                v = one(q)
                flux[q, 4 * t + r] += v
                flux[q, 4 * t + r + 1] -= v
            return 0

        lax.fori_loop(0, 6, inner_radius, 0)

        def inner_theta(r, _):
            one = face(f, VT, (1, r + 1), (2, r + 1))
            for q in range(5):
                v = one(q)
                flux[q, r] += v
                flux[q, 4 + r] -= v
            return 0

        lax.fori_loop(0, 4, inner_theta, 0)

        each(new_v, "wait_recv")

        last = step == STEPS - 1
        for g, fields in ((1, LATE), (0, EARLY)) if last else ((0, (EN,)), (0, (VT, VR)), (1, LATE)):
            if EN in fields:
                each(new_en, "wait_recv")
            if VT in fields:
                each(rest, "wait_recv")
            if DE in fields:
                each(late, "wait_recv")

            def outer_radius(t, _):
                low = face(f, VR, (t + 1, 0), (t + 1, 1))
                high = face(f, VR, (t + 1, 4), (t + 1, 5))
                for q in fields:
                    flux[q, 4 * t] -= low(q)
                    flux[q, 4 * t + 3] += high(q)
                return 0

            lax.fori_loop(0, 2, outer_radius, 0)

            def outer_theta(r, _):
                low = face(f, VT, (0, r + 1), (1, r + 1))
                high = face(f, VT, (2, r + 1), (3, r + 1))
                for q in fields:
                    flux[q, r] -= low(q)
                    flux[q, 4 + r] += high(q)
                return 0

            lax.fori_loop(0, 4, outer_theta, 0)

            def finish(i, t, r):
                for q in fields:
                    moved = f[q, t, r] - 0.025 * flux[q, i]
                    blended[q, i, pl.ds(0, CHUNKS), :] = moved
                    blended[q, i, pl.ds(CHUNKS, CHUNKS), :] = moved

            eight(finish, UNROLL)

            def rotate(i, t, r):
                w = frac_ref[half * 4 + r - 1]
                shift = shift_ref[half * 4 + r - 1]
                views = []
                for back_cells in (0, 1):
                    ahead = lax.rem(2 * CELLS - shift - back_cells, CELLS)
                    views.append((lax.div(ahead, 128), lax.rem(ahead, 128)))
                for q in fields:
                    for m in range(4):
                        parts = []
                        for whole, part in views:
                            near = blended[q, i, pl.ds(whole + 8 * m, 8), :]
                            far = blended[q, i, pl.ds(whole + 8 * m + 1, 8), :]
                            parts.append(pltpu.roll(jnp.where(lane8 < part, far, near), lax.rem(128 - part, 128), 1))
                        out = (1.0 - w) * parts[0] + w * parts[1]
                        if last:
                            ostage[q, pl.ds(64 * m + i, 8, stride=8), :] = out
                        elif q == DE:
                            f1[DE, t, r, pl.ds(8 * m, 8), :] = out
                        else:
                            s1[S_VP if q == VP else q, t, r, pl.ds(8 * m, 8), :] = out

            eight(rotate, UNROLL)
            if last:
                for k in ORDER:
                    to_blocks(k, g).start()
                own_blocks(g).start()
            elif EN in fields:
                each(plans[step + 1][0], "start")
            elif VT in fields:
                each(plans[step + 1][1], "start")

    for step in range(STEPS):
        for copies in plans[step]:
            each(copies, "wait_send")
    for g in range(2):
        for k in range(1, AZ):
            to_rows(k, g).wait_send()
            to_blocks(k, g).wait_send()
    for g in range(2):
        own_blocks(g).wait()
        for k in range(1, AZ):
            to_blocks(k, g).wait_recv()


def write_out(back, den_hbm, vel_hbm, ene_hbm, blocks, den_out, vel_out, ene_out, in_sem, out_sem):
    targets = {
        VT: (vel_out.at[2], vel_hbm.at[2]), EN: (ene_out, ene_hbm), VR: (vel_out.at[1], vel_hbm.at[1]),
        DE: (den_out, den_hbm), VP: (vel_out.at[0], vel_hbm.at[0]),
    }
    reads = [pltpu.make_async_copy(back.at[:, q], blocks.at[:, q], in_sem.at[q]) for q in range(5)]
    for copy in reads:
        copy.start()
    writes = []
    for q in range(5):
        reads[q].wait()
        dst = targets[q][0]

        def one(tp, _):
            for h in range(2):
                src = owner(tp, h)
                for c in range(2):
                    for t in range(2):
                        dst[2 * tp + t, pl.ds(4 * h, 4), pl.ds(128 * c, 128)] = blocks[
                            src, q, pl.ds(c * 8 + t * 4, 4), :
                        ]
            return 0

        lax.fori_loop(0, 8, one, 0, unroll=8)
        writes.append(pltpu.make_async_copy(*targets[q], out_sem.at[q]))
        writes[-1].start()
    for copy in writes:
        copy.wait()


def shards(density, velocity, energy, shifts, fraction):
    hbm = pl.BlockSpec(memory_space=pl.ANY)
    f32 = jnp.float32
    limit = 60 * 1024 * 1024
    block = (AZ, 5, 16, 128)
    dma = pltpu.SemaphoreType.DMA
    fields = [pltpu.VMEM(v.shape, f32) for v in (density, velocity, energy)]
    back = pl.pallas_call(
        kernel,
        out_shape=jax.ShapeDtypeStruct(block, f32),
        in_specs=[hbm] * 5,
        out_specs=hbm,
        scratch_shapes=fields + [
            pltpu.SMEM(shifts.shape, jnp.int32),
            pltpu.SMEM(fraction.shape, f32),
            pltpu.VMEM(block, f32),
            pltpu.VMEM((5, 256, 128), f32),
            pltpu.VMEM((4, 4, 6, CHUNKS, 128), f32),
            pltpu.VMEM((4, 4, 6, CHUNKS, 128), f32),
            pltpu.VMEM((5, 4, 6, CHUNKS, 128), f32),
            pltpu.VMEM((5, 4, 6, CHUNKS, 128), f32),
            pltpu.VMEM((8, CHUNKS, 128), f32),
            pltpu.VMEM((5, 8, CHUNKS, 128), f32),
            pltpu.VMEM((5, 8, 2 * CHUNKS, 128), f32),
            pltpu.VMEM((5, 256, 128), f32),
            dma((2, AZ)),
            dma((2, AZ)),
            dma((6 * STEPS, 4)),
            dma((6 * STEPS, 4)),
            dma((2, AZ)),
            dma((2, AZ)),
            dma((4,)),
            dma((5,)),
        ],
        compiler_params=pltpu.CompilerParams(collective_id=0, has_side_effects=True, vmem_limit_bytes=limit),
    )(density, velocity, energy, shifts, fraction)
    return pl.pallas_call(
        write_out,
        out_shape=tuple(jax.ShapeDtypeStruct(v.shape, f32) for v in (density, velocity, energy)),
        in_specs=[hbm],
        out_specs=(hbm,) * 3,
        scratch_shapes=[pltpu.VMEM(block, f32)] + fields + [dma((5,)), dma((5,))],
        compiler_params=pltpu.CompilerParams(vmem_limit_bytes=limit),
    )(back)


def solution(mesh):
    placed = (
        P(None, "rad", "az"),
        P(None, None, "rad", "az"),
        P(None, "rad", "az"),
        P("rad"),
        P("rad"),
    )
    return jax.shard_map(
        shards,
        mesh=mesh,
        in_specs=placed,
        out_specs=(P(None, "rad", "az"), P(None, None, "rad", "az"), P(None, "rad", "az")),
        check_vma=False,
    )
```

```python
import jax
import jax.numpy as jnp
from jax import lax
from jax.experimental import pallas as pl
from jax.experimental.pallas import tpu as pltpu
from jax.sharding import PartitionSpec as P

MESH = pl.DeviceIdType.MESH
AZ = 16
QUADS = 32
CHUNKS = 32
CELLS = 4096
STEPS = 2

EN, VT, VR, DE, VP = range(5)
EARLY, LATE = (EN, VT, VR), (DE, VP)
GROUPS = (EARLY, LATE)
SPANS = (pl.ds(0, 3), pl.ds(3, 2))
S_AT = {VR: 0, EN: 1, VT: 2, VP: 3}
F_AT = {DE: 0, VP: 1, VR: 2, EN: 3, VT: 4}
UNROLL = 8
ORDER = (10, 8, 6, 4, 14, 12, 2, 11, 9, 7, 5, 15, 13, 3, 1)


def owner(pair, half):
    return lax.div(pair, 2) * 4 + (1 - half) * 2 + lax.rem(pair, 2)


def prev_cell(x, lane):
    x1 = pltpu.roll(x, 1, 1)
    return jnp.where(lane == 0, pltpu.roll(x1, 1, 0), x1)


def next_cell(x, lane):
    x1 = pltpu.roll(x, 127, 1)
    return jnp.where(lane == 127, pltpu.roll(x1, CHUNKS - 1, 0), x1)


def kernel(
    den_hbm, vel_hbm, ene_hbm, shift_hbm, frac_hbm,
    back,
    den_ref, vel_ref, ene_ref, shift_ref, frac_ref,
    stage, rows, s0, s1, f0, f1, speed, factor, along, flux, blended, ostage,
    a_send, a_recv, h_send, h_recv, b_send, b_recv, l_sem, i_sem,
):
    a = lax.axis_index("az")
    rho = lax.axis_index("rad")
    x, y, core = lax.div(a, 4), lax.rem(lax.div(a, 2), 2), lax.rem(a, 2)
    half = 1 - y
    pair = 2 * x + core
    quad = 2 * rho + half
    states, fresh = (s0, s1), (f0, f1)

    loads = [
        pltpu.make_async_copy(src, dst, i_sem.at[n])
        for n, (src, dst) in enumerate((
            (ene_hbm, ene_ref), (vel_hbm, vel_ref), (den_hbm, den_ref), (shift_hbm, shift_ref), (frac_hbm, frac_ref)
        ))
    ]
    for copy in loads[:3]:
        copy.start()

    peers = []
    for k in range(AZ):
        dx, dy, dc = k // 4, (k // 2) % 2, k % 2
        peers.append(lax.rem(x + dx, 4) * 4 + lax.rem(y + dy, 2) * 2 + lax.rem(core + dc, 2))

    barrier = pltpu.get_barrier_semaphore()
    for k in range(1, AZ):
        pl.semaphore_signal(barrier, inc=1, device_id={"az": peers[k], "rad": rho}, device_id_type=MESH)
    cross = lax.rem(quad + 2 * half - 1 + QUADS, QUADS)
    has_cross = jnp.logical_and(quad > 0, quad < QUADS - 1)

    @pl.when(has_cross)
    def _():
        pl.semaphore_signal(
            barrier, inc=1, device_id={"az": owner(pair, lax.rem(cross, 2)), "rad": lax.div(cross, 2)},
            device_id_type=MESH,
        )

    for copy in loads[3:]:
        copy.start()

    inner_t, inner_r = pl.ds(1, 2), pl.ds(1, 4)
    for buf, span in ((s0, pl.ds(0, 3)), (s1, pl.ds(0, 3)), (f0, pl.ds(0, 5)), (f1, pl.ds(0, 5))):
        def clear(where):
            buf[where] = jnp.zeros_like(buf[where])

        pl.when(pair == 0)(lambda: clear((span, 0, inner_r)))
        pl.when(pair == 7)(lambda: clear((span, 3, inner_r)))
        pl.when(quad == 0)(lambda: clear((span, inner_t, 0)))
        pl.when(quad == QUADS - 1)(lambda: clear((span, inner_t, 5)))

    sources = {VT: vel_ref.at[2], EN: ene_ref, VR: vel_ref.at[1], DE: den_ref, VP: vel_ref.at[0]}

    def regroup(fields):
        def one(tp, _):
            for h in range(2):
                dest = owner(tp, h)
                for f in fields:
                    for c in range(2):
                        for t in range(2):
                            stage[dest, f, pl.ds(c * 8 + t * 4, 4), :] = sources[f][
                                2 * tp + t, pl.ds(4 * h, 4), pl.ds(128 * c, 128)
                            ]
            return 0

        lax.fori_loop(0, 8, one, 0)

    def to_rows(k, g):
        dest = peers[k]
        return pltpu.make_async_remote_copy(
            src_ref=stage.at[dest, SPANS[g]],
            dst_ref=rows.at[SPANS[g], pl.ds(pl.multiple_of(a * 16, 16), 16), :],
            send_sem=a_send.at[g, k],
            recv_sem=a_recv.at[g],
            device_id={"az": dest, "rad": rho},
            device_id_type=MESH,
        )

    def own_rows(g):
        return pltpu.make_async_copy(
            stage.at[a, SPANS[g]], rows.at[SPANS[g], pl.ds(pl.multiple_of(a * 16, 16), 16), :], a_recv.at[g]
        )

    for copy in loads[:2]:
        copy.wait()
    regroup(EARLY)
    pl.semaphore_wait(barrier, AZ - 1 + has_cross.astype(jnp.int32))
    for k in ORDER:
        to_rows(k, 0).start()
    own_rows(0).start()
    for copy in loads[2:]:
        copy.wait()
    regroup(LATE)
    for k in ORDER:
        to_rows(k, 1).start()
    own_rows(1).start()

    lane = lax.broadcasted_iota(jnp.int32, (CHUNKS, 128), 1)
    lane8 = lax.broadcasted_iota(jnp.int32, (8, 128), 1)

    t_up, t_dn = lax.rem(pair + 1, 8), lax.rem(pair + 7, 8)
    r_up, r_dn = lax.rem(quad + 1, QUADS), lax.rem(quad + QUADS - 1, QUADS)
    has_tup, has_tdn = pair < 7, pair > 0
    has_rup, has_rdn = quad < QUADS - 1, quad > 0
    id_tup = {"az": owner(t_up, half), "rad": rho}
    id_tdn = {"az": owner(t_dn, half), "rad": rho}
    id_rup = {"az": owner(pair, lax.rem(r_up, 2)), "rad": lax.div(r_up, 2)}
    id_rdn = {"az": owner(pair, lax.rem(r_dn, 2)), "rad": lax.div(r_dn, 2)}

    def halo(buf, t_fields, r_fields, slot):
        def one(src, dst, ident, d):
            return pltpu.make_async_remote_copy(
                src_ref=src, dst_ref=dst, send_sem=h_send.at[slot, d], recv_sem=h_recv.at[slot, d],
                device_id=ident, device_id_type=MESH,
            )

        return (
            (one(buf.at[r_fields, inner_t, 4], buf.at[r_fields, inner_t, 0], id_rup, 2), has_rup, has_rdn),
            (one(buf.at[r_fields, inner_t, 1], buf.at[r_fields, inner_t, 5], id_rdn, 3), has_rdn, has_rup),
            (one(buf.at[t_fields, 2, inner_r], buf.at[t_fields, 0, inner_r], id_tup, 0), has_tup, has_tdn),
            (one(buf.at[t_fields, 1, inner_r], buf.at[t_fields, 3, inner_r], id_tdn, 1), has_tdn, has_tup),
        )

    def each(copies, what):
        for copy, sends, gets in copies:
            @pl.when(gets if what == "wait_recv" else sends)
            def _():
                getattr(copy, what)()

    def eight(body, unroll=1):
        def one(i, _):
            body(i, lax.div(i, 4) + 1, lax.rem(i, 4) + 1)
            return 0

        lax.fori_loop(0, 8, one, 0, unroll=unroll)

    def unpack(fields):
        def one(i, t, r):
            for q in fields:
                value = rows[q, pl.ds(i, CHUNKS, stride=8), :]
                if q == DE:
                    f0[F_AT[DE], t, r] = value
                else:
                    s0[S_AT[q], t, r] = value

        eight(one)

    def to_blocks(k, g):
        dest = peers[k]
        return pltpu.make_async_remote_copy(
            src_ref=ostage.at[SPANS[g], pl.ds(pl.multiple_of(dest * 16, 16), 16), :],
            dst_ref=back.at[a, SPANS[g]],
            send_sem=b_send.at[g, k],
            recv_sem=b_recv.at[g],
            device_id={"az": dest, "rad": rho},
            device_id_type=MESH,
        )

    def own_blocks(g):
        return pltpu.make_async_copy(
            ostage.at[SPANS[g], pl.ds(pl.multiple_of(a * 16, 16), 16), :], back.at[a, SPANS[g]], b_recv.at[g]
        )

    def old_halo(step, slot):
        return halo(states[step], S_AT[EN], S_AT[EN], slot), halo(states[step], S_AT[VT], S_AT[VR], slot + 1)

    def new_halo(step, slot):
        f = fresh[step]
        return halo(f, pl.ds(0, 2), pl.ds(0, 2), slot), halo(f, F_AT[VT], F_AT[VR], slot + 1)

    old_both = halo(s0, pl.ds(1, 2), pl.ds(0, 2), 0)
    new_en, rest = halo(f0, F_AT[EN], F_AT[EN], 1), halo(f0, F_AT[VR], F_AT[VT], 2)
    late0, new_v0 = new_halo(0, 3)
    old_en, old_v = old_halo(1, 5)
    late1, new_v1 = new_halo(1, 7)
    new_both = halo(f1, pl.ds(2, 2), pl.ds(3, 2), 9)
    lates, news = (late0, late1), (new_v0, new_v1)
    halos = (old_both, new_en, rest, late0, new_v0, old_en, old_v, late1, new_v1, new_both)

    def along_azimuth(f, i, t, r, fields):
        p_lo = speed[i]
        for q in fields:
            v = f[F_AT[q], t, r]
            low = p_lo * jnp.where(p_lo > 0, prev_cell(v, lane), v)
            flux[q, i] = next_cell(low, lane) - low

    def face(f, u, below, above):
        s = f[(F_AT[u],) + below] + f[(F_AT[u],) + above]
        up = s > 0
        return lambda q: s * jnp.where(up, f[(F_AT[q],) + below], f[(F_AT[q],) + above])

    def begin(step):
        s, f = states[step], fresh[step]

        def source_azimuth(i, t, r):
            den = f[F_AT[DE], t, r]
            k = 0.01 / jnp.where(den > 0, den, 1.0)
            e = s[S_AT[EN], t, r]
            vp = s[S_AT[VP], t, r]
            new = vp - k * (next_cell(e, lane) - prev_cell(e, lane))
            f[F_AT[VP], t, r] = new
            factor[i] = k
            along[i] = next_cell(vp, lane) - prev_cell(vp, lane)
            speed[i] = new + prev_cell(new, lane)

        eight(source_azimuth, UNROLL)
        each(lates[step], "start")

    for step in range(STEPS):
        s, f = states[step], fresh[step]
        last = step == STEPS - 1

        if step == 0:
            pltpu.make_async_copy(rows.at[SPANS[0]], rows.at[SPANS[0]], a_recv.at[0]).wait()
            unpack(EARLY)
            each(old_both, "start")
            pltpu.make_async_copy(rows.at[SPANS[1]], rows.at[SPANS[1]], a_recv.at[1]).wait()
            unpack(LATE)
            begin(0)

        def azimuth_late(i, t, r):
            along_azimuth(f, i, t, r, LATE)

        eight(azimuth_late)

        def source_speeds(i, t, r):
            k = factor[i]
            f[F_AT[VR], t, r] = s[S_AT[VR], t, r] - k * (s[S_AT[EN], t, r + 1] - s[S_AT[EN], t, r - 1])
            f[F_AT[VT], t, r] = s[S_AT[VT], t, r] - k * (s[S_AT[EN], t + 1, r] - s[S_AT[EN], t - 1, r])

        def source_energy(i, t, r):
            e = s[S_AT[EN], t, r]
            div = (
                along[i]
                + (s[S_AT[VR], t, r + 1] - s[S_AT[VR], t, r - 1])
                + (s[S_AT[VT], t + 1, r] - s[S_AT[VT], t - 1, r])
            )
            f[F_AT[EN], t, r] = e - 0.01 * e * div

        if last:
            each(old_en, "wait_recv")
            eight(source_speeds, UNROLL)
            each(new_v1, "start")
            each(old_v, "wait_recv")
            eight(source_energy, UNROLL)
            each(new_both, "start")
        else:
            each(old_both, "wait_recv")
            eight(source_energy, UNROLL)
            each(new_en, "start")
            eight(source_speeds, UNROLL)
            each(new_v0, "start")
            each(rest, "start")

        def azimuth_early(i, t, r):
            along_azimuth(f, i, t, r, EARLY)

        eight(azimuth_early)

        def inner_radius(n, _):
            t, r = lax.div(n, 3), lax.rem(n, 3)
            one = face(f, VR, (t + 1, r + 1), (t + 1, r + 2))
            for q in range(5):
                v = one(q)
                flux[q, 4 * t + r] += v
                flux[q, 4 * t + r + 1] -= v
            return 0

        lax.fori_loop(0, 6, inner_radius, 0)

        def inner_theta(r, _):
            one = face(f, VT, (1, r + 1), (2, r + 1))
            for q in range(5):
                v = one(q)
                flux[q, r] += v
                flux[q, 4 + r] -= v
            return 0

        lax.fori_loop(0, 4, inner_theta, 0)

        each(news[step], "wait_recv")

        for g, fields in ((1, LATE), (0, EARLY)) if last else ((0, (EN,)), (0, (VT, VR)), (1, LATE)):
            if DE in fields:
                each(lates[step], "wait_recv")
            elif last:
                each(new_both, "wait_recv")
            else:
                each(new_en if EN in fields else rest, "wait_recv")

            def outer_radius(t, _):
                low = face(f, VR, (t + 1, 0), (t + 1, 1))
                high = face(f, VR, (t + 1, 4), (t + 1, 5))
                for q in fields:
                    flux[q, 4 * t] -= low(q)
                    flux[q, 4 * t + 3] += high(q)
                return 0

            lax.fori_loop(0, 2, outer_radius, 0)

            def outer_theta(r, _):
                low = face(f, VT, (0, r + 1), (1, r + 1))
                high = face(f, VT, (2, r + 1), (3, r + 1))
                for q in fields:
                    flux[q, r] -= low(q)
                    flux[q, 4 + r] += high(q)
                return 0

            lax.fori_loop(0, 4, outer_theta, 0)

            def finish(i, t, r):
                for q in fields:
                    moved = f[F_AT[q], t, r] - 0.025 * flux[q, i]
                    blended[q, i, pl.ds(0, CHUNKS), :] = moved
                    blended[q, i, pl.ds(CHUNKS, CHUNKS), :] = moved

            eight(finish, UNROLL)

            def rotate(i, t, r):
                w = frac_ref[half * 4 + r - 1]
                shift = shift_ref[half * 4 + r - 1]
                views = []
                for back_cells in (0, 1):
                    ahead = lax.rem(2 * CELLS - shift - back_cells, CELLS)
                    views.append((lax.div(ahead, 128), lax.rem(ahead, 128)))
                for q in fields:
                    for m in range(4):
                        parts = []
                        for whole, part in views:
                            near = blended[q, i, pl.ds(whole + 8 * m, 8), :]
                            far = blended[q, i, pl.ds(whole + 8 * m + 1, 8), :]
                            parts.append(pltpu.roll(jnp.where(lane8 < part, far, near), lax.rem(128 - part, 128), 1))
                        out = (1.0 - w) * parts[0] + w * parts[1]
                        if last:
                            ostage[q, pl.ds(64 * m + i, 8, stride=8), :] = out
                        elif q == DE:
                            f1[F_AT[DE], t, r, pl.ds(8 * m, 8), :] = out
                        else:
                            s1[S_AT[q], t, r, pl.ds(8 * m, 8), :] = out

            eight(rotate, UNROLL)
            if last:
                for k in ORDER:
                    to_blocks(k, g).start()
                own_blocks(g).start()
            elif EN in fields:
                each(old_en, "start")
            elif VT in fields:
                each(old_v, "start")
            else:
                begin(step + 1)

    for copies in halos:
        each(copies, "wait_send")
    for g in range(2):
        for k in range(1, AZ):
            to_rows(k, g).wait_send()
            to_blocks(k, g).wait_send()
    for g in range(2):
        pltpu.make_async_copy(back.at[:, SPANS[g]], back.at[:, SPANS[g]], b_recv.at[g]).wait()


def write_out(back, den_hbm, vel_hbm, ene_hbm, blocks, den_out, vel_out, ene_out, in_sem, out_sem):
    targets = {
        VT: (vel_out.at[2], vel_hbm.at[2]), EN: (ene_out, ene_hbm), VR: (vel_out.at[1], vel_hbm.at[1]),
        DE: (den_out, den_hbm), VP: (vel_out.at[0], vel_hbm.at[0]),
    }
    reads = [pltpu.make_async_copy(back.at[:, q], blocks.at[:, q], in_sem.at[q]) for q in range(5)]
    for copy in reads:
        copy.start()
    writes = []
    for q in range(5):
        reads[q].wait()
        dst = targets[q][0]

        def one(tp, _):
            for h in range(2):
                src = owner(tp, h)
                for c in range(2):
                    for t in range(2):
                        dst[2 * tp + t, pl.ds(4 * h, 4), pl.ds(128 * c, 128)] = blocks[
                            src, q, pl.ds(c * 8 + t * 4, 4), :
                        ]
            return 0

        lax.fori_loop(0, 8, one, 0, unroll=8)
        writes.append(pltpu.make_async_copy(*targets[q], out_sem.at[q]))
        writes[-1].start()
    for copy in writes:
        copy.wait()


def shards(density, velocity, energy, shifts, fraction):
    hbm = pl.BlockSpec(memory_space=pl.ANY)
    f32 = jnp.float32
    limit = 60 * 1024 * 1024
    block = (AZ, 5, 16, 128)
    dma = pltpu.SemaphoreType.DMA
    fields = [pltpu.VMEM(v.shape, f32) for v in (density, velocity, energy)]
    back = pl.pallas_call(
        kernel,
        out_shape=jax.ShapeDtypeStruct(block, f32),
        in_specs=[hbm] * 5,
        out_specs=hbm,
        scratch_shapes=fields + [
            pltpu.SMEM(shifts.shape, jnp.int32),
            pltpu.SMEM(fraction.shape, f32),
            pltpu.VMEM(block, f32),
            pltpu.VMEM((5, 256, 128), f32),
            pltpu.VMEM((4, 4, 6, CHUNKS, 128), f32),
            pltpu.VMEM((4, 4, 6, CHUNKS, 128), f32),
            pltpu.VMEM((5, 4, 6, CHUNKS, 128), f32),
            pltpu.VMEM((5, 4, 6, CHUNKS, 128), f32),
            pltpu.VMEM((8, CHUNKS, 128), f32),
            pltpu.VMEM((8, CHUNKS, 128), f32),
            pltpu.VMEM((8, CHUNKS, 128), f32),
            pltpu.VMEM((5, 8, CHUNKS, 128), f32),
            pltpu.VMEM((5, 8, 2 * CHUNKS, 128), f32),
            pltpu.VMEM((5, 256, 128), f32),
            dma((2, AZ)),
            dma((2,)),
            dma((10, 4)),
            dma((10, 4)),
            dma((2, AZ)),
            dma((2,)),
            dma((4,)),
            dma((5,)),
        ],
        compiler_params=pltpu.CompilerParams(collective_id=0, has_side_effects=True, vmem_limit_bytes=limit),
    )(density, velocity, energy, shifts, fraction)
    return pl.pallas_call(
        write_out,
        out_shape=tuple(jax.ShapeDtypeStruct(v.shape, f32) for v in (density, velocity, energy)),
        in_specs=[hbm],
        out_specs=(hbm,) * 3,
        scratch_shapes=[pltpu.VMEM(block, f32)] + fields + [dma((5,)), dma((5,))],
        compiler_params=pltpu.CompilerParams(vmem_limit_bytes=limit),
    )(back)


def solution(mesh):
    placed = (
        P(None, "rad", "az"),
        P(None, None, "rad", "az"),
        P(None, "rad", "az"),
        P("rad"),
        P("rad"),
    )
    return jax.shard_map(
        shards,
        mesh=mesh,
        in_specs=placed,
        out_specs=(P(None, "rad", "az"), P(None, None, "rad", "az"), P(None, "rad", "az")),
        check_vma=False,
    )
```

```python
import jax
import jax.numpy as jnp
from jax import lax
from jax.experimental import pallas as pl
from jax.experimental.pallas import tpu as pltpu
from jax.sharding import PartitionSpec as P

MESH = pl.DeviceIdType.MESH
AZ = 16
QUADS = 32
CHUNKS = 32
CELLS = 4096
STEPS = 2

EN, VT, VR, DE, VP = range(5)
EARLY, LATE = (EN, VT, VR), (DE, VP)
GROUPS = (EARLY, LATE)
SPANS = (pl.ds(0, 3), pl.ds(3, 2))
S_AT = {VR: 0, EN: 1, VT: 2, VP: 3}
F_AT = {DE: 0, VP: 1, VR: 2, EN: 3, VT: 4}
UNROLL = 8
ORDER = (10, 8, 6, 4, 14, 12, 2, 11, 9, 7, 5, 15, 13, 3, 1)


def owner(pair, half):
    return lax.div(pair, 2) * 4 + (1 - half) * 2 + lax.rem(pair, 2)


def prev_cell(x, lane):
    x1 = pltpu.roll(x, 1, 1)
    return jnp.where(lane == 0, pltpu.roll(x1, 1, 0), x1)


def next_cell(x, lane):
    x1 = pltpu.roll(x, 127, 1)
    return jnp.where(lane == 127, pltpu.roll(x1, CHUNKS - 1, 0), x1)


def kernel(
    den_hbm, vel_hbm, ene_hbm, shift_hbm, frac_hbm,
    back,
    den_ref, vel_ref, ene_ref, shift_ref, frac_ref,
    stage, rows, s0, s1, f0, f1, speed, factor, along, flux, blended, ostage,
    a_send, a_recv, h_send, h_recv, b_send, b_recv, l_sem, i_sem,
):
    a = lax.axis_index("az")
    rho = lax.axis_index("rad")
    x, y, core = lax.div(a, 4), lax.rem(lax.div(a, 2), 2), lax.rem(a, 2)
    half = 1 - y
    pair = 2 * x + core
    quad = 2 * rho + half
    states, fresh = (s0, s1), (f0, f1)

    loads = [
        pltpu.make_async_copy(src, dst, i_sem.at[n])
        for n, (src, dst) in enumerate((
            (ene_hbm, ene_ref), (vel_hbm, vel_ref), (den_hbm, den_ref), (shift_hbm, shift_ref), (frac_hbm, frac_ref)
        ))
    ]
    for copy in loads[:3]:
        copy.start()

    peers = []
    for k in range(AZ):
        dx, dy, dc = k // 4, (k // 2) % 2, k % 2
        peers.append(lax.rem(x + dx, 4) * 4 + lax.rem(y + dy, 2) * 2 + lax.rem(core + dc, 2))

    barrier = pltpu.get_barrier_semaphore()
    for k in range(1, AZ):
        pl.semaphore_signal(barrier, inc=1, device_id={"az": peers[k], "rad": rho}, device_id_type=MESH)
    cross = lax.rem(quad + 2 * half - 1 + QUADS, QUADS)
    has_cross = jnp.logical_and(quad > 0, quad < QUADS - 1)

    @pl.when(has_cross)
    def _():
        pl.semaphore_signal(
            barrier, inc=1, device_id={"az": owner(pair, lax.rem(cross, 2)), "rad": lax.div(cross, 2)},
            device_id_type=MESH,
        )

    for copy in loads[3:]:
        copy.start()

    inner_t, inner_r = pl.ds(1, 2), pl.ds(1, 4)
    for buf, span in ((s0, pl.ds(0, 3)), (s1, pl.ds(0, 3)), (f0, pl.ds(0, 5)), (f1, pl.ds(0, 5))):
        def clear(where):
            buf[where] = jnp.zeros_like(buf[where])

        pl.when(pair == 0)(lambda: clear((span, 0, inner_r)))
        pl.when(pair == 7)(lambda: clear((span, 3, inner_r)))
        pl.when(quad == 0)(lambda: clear((span, inner_t, 0)))
        pl.when(quad == QUADS - 1)(lambda: clear((span, inner_t, 5)))

    sources = {VT: vel_ref.at[2], EN: ene_ref, VR: vel_ref.at[1], DE: den_ref, VP: vel_ref.at[0]}

    def regroup(fields):
        def one(tp, _):
            for h in range(2):
                dest = owner(tp, h)
                for f in fields:
                    for c in range(2):
                        for t in range(2):
                            stage[dest, f, pl.ds(c * 8 + t * 4, 4), :] = sources[f][
                                2 * tp + t, pl.ds(4 * h, 4), pl.ds(128 * c, 128)
                            ]
            return 0

        lax.fori_loop(0, 8, one, 0)

    def to_rows(k, g):
        dest = peers[k]
        return pltpu.make_async_remote_copy(
            src_ref=stage.at[dest, SPANS[g]],
            dst_ref=rows.at[SPANS[g], pl.ds(pl.multiple_of(a * 16, 16), 16), :],
            send_sem=a_send.at[g, k],
            recv_sem=a_recv.at[g],
            device_id={"az": dest, "rad": rho},
            device_id_type=MESH,
        )

    def own_rows(g):
        return pltpu.make_async_copy(
            stage.at[a, SPANS[g]], rows.at[SPANS[g], pl.ds(pl.multiple_of(a * 16, 16), 16), :], a_recv.at[g]
        )

    for copy in loads[:2]:
        copy.wait()
    regroup(EARLY)
    pl.semaphore_wait(barrier, AZ - 1 + has_cross.astype(jnp.int32))
    for k in ORDER:
        to_rows(k, 0).start()
    own_rows(0).start()
    for copy in loads[2:]:
        copy.wait()
    regroup(LATE)
    for k in ORDER:
        to_rows(k, 1).start()
    own_rows(1).start()

    lane = lax.broadcasted_iota(jnp.int32, (CHUNKS, 128), 1)
    lane8 = lax.broadcasted_iota(jnp.int32, (8, 128), 1)

    t_up, t_dn = lax.rem(pair + 1, 8), lax.rem(pair + 7, 8)
    r_up, r_dn = lax.rem(quad + 1, QUADS), lax.rem(quad + QUADS - 1, QUADS)
    has_tup, has_tdn = pair < 7, pair > 0
    has_rup, has_rdn = quad < QUADS - 1, quad > 0
    id_tup = {"az": owner(t_up, half), "rad": rho}
    id_tdn = {"az": owner(t_dn, half), "rad": rho}
    id_rup = {"az": owner(pair, lax.rem(r_up, 2)), "rad": lax.div(r_up, 2)}
    id_rdn = {"az": owner(pair, lax.rem(r_dn, 2)), "rad": lax.div(r_dn, 2)}

    def halo(buf, t_fields, r_fields, slot):
        def one(src, dst, ident, d):
            return pltpu.make_async_remote_copy(
                src_ref=src, dst_ref=dst, send_sem=h_send.at[slot, d], recv_sem=h_recv.at[slot, d],
                device_id=ident, device_id_type=MESH,
            )

        return (
            (one(buf.at[r_fields, inner_t, 4], buf.at[r_fields, inner_t, 0], id_rup, 2), has_rup, has_rdn),
            (one(buf.at[r_fields, inner_t, 1], buf.at[r_fields, inner_t, 5], id_rdn, 3), has_rdn, has_rup),
            (one(buf.at[t_fields, 2, inner_r], buf.at[t_fields, 0, inner_r], id_tup, 0), has_tup, has_tdn),
            (one(buf.at[t_fields, 1, inner_r], buf.at[t_fields, 3, inner_r], id_tdn, 1), has_tdn, has_tup),
        )

    def each(copies, what):
        for copy, sends, gets in copies:
            @pl.when(gets if what == "wait_recv" else sends)
            def _():
                getattr(copy, what)()

    def eight(body, unroll=1):
        def one(i, _):
            body(i, lax.div(i, 4) + 1, lax.rem(i, 4) + 1)
            return 0

        lax.fori_loop(0, 8, one, 0, unroll=unroll)

    def unpack(fields):
        def one(i, t, r):
            for q in fields:
                value = rows[q, pl.ds(i, CHUNKS, stride=8), :]
                if q == DE:
                    f0[F_AT[DE], t, r] = value
                else:
                    s0[S_AT[q], t, r] = value

        eight(one)

    def to_blocks(k, g):
        dest = peers[k]
        return pltpu.make_async_remote_copy(
            src_ref=ostage.at[SPANS[g], pl.ds(pl.multiple_of(dest * 16, 16), 16), :],
            dst_ref=back.at[a, SPANS[g]],
            send_sem=b_send.at[g, k],
            recv_sem=b_recv.at[g],
            device_id={"az": dest, "rad": rho},
            device_id_type=MESH,
        )

    def own_blocks(g):
        return pltpu.make_async_copy(
            ostage.at[SPANS[g], pl.ds(pl.multiple_of(a * 16, 16), 16), :], back.at[a, SPANS[g]], b_recv.at[g]
        )

    def old_halo(step, slot):
        return halo(states[step], S_AT[EN], S_AT[EN], slot), halo(states[step], S_AT[VT], S_AT[VR], slot + 1)

    def new_halo(step, slot):
        f = fresh[step]
        return halo(f, pl.ds(0, 2), pl.ds(0, 2), slot), halo(f, F_AT[VT], F_AT[VR], slot + 1)

    old_both = halo(s0, pl.ds(1, 2), pl.ds(0, 2), 0)
    new_en, rest = halo(f0, F_AT[EN], F_AT[EN], 1), halo(f0, F_AT[VR], F_AT[VT], 2)
    late0, new_v0 = new_halo(0, 3)
    old_en, old_v = old_halo(1, 5)
    late1, new_v1 = new_halo(1, 7)
    new_both = halo(f1, pl.ds(2, 2), pl.ds(3, 2), 9)
    lates, news = (late0, late1), (new_v0, new_v1)
    halos = (old_both, new_en, rest, late0, new_v0, old_en, old_v, late1, new_v1, new_both)

    def along_azimuth(f, i, t, r, fields):
        p_lo = speed[i]
        for q in fields:
            v = f[F_AT[q], t, r]
            low = p_lo * jnp.where(p_lo > 0, prev_cell(v, lane), v)
            flux[q, i] = next_cell(low, lane) - low

    def face(f, u, below, above):
        s = f[(F_AT[u],) + below] + f[(F_AT[u],) + above]
        up = s > 0
        return lambda q: s * jnp.where(up, f[(F_AT[q],) + below], f[(F_AT[q],) + above])

    def begin(step):
        s, f = states[step], fresh[step]

        def source_azimuth(i, t, r):
            den = f[F_AT[DE], t, r]
            k = 0.01 / jnp.where(den > 0, den, 1.0)
            e = s[S_AT[EN], t, r]
            vp = s[S_AT[VP], t, r]
            new = vp - k * (next_cell(e, lane) - prev_cell(e, lane))
            f[F_AT[VP], t, r] = new
            factor[i] = k
            along[i] = next_cell(vp, lane) - prev_cell(vp, lane)
            speed[i] = new + prev_cell(new, lane)

        eight(source_azimuth, UNROLL)
        each(lates[step], "start")

    for step in range(STEPS):
        s, f = states[step], fresh[step]
        last = step == STEPS - 1

        if step == 0:
            pltpu.make_async_copy(rows.at[SPANS[0]], rows.at[SPANS[0]], a_recv.at[0]).wait()
            unpack(EARLY)
            each(old_both, "start")
            pltpu.make_async_copy(rows.at[SPANS[1]], rows.at[SPANS[1]], a_recv.at[1]).wait()
            unpack(LATE)
            begin(0)

        def azimuth_late(i, t, r):
            along_azimuth(f, i, t, r, LATE)

        eight(azimuth_late)

        def source_speeds(i, t, r):
            k = factor[i]
            f[F_AT[VR], t, r] = s[S_AT[VR], t, r] - k * (s[S_AT[EN], t, r + 1] - s[S_AT[EN], t, r - 1])
            f[F_AT[VT], t, r] = s[S_AT[VT], t, r] - k * (s[S_AT[EN], t + 1, r] - s[S_AT[EN], t - 1, r])

        def source_energy(i, t, r):
            e = s[S_AT[EN], t, r]
            div = (
                along[i]
                + (s[S_AT[VR], t, r + 1] - s[S_AT[VR], t, r - 1])
                + (s[S_AT[VT], t + 1, r] - s[S_AT[VT], t - 1, r])
            )
            f[F_AT[EN], t, r] = e - 0.01 * e * div

        if last:
            each(old_en, "wait_recv")
            eight(source_speeds, UNROLL)
            each(new_v1, "start")
            each(old_v, "wait_recv")
            eight(source_energy, UNROLL)
            each(new_both, "start")
        else:
            each(old_both, "wait_recv")
            eight(source_energy, UNROLL)
            each(new_en, "start")
            eight(source_speeds, UNROLL)
            each(new_v0, "start")
            each(rest, "start")

        def azimuth_early(i, t, r):
            along_azimuth(f, i, t, r, EARLY)

        eight(azimuth_early)

        def inner_radius(n, _):
            t, r = lax.div(n, 3), lax.rem(n, 3)
            one = face(f, VR, (t + 1, r + 1), (t + 1, r + 2))
            for q in range(5):
                v = one(q)
                flux[q, 4 * t + r] += v
                flux[q, 4 * t + r + 1] -= v
            return 0

        lax.fori_loop(0, 6, inner_radius, 0)

        def inner_theta(r, _):
            one = face(f, VT, (1, r + 1), (2, r + 1))
            for q in range(5):
                v = one(q)
                flux[q, r] += v
                flux[q, 4 + r] -= v
            return 0

        lax.fori_loop(0, 4, inner_theta, 0)

        each(news[step], "wait_recv")

        for g, fields in ((1, LATE), (0, EARLY)) if last else ((0, (EN,)), (0, (VT, VR)), (1, LATE)):
            if DE in fields:
                each(lates[step], "wait_recv")
            elif last:
                each(new_both, "wait_recv")
            else:
                each(new_en if EN in fields else rest, "wait_recv")

            def outer_radius(t, _):
                low = face(f, VR, (t + 1, 0), (t + 1, 1))
                high = face(f, VR, (t + 1, 4), (t + 1, 5))
                for q in fields:
                    flux[q, 4 * t] -= low(q)
                    flux[q, 4 * t + 3] += high(q)
                return 0

            lax.fori_loop(0, 2, outer_radius, 0)

            def outer_theta(r, _):
                low = face(f, VT, (0, r + 1), (1, r + 1))
                high = face(f, VT, (2, r + 1), (3, r + 1))
                for q in fields:
                    flux[q, r] -= low(q)
                    flux[q, 4 + r] += high(q)
                return 0

            lax.fori_loop(0, 4, outer_theta, 0)

            def finish(i, t, r):
                for q in fields:
                    moved = f[F_AT[q], t, r] - 0.025 * flux[q, i]
                    blended[q, i, pl.ds(0, CHUNKS), :] = moved
                    blended[q, i, pl.ds(CHUNKS, CHUNKS), :] = moved

            eight(finish, UNROLL)

            def rotate(i, t, r):
                w = frac_ref[half * 4 + r - 1]
                shift = shift_ref[half * 4 + r - 1]
                views = []
                for back_cells in (0, 1):
                    ahead = lax.rem(2 * CELLS - shift - back_cells, CELLS)
                    views.append((lax.div(ahead, 128), lax.rem(ahead, 128)))
                for q in fields:
                    for m in range(4):
                        parts = []
                        for whole, part in views:
                            near = blended[q, i, pl.ds(whole + 8 * m, 8), :]
                            far = blended[q, i, pl.ds(whole + 8 * m + 1, 8), :]
                            parts.append(pltpu.roll(jnp.where(lane8 < part, far, near), lax.rem(128 - part, 128), 1))
                        out = (1.0 - w) * parts[0] + w * parts[1]
                        if last:
                            ostage[q, pl.ds(64 * m + i, 8, stride=8), :] = out
                        elif q == DE:
                            f1[F_AT[DE], t, r, pl.ds(8 * m, 8), :] = out
                        else:
                            s1[S_AT[q], t, r, pl.ds(8 * m, 8), :] = out

            eight(rotate, UNROLL)
            if last:
                for k in ORDER:
                    to_blocks(k, g).start()
                own_blocks(g).start()
            elif EN in fields:
                each(old_en, "start")
            elif VT in fields:
                each(old_v, "start")
            else:
                begin(step + 1)

    for copies in halos:
        each(copies, "wait_send")
    for g in range(2):
        for k in range(1, AZ):
            to_rows(k, g).wait_send()
            to_blocks(k, g).wait_send()
    for g in range(2):
        pltpu.make_async_copy(back.at[:, SPANS[g]], back.at[:, SPANS[g]], b_recv.at[g]).wait()


def write_out(back, den_hbm, vel_hbm, ene_hbm, den_out, vel_out, ene_out, out_sem):
    targets = {
        VT: (vel_out.at[2], vel_hbm.at[2]), EN: (ene_out, ene_hbm), VR: (vel_out.at[1], vel_hbm.at[1]),
        DE: (den_out, den_hbm), VP: (vel_out.at[0], vel_hbm.at[0]),
    }
    writes = []
    for q in range(5):
        dst = targets[q][0]

        def one(tp, _):
            for h in range(2):
                src = owner(tp, h)
                for c in range(2):
                    for t in range(2):
                        dst[2 * tp + t, pl.ds(4 * h, 4), pl.ds(128 * c, 128)] = back[
                            src, q, pl.ds(c * 8 + t * 4, 4), :
                        ]
            return 0

        lax.fori_loop(0, 8, one, 0, unroll=8)
        writes.append(pltpu.make_async_copy(*targets[q], out_sem.at[q]))
        writes[-1].start()
    for copy in writes:
        copy.wait()


def shards(density, velocity, energy, shifts, fraction):
    hbm = pl.BlockSpec(memory_space=pl.ANY)
    f32 = jnp.float32
    limit = 40 * 1024 * 1024
    block = (AZ, 5, 16, 128)
    dma = pltpu.SemaphoreType.DMA
    fields = [pltpu.VMEM(v.shape, f32) for v in (density, velocity, energy)]
    back = pl.pallas_call(
        kernel,
        out_shape=pltpu.VMEM(block, f32),
        in_specs=[hbm] * 5,
        out_specs=hbm,
        scratch_shapes=fields + [
            pltpu.SMEM(shifts.shape, jnp.int32),
            pltpu.SMEM(fraction.shape, f32),
            pltpu.VMEM(block, f32),
            pltpu.VMEM((5, 256, 128), f32),
            pltpu.VMEM((4, 4, 6, CHUNKS, 128), f32),
            pltpu.VMEM((4, 4, 6, CHUNKS, 128), f32),
            pltpu.VMEM((5, 4, 6, CHUNKS, 128), f32),
            pltpu.VMEM((5, 4, 6, CHUNKS, 128), f32),
            pltpu.VMEM((8, CHUNKS, 128), f32),
            pltpu.VMEM((8, CHUNKS, 128), f32),
            pltpu.VMEM((8, CHUNKS, 128), f32),
            pltpu.VMEM((5, 8, CHUNKS, 128), f32),
            pltpu.VMEM((5, 8, 2 * CHUNKS, 128), f32),
            pltpu.VMEM((5, 256, 128), f32),
            dma((2, AZ)),
            dma((2,)),
            dma((10, 4)),
            dma((10, 4)),
            dma((2, AZ)),
            dma((2,)),
            dma((4,)),
            dma((5,)),
        ],
        compiler_params=pltpu.CompilerParams(collective_id=0, has_side_effects=True, vmem_limit_bytes=limit),
    )(*(pltpu.with_memory_space_constraint(v, pltpu.HBM) for v in (density, velocity, energy, shifts, fraction)))
    return pl.pallas_call(
        write_out,
        out_shape=tuple(jax.ShapeDtypeStruct(v.shape, f32) for v in (density, velocity, energy)),
        in_specs=[pl.BlockSpec(memory_space=pltpu.VMEM)],
        out_specs=(hbm,) * 3,
        scratch_shapes=fields + [dma((5,))],
        compiler_params=pltpu.CompilerParams(vmem_limit_bytes=16 * 1024 * 1024),
    )(pltpu.with_memory_space_constraint(back, pltpu.VMEM))


def solution(mesh):
    placed = (
        P(None, "rad", "az"),
        P(None, None, "rad", "az"),
        P(None, "rad", "az"),
        P("rad"),
        P("rad"),
    )
    return jax.shard_map(
        shards,
        mesh=mesh,
        in_specs=placed,
        out_specs=(P(None, "rad", "az"), P(None, None, "rad", "az"), P(None, "rad", "az")),
        check_vma=False,
    )
```

```python
import jax
import jax.numpy as jnp
from jax import lax
from jax.experimental import pallas as pl
from jax.experimental.pallas import tpu as pltpu
from jax.sharding import PartitionSpec as P

MESH = pl.DeviceIdType.MESH
AZ = 16
QUADS = 32
CHUNKS = 32
CELLS = 4096
STEPS = 2

EN, VT, VR, DE, VP = range(5)
EARLY, LATE = (EN, VT, VR), (DE, VP)
GROUPS = (EARLY, LATE)
SPANS = (pl.ds(0, 3), pl.ds(3, 2))
S_AT = {VR: 0, EN: 1, VT: 2, VP: 3}
F_AT = {DE: 0, VP: 1, VR: 2, EN: 3, VT: 4}
UNROLL = 8
ORDER = (10, 8, 6, 4, 14, 12, 2, 11, 9, 7, 5, 15, 13, 3, 1)


def owner(pair, half):
    return lax.div(pair, 2) * 4 + (1 - half) * 2 + lax.rem(pair, 2)


def prev_cell(x, lane):
    x1 = pltpu.roll(x, 1, 1)
    return jnp.where(lane == 0, pltpu.roll(x1, 1, 0), x1)


def next_cell(x, lane):
    x1 = pltpu.roll(x, 127, 1)
    return jnp.where(lane == 127, pltpu.roll(x1, CHUNKS - 1, 0), x1)


def kernel(
    den_hbm, vel_hbm, ene_hbm, shift_hbm, frac_hbm,
    back,
    den_ref, vel_ref, ene_ref, shift_ref, frac_ref,
    stage, rows, s0, s1, f0, f1, speed, factor, along, flux, blended, ostage,
    a_send, a_recv, h_send, h_recv, b_send, b_recv, l_sem, i_sem,
):
    a = lax.axis_index("az")
    rho = lax.axis_index("rad")
    x, y, core = lax.div(a, 4), lax.rem(lax.div(a, 2), 2), lax.rem(a, 2)
    half = 1 - y
    pair = 2 * x + core
    quad = 2 * rho + half
    states, fresh = (s0, s1), (f0, f1)

    loads = [
        pltpu.make_async_copy(src, dst, i_sem.at[n])
        for n, (src, dst) in enumerate((
            (ene_hbm, ene_ref), (vel_hbm, vel_ref), (den_hbm, den_ref), (shift_hbm, shift_ref), (frac_hbm, frac_ref)
        ))
    ]
    for copy in loads[:3]:
        copy.start()

    peers = []
    for k in range(AZ):
        dx, dy, dc = k // 4, (k // 2) % 2, k % 2
        peers.append(lax.rem(x + dx, 4) * 4 + lax.rem(y + dy, 2) * 2 + lax.rem(core + dc, 2))

    barrier = pltpu.get_barrier_semaphore()
    for k in range(1, AZ):
        pl.semaphore_signal(barrier, inc=1, device_id={"az": peers[k], "rad": rho}, device_id_type=MESH)
    cross = lax.rem(quad + 2 * half - 1 + QUADS, QUADS)
    has_cross = jnp.logical_and(quad > 0, quad < QUADS - 1)

    @pl.when(has_cross)
    def _():
        pl.semaphore_signal(
            barrier, inc=1, device_id={"az": owner(pair, lax.rem(cross, 2)), "rad": lax.div(cross, 2)},
            device_id_type=MESH,
        )

    for copy in loads[3:]:
        copy.start()

    inner_t, inner_r = pl.ds(1, 2), pl.ds(1, 4)
    own_t, own_r = pl.ds(2, 2), pl.ds(2, 4)
    low_two = pl.ds(0, 2)

    def clear(buf, where):
        buf[where] = jnp.zeros_like(buf[where])

    for buf in (f0, f1):
        pl.when(pair == 0)(lambda: clear(buf, (pl.ds(0, 5), 0, inner_r)))
        pl.when(pair == 7)(lambda: clear(buf, (pl.ds(0, 5), 3, inner_r)))
        pl.when(quad == 0)(lambda: clear(buf, (pl.ds(0, 5), inner_t, 0)))
        pl.when(quad == QUADS - 1)(lambda: clear(buf, (pl.ds(0, 5), inner_t, 5)))
    for buf in (s0, s1):
        pl.when(pair == 0)(lambda: clear(buf, (pl.ds(0, 3), low_two, own_r)))
        pl.when(pair == 7)(lambda: clear(buf, (pl.ds(0, 3), pl.ds(4, 2), own_r)))
        pl.when(quad == 0)(lambda: clear(buf, (pl.ds(0, 3), own_t, low_two)))
        pl.when(quad == QUADS - 1)(lambda: clear(buf, (pl.ds(0, 3), own_t, pl.ds(6, 2))))

    sources = {VT: vel_ref.at[2], EN: ene_ref, VR: vel_ref.at[1], DE: den_ref, VP: vel_ref.at[0]}

    def regroup(fields):
        def one(tp, _):
            for h in range(2):
                dest = owner(tp, h)
                for f in fields:
                    for c in range(2):
                        for t in range(2):
                            stage[dest, f, pl.ds(c * 8 + t * 4, 4), :] = sources[f][
                                2 * tp + t, pl.ds(4 * h, 4), pl.ds(128 * c, 128)
                            ]
            return 0

        lax.fori_loop(0, 8, one, 0)

    def to_rows(k, g):
        dest = peers[k]
        return pltpu.make_async_remote_copy(
            src_ref=stage.at[dest, SPANS[g]],
            dst_ref=rows.at[SPANS[g], pl.ds(pl.multiple_of(a * 16, 16), 16), :],
            send_sem=a_send.at[g, k],
            recv_sem=a_recv.at[g],
            device_id={"az": dest, "rad": rho},
            device_id_type=MESH,
        )

    def own_rows(g):
        return pltpu.make_async_copy(
            stage.at[a, SPANS[g]], rows.at[SPANS[g], pl.ds(pl.multiple_of(a * 16, 16), 16), :], a_recv.at[g]
        )

    for copy in loads[:2]:
        copy.wait()
    regroup(EARLY)
    pl.semaphore_wait(barrier, AZ - 1 + has_cross.astype(jnp.int32))
    for k in ORDER:
        to_rows(k, 0).start()
    own_rows(0).start()
    for copy in loads[2:]:
        copy.wait()
    regroup(LATE)
    for k in ORDER:
        to_rows(k, 1).start()
    own_rows(1).start()

    lane = lax.broadcasted_iota(jnp.int32, (CHUNKS, 128), 1)
    lane8 = lax.broadcasted_iota(jnp.int32, (8, 128), 1)

    t_up, t_dn = lax.rem(pair + 1, 8), lax.rem(pair + 7, 8)
    r_up, r_dn = lax.rem(quad + 1, QUADS), lax.rem(quad + QUADS - 1, QUADS)
    has_tup, has_tdn = pair < 7, pair > 0
    has_rup, has_rdn = quad < QUADS - 1, quad > 0
    id_tup = {"az": owner(t_up, half), "rad": rho}
    id_tdn = {"az": owner(t_dn, half), "rad": rho}
    id_rup = {"az": owner(pair, lax.rem(r_up, 2)), "rad": lax.div(r_up, 2)}
    id_rdn = {"az": owner(pair, lax.rem(r_dn, 2)), "rad": lax.div(r_dn, 2)}

    def four(slot, r_up, r_dn, t_up, t_dn):
        def one(pair_of_refs, ident, d):
            return pltpu.make_async_remote_copy(
                src_ref=pair_of_refs[0], dst_ref=pair_of_refs[1], send_sem=h_send.at[slot, d],
                recv_sem=h_recv.at[slot, d], device_id=ident, device_id_type=MESH,
            )

        return (
            (one(r_up, id_rup, 2), has_rup, has_rdn),
            (one(r_dn, id_rdn, 3), has_rdn, has_rup),
            (one(t_up, id_tup, 0), has_tup, has_tdn),
            (one(t_dn, id_tdn, 1), has_tdn, has_tup),
        )

    def old_energy(step, slot):
        en = states[step].at[S_AT[EN]]
        return four(
            slot,
            (en.at[own_t, pl.ds(4, 2)], en.at[own_t, low_two]),
            (en.at[own_t, pl.ds(2, 2)], en.at[own_t, pl.ds(6, 2)]),
            (en.at[own_t, own_r], en.at[low_two, own_r]),
            (en.at[own_t, own_r], en.at[pl.ds(4, 2), own_r]),
        )

    def old_speeds(step, slot):
        vt, vr = states[step].at[S_AT[VT]], states[step].at[S_AT[VR]]
        return four(
            slot,
            (vr.at[own_t, 5], vr.at[own_t, 1]),
            (vr.at[own_t, 2], vr.at[own_t, 6]),
            (vt.at[3, own_r], vt.at[1, own_r]),
            (vt.at[2, own_r], vt.at[4, own_r]),
        )

    def halo(buf, t_fields, r_fields, slot):
        return four(
            slot,
            (buf.at[r_fields, inner_t, 4], buf.at[r_fields, inner_t, 0]),
            (buf.at[r_fields, inner_t, 1], buf.at[r_fields, inner_t, 5]),
            (buf.at[t_fields, 2, inner_r], buf.at[t_fields, 0, inner_r]),
            (buf.at[t_fields, 1, inner_r], buf.at[t_fields, 3, inner_r]),
        )

    def each(copies, what):
        for copy, sends, gets in copies:
            @pl.when(gets if what == "wait_recv" else sends)
            def _():
                getattr(copy, what)()

    def eight(body, unroll=1):
        def one(i, _):
            body(i, lax.div(i, 4) + 1, lax.rem(i, 4) + 1)
            return 0

        lax.fori_loop(0, 8, one, 0, unroll=unroll)

    def unpack(fields):
        def one(i, t, r):
            for q in fields:
                value = rows[q, pl.ds(i, CHUNKS, stride=8), :]
                if q == DE:
                    f0[F_AT[DE], t, r] = value
                else:
                    s0[S_AT[q], t + 1, r + 1] = value

        eight(one)

    def to_blocks(k, g):
        dest = peers[k]
        return pltpu.make_async_remote_copy(
            src_ref=ostage.at[SPANS[g], pl.ds(pl.multiple_of(dest * 16, 16), 16), :],
            dst_ref=back.at[a, SPANS[g]],
            send_sem=b_send.at[g, k],
            recv_sem=b_recv.at[g],
            device_id={"az": dest, "rad": rho},
            device_id_type=MESH,
        )

    def own_blocks(g):
        return pltpu.make_async_copy(
            ostage.at[SPANS[g], pl.ds(pl.multiple_of(a * 16, 16), 16), :], back.at[a, SPANS[g]], b_recv.at[g]
        )

    olds_en = (old_energy(0, 0), old_energy(1, 1))
    olds_v = (old_speeds(0, 2), old_speeds(1, 3))
    lates = tuple(halo(fresh[step], pl.ds(0, 2), pl.ds(0, 2), 4 + step) for step in range(STEPS))
    new_ens = tuple(halo(fresh[step], F_AT[EN], F_AT[EN], 6 + step) for step in range(STEPS))
    rests = tuple(halo(fresh[step], F_AT[VR], F_AT[VT], 8 + step) for step in range(STEPS))
    halos = olds_en + olds_v + lates + new_ens + rests

    def along_azimuth(f, i, t, r, fields):
        p_lo = speed[i]
        for q in fields:
            v = f[F_AT[q], t, r]
            low = p_lo * jnp.where(p_lo > 0, prev_cell(v, lane), v)
            flux[q, i] = next_cell(low, lane) - low

    def face(f, u, below, above):
        s = f[(F_AT[u],) + below] + f[(F_AT[u],) + above]
        up = s > 0
        return lambda q: s * jnp.where(up, f[(F_AT[q],) + below], f[(F_AT[q],) + above])

    def begin(step):
        s, f = states[step], fresh[step]

        def source_azimuth(i, t, r):
            den = f[F_AT[DE], t, r]
            k = 0.01 / jnp.where(den > 0, den, 1.0)
            e = s[S_AT[EN], t + 1, r + 1]
            vp = s[S_AT[VP], t + 1, r + 1]
            new = vp - k * (next_cell(e, lane) - prev_cell(e, lane))
            f[F_AT[VP], t, r] = new
            factor[i] = k
            along[i] = next_cell(vp, lane) - prev_cell(vp, lane)
            speed[i] = new + prev_cell(new, lane)

        eight(source_azimuth, UNROLL)
        each(lates[step], "start")

    for step in range(STEPS):
        s, f = states[step], fresh[step]
        last = step == STEPS - 1

        if step == 0:
            pltpu.make_async_copy(rows.at[SPANS[0]], rows.at[SPANS[0]], a_recv.at[0]).wait()
            unpack(EARLY)
            each(olds_en[0], "start")
            each(olds_v[0], "start")
            pltpu.make_async_copy(rows.at[SPANS[1]], rows.at[SPANS[1]], a_recv.at[1]).wait()
            unpack(LATE)
            begin(0)

        def azimuth_late(i, t, r):
            along_azimuth(f, i, t, r, LATE)

        eight(azimuth_late)

        def source_speeds(i, t, r):
            k = factor[i]
            f[F_AT[VR], t, r] = s[S_AT[VR], t + 1, r + 1] - k * (s[S_AT[EN], t + 1, r + 2] - s[S_AT[EN], t + 1, r])
            f[F_AT[VT], t, r] = s[S_AT[VT], t + 1, r + 1] - k * (s[S_AT[EN], t + 2, r + 1] - s[S_AT[EN], t, r + 1])

        def source_energy(i, t, r):
            e = s[S_AT[EN], t + 1, r + 1]
            div = (
                along[i]
                + (s[S_AT[VR], t + 1, r + 2] - s[S_AT[VR], t + 1, r])
                + (s[S_AT[VT], t + 2, r + 1] - s[S_AT[VT], t, r + 1])
            )
            f[F_AT[EN], t, r] = e - 0.01 * e * div

        def beyond(u, place, near, far, own):
            den = f[(F_AT[DE],) + place]
            k = 0.01 / jnp.where(den > 0, den, 1.0)
            low, high = (far, own) if near < own else (own, far)
            en = S_AT[EN]
            t, r = place
            if u == VT:
                new = s[S_AT[VT], near, r + 1] - k * (s[en, high, r + 1] - s[en, low, r + 1])
            else:
                new = s[S_AT[VR], t + 1, near] - k * (s[en, t + 1, high] - s[en, t + 1, low])
            f[(F_AT[u],) + place] = new

        def all_beyond():
            @pl.when(has_tdn)
            def _():
                for r in range(1, 5):
                    beyond(VT, (0, r), 1, 0, 2)

            @pl.when(has_tup)
            def _():
                for r in range(1, 5):
                    beyond(VT, (3, r), 4, 5, 3)

            @pl.when(has_rdn)
            def _():
                for t in range(1, 3):
                    beyond(VR, (t, 0), 1, 0, 2)

            @pl.when(has_rup)
            def _():
                for t in range(1, 3):
                    beyond(VR, (t, 5), 6, 7, 5)

        if last:
            each(olds_v[1], "wait_recv")
            eight(source_energy, UNROLL)
            each(new_ens[1], "start")
            each(olds_en[1], "wait_recv")
            eight(source_speeds, UNROLL)
            each(rests[1], "start")
        else:
            each(olds_en[0], "wait_recv")
            eight(source_speeds, UNROLL)
            each(rests[0], "start")
            each(olds_v[0], "wait_recv")
            eight(source_energy, UNROLL)
            each(new_ens[0], "start")

        def azimuth_early(i, t, r):
            along_azimuth(f, i, t, r, EARLY)

        def inner_faces(fields):
            def inner_radius(n, _):
                t, r = lax.div(n, 3), lax.rem(n, 3)
                one = face(f, VR, (t + 1, r + 1), (t + 1, r + 2))
                for q in fields:
                    v = one(q)
                    flux[q, 4 * t + r] += v
                    flux[q, 4 * t + r + 1] -= v
                return 0

            lax.fori_loop(0, 6, inner_radius, 0)

            def inner_theta(r, _):
                one = face(f, VT, (1, r + 1), (2, r + 1))
                for q in fields:
                    v = one(q)
                    flux[q, r] += v
                    flux[q, 4 + r] -= v
                return 0

            lax.fori_loop(0, 4, inner_theta, 0)

        inner_faces(LATE)
        if not last:
            eight(azimuth_early)
            inner_faces(EARLY)
        each(lates[step], "wait_recv")
        all_beyond()

        for g, fields in ((1, LATE), (0, EARLY)) if last else ((0, (VT, VR)), (0, (EN,)), (1, LATE)):
            if last and EN in fields:
                eight(azimuth_early)
                inner_faces(EARLY)
                each(rests[1], "wait_recv")
                each(new_ens[1], "wait_recv")
            elif not last and DE not in fields:
                each(new_ens[0] if EN in fields else rests[0], "wait_recv")

            def outer_radius(t, _):
                low = face(f, VR, (t + 1, 0), (t + 1, 1))
                high = face(f, VR, (t + 1, 4), (t + 1, 5))
                for q in fields:
                    flux[q, 4 * t] -= low(q)
                    flux[q, 4 * t + 3] += high(q)
                return 0

            lax.fori_loop(0, 2, outer_radius, 0)

            def outer_theta(r, _):
                low = face(f, VT, (0, r + 1), (1, r + 1))
                high = face(f, VT, (2, r + 1), (3, r + 1))
                for q in fields:
                    flux[q, r] -= low(q)
                    flux[q, 4 + r] += high(q)
                return 0

            lax.fori_loop(0, 4, outer_theta, 0)

            def finish(i, t, r):
                for q in fields:
                    moved = f[F_AT[q], t, r] - 0.025 * flux[q, i]
                    blended[q, i, pl.ds(0, CHUNKS), :] = moved
                    blended[q, i, pl.ds(CHUNKS, CHUNKS), :] = moved

            eight(finish, UNROLL)

            def rotate(i, t, r):
                w = frac_ref[half * 4 + r - 1]
                shift = shift_ref[half * 4 + r - 1]
                views = []
                for back_cells in (0, 1):
                    ahead = lax.rem(2 * CELLS - shift - back_cells, CELLS)
                    views.append((lax.div(ahead, 128), lax.rem(ahead, 128)))
                for q in fields:
                    for m in range(4):
                        parts = []
                        for whole, part in views:
                            near = blended[q, i, pl.ds(whole + 8 * m, 8), :]
                            far = blended[q, i, pl.ds(whole + 8 * m + 1, 8), :]
                            parts.append(pltpu.roll(jnp.where(lane8 < part, far, near), lax.rem(128 - part, 128), 1))
                        out = (1.0 - w) * parts[0] + w * parts[1]
                        if last:
                            ostage[q, pl.ds(64 * m + i, 8, stride=8), :] = out
                        elif q == DE:
                            f1[F_AT[DE], t, r, pl.ds(8 * m, 8), :] = out
                        else:
                            s1[S_AT[q], t + 1, r + 1, pl.ds(8 * m, 8), :] = out

            eight(rotate, UNROLL)
            if last:
                for k in ORDER:
                    to_blocks(k, g).start()
                own_blocks(g).start()
            elif EN in fields:
                each(olds_en[1], "start")
            elif VT in fields:
                each(olds_v[1], "start")
            else:
                begin(step + 1)

    for copies in halos:
        each(copies, "wait_send")
    for g in range(2):
        for k in range(1, AZ):
            to_rows(k, g).wait_send()
            to_blocks(k, g).wait_send()
    for g in range(2):
        pltpu.make_async_copy(back.at[:, SPANS[g]], back.at[:, SPANS[g]], b_recv.at[g]).wait()


def write_out(back, den_hbm, vel_hbm, ene_hbm, den_out, vel_out, ene_out, out_sem):
    targets = {
        VT: (vel_out.at[2], vel_hbm.at[2]), EN: (ene_out, ene_hbm), VR: (vel_out.at[1], vel_hbm.at[1]),
        DE: (den_out, den_hbm), VP: (vel_out.at[0], vel_hbm.at[0]),
    }
    writes = []
    for q in range(5):
        dst = targets[q][0]

        def one(tp, _):
            for h in range(2):
                src = owner(tp, h)
                for c in range(2):
                    for t in range(2):
                        dst[2 * tp + t, pl.ds(4 * h, 4), pl.ds(128 * c, 128)] = back[
                            src, q, pl.ds(c * 8 + t * 4, 4), :
                        ]
            return 0

        lax.fori_loop(0, 8, one, 0, unroll=8)
        writes.append(pltpu.make_async_copy(*targets[q], out_sem.at[q]))
        writes[-1].start()
    for copy in writes:
        copy.wait()


def shards(density, velocity, energy, shifts, fraction):
    hbm = pl.BlockSpec(memory_space=pl.ANY)
    f32 = jnp.float32
    limit = 40 * 1024 * 1024
    block = (AZ, 5, 16, 128)
    dma = pltpu.SemaphoreType.DMA
    fields = [pltpu.VMEM(v.shape, f32) for v in (density, velocity, energy)]
    back = pl.pallas_call(
        kernel,
        out_shape=pltpu.VMEM(block, f32),
        in_specs=[hbm] * 5,
        out_specs=hbm,
        scratch_shapes=fields + [
            pltpu.SMEM(shifts.shape, jnp.int32),
            pltpu.SMEM(fraction.shape, f32),
            pltpu.VMEM(block, f32),
            pltpu.VMEM((5, 256, 128), f32),
            pltpu.VMEM((4, 6, 8, CHUNKS, 128), f32),
            pltpu.VMEM((4, 6, 8, CHUNKS, 128), f32),
            pltpu.VMEM((5, 4, 6, CHUNKS, 128), f32),
            pltpu.VMEM((5, 4, 6, CHUNKS, 128), f32),
            pltpu.VMEM((8, CHUNKS, 128), f32),
            pltpu.VMEM((8, CHUNKS, 128), f32),
            pltpu.VMEM((8, CHUNKS, 128), f32),
            pltpu.VMEM((5, 8, CHUNKS, 128), f32),
            pltpu.VMEM((5, 8, 2 * CHUNKS, 128), f32),
            pltpu.VMEM((5, 256, 128), f32),
            dma((2, AZ)),
            dma((2,)),
            dma((10, 4)),
            dma((10, 4)),
            dma((2, AZ)),
            dma((2,)),
            dma((4,)),
            dma((5,)),
        ],
        compiler_params=pltpu.CompilerParams(collective_id=0, has_side_effects=True, vmem_limit_bytes=limit),
    )(*(pltpu.with_memory_space_constraint(v, pltpu.HBM) for v in (density, velocity, energy, shifts, fraction)))
    return pl.pallas_call(
        write_out,
        out_shape=tuple(jax.ShapeDtypeStruct(v.shape, f32) for v in (density, velocity, energy)),
        in_specs=[pl.BlockSpec(memory_space=pltpu.VMEM)],
        out_specs=(hbm,) * 3,
        scratch_shapes=fields + [dma((5,))],
        compiler_params=pltpu.CompilerParams(vmem_limit_bytes=16 * 1024 * 1024),
    )(pltpu.with_memory_space_constraint(back, pltpu.VMEM))


def solution(mesh):
    placed = (
        P(None, "rad", "az"),
        P(None, None, "rad", "az"),
        P(None, "rad", "az"),
        P("rad"),
        P("rad"),
    )
    return jax.shard_map(
        shards,
        mesh=mesh,
        in_specs=placed,
        out_specs=(P(None, "rad", "az"), P(None, None, "rad", "az"), P(None, "rad", "az")),
        check_vma=False,
    )
```

```python
import jax
import jax.numpy as jnp
from jax import lax
from jax.experimental import pallas as pl
from jax.experimental.pallas import tpu as pltpu
from jax.sharding import PartitionSpec as P

MESH = pl.DeviceIdType.MESH
AZ = 16
QUADS = 32
CHUNKS = 32
CELLS = 4096
STEPS = 2

EN, VT, VR, DE, VP = range(5)
EARLY, LATE = (EN, VT, VR), (DE, VP)
GROUPS = (EARLY, LATE)
SPANS = (pl.ds(0, 3), pl.ds(3, 2))
S_AT = {VR: 0, EN: 1, VT: 2, VP: 3}
F_AT = {DE: 0, VP: 1, VR: 2, EN: 3, VT: 4}
UNROLL = 8
ORDER = (10, 8, 6, 4, 14, 12, 2, 11, 9, 7, 5, 15, 13, 3, 1)


def owner(pair, half):
    return lax.div(pair, 2) * 4 + (1 - half) * 2 + lax.rem(pair, 2)


def prev_cell(x, lane):
    x1 = pltpu.roll(x, 1, 1)
    return jnp.where(lane == 0, pltpu.roll(x1, 1, 0), x1)


def next_cell(x, lane):
    x1 = pltpu.roll(x, 127, 1)
    return jnp.where(lane == 127, pltpu.roll(x1, CHUNKS - 1, 0), x1)


def kernel(
    den_hbm, vel_hbm, ene_hbm, shift_hbm, frac_hbm,
    back,
    den_ref, vel_ref, ene_ref, shift_ref, frac_ref,
    stage, rows, s0, s1, f0, f1, speed, factor, along, flux, blended, ostage,
    a_send, a_recv, h_send, h_recv, b_send, b_recv, l_sem, i_sem,
):
    a = lax.axis_index("az")
    rho = lax.axis_index("rad")
    x, y, core = lax.div(a, 4), lax.rem(lax.div(a, 2), 2), lax.rem(a, 2)
    half = 1 - y
    pair = 2 * x + core
    quad = 2 * rho + half
    states, fresh = (s0, s1), (f0, f1)

    loads = [
        pltpu.make_async_copy(src, dst, i_sem.at[n])
        for n, (src, dst) in enumerate((
            (ene_hbm, ene_ref), (vel_hbm, vel_ref), (den_hbm, den_ref), (shift_hbm, shift_ref), (frac_hbm, frac_ref)
        ))
    ]
    for copy in loads[:3]:
        copy.start()

    peers = []
    for k in range(AZ):
        dx, dy, dc = k // 4, (k // 2) % 2, k % 2
        peers.append(lax.rem(x + dx, 4) * 4 + lax.rem(y + dy, 2) * 2 + lax.rem(core + dc, 2))

    barrier = pltpu.get_barrier_semaphore()
    for k in range(1, AZ):
        pl.semaphore_signal(barrier, inc=1, device_id={"az": peers[k], "rad": rho}, device_id_type=MESH)
    cross = lax.rem(quad + 2 * half - 1 + QUADS, QUADS)
    has_cross = jnp.logical_and(quad > 0, quad < QUADS - 1)

    @pl.when(has_cross)
    def _():
        pl.semaphore_signal(
            barrier, inc=1, device_id={"az": owner(pair, lax.rem(cross, 2)), "rad": lax.div(cross, 2)},
            device_id_type=MESH,
        )

    for copy in loads[3:]:
        copy.start()

    inner_t, inner_r = pl.ds(1, 2), pl.ds(1, 4)
    own_t, own_r = pl.ds(2, 2), pl.ds(2, 4)
    low_two = pl.ds(0, 2)

    def clear(buf, where):
        buf[where] = jnp.zeros_like(buf[where])

    for buf in (f0, f1):
        pl.when(pair == 0)(lambda: clear(buf, (pl.ds(0, 5), 0, inner_r)))
        pl.when(pair == 7)(lambda: clear(buf, (pl.ds(0, 5), 3, inner_r)))
        pl.when(quad == 0)(lambda: clear(buf, (pl.ds(0, 5), inner_t, 0)))
        pl.when(quad == QUADS - 1)(lambda: clear(buf, (pl.ds(0, 5), inner_t, 5)))
    for buf in (s0, s1):
        pl.when(pair == 0)(lambda: clear(buf, (pl.ds(0, 3), low_two, own_r)))
        pl.when(pair == 7)(lambda: clear(buf, (pl.ds(0, 3), pl.ds(4, 2), own_r)))
        pl.when(quad == 0)(lambda: clear(buf, (pl.ds(0, 3), own_t, low_two)))
        pl.when(quad == QUADS - 1)(lambda: clear(buf, (pl.ds(0, 3), own_t, pl.ds(6, 2))))

    sources = {VT: vel_ref.at[2], EN: ene_ref, VR: vel_ref.at[1], DE: den_ref, VP: vel_ref.at[0]}

    def regroup(fields):
        def one(tp, _):
            for h in range(2):
                dest = owner(tp, h)
                for f in fields:
                    for c in range(2):
                        for t in range(2):
                            stage[dest, f, pl.ds(c * 8 + t * 4, 4), :] = sources[f][
                                2 * tp + t, pl.ds(4 * h, 4), pl.ds(128 * c, 128)
                            ]
            return 0

        lax.fori_loop(0, 8, one, 0, unroll=4)

    def to_rows(k, g):
        dest = peers[k]
        return pltpu.make_async_remote_copy(
            src_ref=stage.at[dest, SPANS[g]],
            dst_ref=rows.at[SPANS[g], pl.ds(pl.multiple_of(a * 16, 16), 16), :],
            send_sem=a_send.at[g, k],
            recv_sem=a_recv.at[g],
            device_id={"az": dest, "rad": rho},
            device_id_type=MESH,
        )

    def own_rows(g):
        return pltpu.make_async_copy(
            stage.at[a, SPANS[g]], rows.at[SPANS[g], pl.ds(pl.multiple_of(a * 16, 16), 16), :], a_recv.at[g]
        )

    for copy in loads[:2]:
        copy.wait()
    regroup(EARLY)
    pl.semaphore_wait(barrier, AZ - 1 + has_cross.astype(jnp.int32))
    for k in ORDER:
        to_rows(k, 0).start()
    own_rows(0).start()
    for copy in loads[2:]:
        copy.wait()
    regroup(LATE)
    for k in ORDER:
        to_rows(k, 1).start()
    own_rows(1).start()

    lane = lax.broadcasted_iota(jnp.int32, (CHUNKS, 128), 1)
    lane8 = lax.broadcasted_iota(jnp.int32, (8, 128), 1)

    t_up, t_dn = lax.rem(pair + 1, 8), lax.rem(pair + 7, 8)
    r_up, r_dn = lax.rem(quad + 1, QUADS), lax.rem(quad + QUADS - 1, QUADS)
    has_tup, has_tdn = pair < 7, pair > 0
    has_rup, has_rdn = quad < QUADS - 1, quad > 0
    id_tup = {"az": owner(t_up, half), "rad": rho}
    id_tdn = {"az": owner(t_dn, half), "rad": rho}
    id_rup = {"az": owner(pair, lax.rem(r_up, 2)), "rad": lax.div(r_up, 2)}
    id_rdn = {"az": owner(pair, lax.rem(r_dn, 2)), "rad": lax.div(r_dn, 2)}

    def four(slot, r_up, r_dn, t_up, t_dn):
        def one(pair_of_refs, ident, d):
            return pltpu.make_async_remote_copy(
                src_ref=pair_of_refs[0], dst_ref=pair_of_refs[1], send_sem=h_send.at[slot, d],
                recv_sem=h_recv.at[slot, d], device_id=ident, device_id_type=MESH,
            )

        return (
            (one(r_up, id_rup, 2), has_rup, has_rdn),
            (one(r_dn, id_rdn, 3), has_rdn, has_rup),
            (one(t_up, id_tup, 0), has_tup, has_tdn),
            (one(t_dn, id_tdn, 1), has_tdn, has_tup),
        )

    def old_energy(step, slot):
        en = states[step].at[S_AT[EN]]
        return four(
            slot,
            (en.at[own_t, pl.ds(4, 2)], en.at[own_t, low_two]),
            (en.at[own_t, pl.ds(2, 2)], en.at[own_t, pl.ds(6, 2)]),
            (en.at[own_t, own_r], en.at[low_two, own_r]),
            (en.at[own_t, own_r], en.at[pl.ds(4, 2), own_r]),
        )

    def old_speeds(step, slot):
        vt, vr = states[step].at[S_AT[VT]], states[step].at[S_AT[VR]]
        return four(
            slot,
            (vr.at[own_t, 5], vr.at[own_t, 1]),
            (vr.at[own_t, 2], vr.at[own_t, 6]),
            (vt.at[3, own_r], vt.at[1, own_r]),
            (vt.at[2, own_r], vt.at[4, own_r]),
        )

    def halo(buf, t_fields, r_fields, slot):
        return four(
            slot,
            (buf.at[r_fields, inner_t, 4], buf.at[r_fields, inner_t, 0]),
            (buf.at[r_fields, inner_t, 1], buf.at[r_fields, inner_t, 5]),
            (buf.at[t_fields, 2, inner_r], buf.at[t_fields, 0, inner_r]),
            (buf.at[t_fields, 1, inner_r], buf.at[t_fields, 3, inner_r]),
        )

    def each(copies, what):
        for copy, sends, gets in copies:
            @pl.when(gets if what == "wait_recv" else sends)
            def _():
                getattr(copy, what)()

    def eight(body, unroll=1):
        def one(i, _):
            body(i, lax.div(i, 4) + 1, lax.rem(i, 4) + 1)
            return 0

        lax.fori_loop(0, 8, one, 0, unroll=unroll)

    def unpack(fields):
        def one(i, t, r):
            for q in fields:
                value = rows[q, pl.ds(i, CHUNKS, stride=8), :]
                if q == DE:
                    f0[F_AT[DE], t, r] = value
                else:
                    s0[S_AT[q], t + 1, r + 1] = value

        eight(one, UNROLL)

    def to_blocks(k, g):
        dest = peers[k]
        return pltpu.make_async_remote_copy(
            src_ref=ostage.at[SPANS[g], pl.ds(pl.multiple_of(dest * 16, 16), 16), :],
            dst_ref=back.at[a, SPANS[g]],
            send_sem=b_send.at[g, k],
            recv_sem=b_recv.at[g],
            device_id={"az": dest, "rad": rho},
            device_id_type=MESH,
        )

    def own_blocks(g):
        return pltpu.make_async_copy(
            ostage.at[SPANS[g], pl.ds(pl.multiple_of(a * 16, 16), 16), :], back.at[a, SPANS[g]], b_recv.at[g]
        )

    olds_en = (old_energy(0, 0), old_energy(1, 1))
    olds_v = (old_speeds(0, 2), old_speeds(1, 3))
    lates = tuple(halo(fresh[step], pl.ds(0, 2), pl.ds(0, 2), 4 + step) for step in range(STEPS))
    new_ens = tuple(halo(fresh[step], F_AT[EN], F_AT[EN], 6 + step) for step in range(STEPS))
    rests = tuple(halo(fresh[step], F_AT[VR], F_AT[VT], 8 + step) for step in range(STEPS))
    halos = olds_en + olds_v + lates + new_ens + rests

    def along_azimuth(f, i, t, r, fields):
        p_lo = speed[i]
        for q in fields:
            v = f[F_AT[q], t, r]
            low = p_lo * jnp.where(p_lo > 0, prev_cell(v, lane), v)
            flux[q, i] = next_cell(low, lane) - low

    def face(f, u, below, above):
        s = f[(F_AT[u],) + below] + f[(F_AT[u],) + above]
        up = s > 0
        return lambda q: s * jnp.where(up, f[(F_AT[q],) + below], f[(F_AT[q],) + above])

    def begin(step):
        s, f = states[step], fresh[step]

        def source_azimuth(i, t, r):
            den = f[F_AT[DE], t, r]
            k = 0.01 / jnp.where(den > 0, den, 1.0)
            e = s[S_AT[EN], t + 1, r + 1]
            vp = s[S_AT[VP], t + 1, r + 1]
            new = vp - k * (next_cell(e, lane) - prev_cell(e, lane))
            f[F_AT[VP], t, r] = new
            factor[i] = k
            along[i] = next_cell(vp, lane) - prev_cell(vp, lane)
            speed[i] = new + prev_cell(new, lane)

        eight(source_azimuth, UNROLL)
        each(lates[step], "start")

    for step in range(STEPS):
        s, f = states[step], fresh[step]
        last = step == STEPS - 1

        if step == 0:
            pltpu.make_async_copy(rows.at[SPANS[0]], rows.at[SPANS[0]], a_recv.at[0]).wait()
            unpack(EARLY)
            each(olds_en[0], "start")
            each(olds_v[0], "start")
            pltpu.make_async_copy(rows.at[SPANS[1]], rows.at[SPANS[1]], a_recv.at[1]).wait()
            unpack(LATE)
            begin(0)

        def azimuth_late(i, t, r):
            along_azimuth(f, i, t, r, LATE)

        eight(azimuth_late)

        def source_speeds(i, t, r):
            k = factor[i]
            f[F_AT[VR], t, r] = s[S_AT[VR], t + 1, r + 1] - k * (s[S_AT[EN], t + 1, r + 2] - s[S_AT[EN], t + 1, r])
            f[F_AT[VT], t, r] = s[S_AT[VT], t + 1, r + 1] - k * (s[S_AT[EN], t + 2, r + 1] - s[S_AT[EN], t, r + 1])

        def source_energy(i, t, r):
            e = s[S_AT[EN], t + 1, r + 1]
            div = (
                along[i]
                + (s[S_AT[VR], t + 1, r + 2] - s[S_AT[VR], t + 1, r])
                + (s[S_AT[VT], t + 2, r + 1] - s[S_AT[VT], t, r + 1])
            )
            f[F_AT[EN], t, r] = e - 0.01 * e * div

        def beyond(u, place, near, far, own):
            den = f[(F_AT[DE],) + place]
            k = 0.01 / jnp.where(den > 0, den, 1.0)
            low, high = (far, own) if near < own else (own, far)
            en = S_AT[EN]
            t, r = place
            if u == VT:
                new = s[S_AT[VT], near, r + 1] - k * (s[en, high, r + 1] - s[en, low, r + 1])
            else:
                new = s[S_AT[VR], t + 1, near] - k * (s[en, t + 1, high] - s[en, t + 1, low])
            f[(F_AT[u],) + place] = new

        def all_beyond():
            @pl.when(has_tdn)
            def _():
                for r in range(1, 5):
                    beyond(VT, (0, r), 1, 0, 2)

            @pl.when(has_tup)
            def _():
                for r in range(1, 5):
                    beyond(VT, (3, r), 4, 5, 3)

            @pl.when(has_rdn)
            def _():
                for t in range(1, 3):
                    beyond(VR, (t, 0), 1, 0, 2)

            @pl.when(has_rup)
            def _():
                for t in range(1, 3):
                    beyond(VR, (t, 5), 6, 7, 5)

        if last:
            each(olds_v[1], "wait_recv")
            eight(source_energy, UNROLL)
            each(new_ens[1], "start")
            each(olds_en[1], "wait_recv")
            eight(source_speeds, UNROLL)
            each(rests[1], "start")
        else:
            each(olds_en[0], "wait_recv")
            eight(source_speeds, UNROLL)
            each(rests[0], "start")
            each(olds_v[0], "wait_recv")
            eight(source_energy, UNROLL)
            each(new_ens[0], "start")

        def azimuth_early(i, t, r):
            along_azimuth(f, i, t, r, EARLY)

        def inner_faces(fields):
            def inner_radius(n, _):
                t, r = lax.div(n, 3), lax.rem(n, 3)
                one = face(f, VR, (t + 1, r + 1), (t + 1, r + 2))
                for q in fields:
                    v = one(q)
                    flux[q, 4 * t + r] += v
                    flux[q, 4 * t + r + 1] -= v
                return 0

            lax.fori_loop(0, 6, inner_radius, 0)

            def inner_theta(r, _):
                one = face(f, VT, (1, r + 1), (2, r + 1))
                for q in fields:
                    v = one(q)
                    flux[q, r] += v
                    flux[q, 4 + r] -= v
                return 0

            lax.fori_loop(0, 4, inner_theta, 0)

        inner_faces(LATE)
        if not last:
            eight(azimuth_early)
            inner_faces(EARLY)
        each(lates[step], "wait_recv")
        all_beyond()

        for g, fields in ((1, LATE), (0, EARLY)) if last else ((0, (VT, VR)), (0, (EN,)), (1, LATE)):
            if last and EN in fields:
                eight(azimuth_early)
                inner_faces(EARLY)
                each(rests[1], "wait_recv")
                each(new_ens[1], "wait_recv")
            elif not last and DE not in fields:
                each(new_ens[0] if EN in fields else rests[0], "wait_recv")

            def outer_radius(t, _):
                low = face(f, VR, (t + 1, 0), (t + 1, 1))
                high = face(f, VR, (t + 1, 4), (t + 1, 5))
                for q in fields:
                    flux[q, 4 * t] -= low(q)
                    flux[q, 4 * t + 3] += high(q)
                return 0

            lax.fori_loop(0, 2, outer_radius, 0)

            def outer_theta(r, _):
                low = face(f, VT, (0, r + 1), (1, r + 1))
                high = face(f, VT, (2, r + 1), (3, r + 1))
                for q in fields:
                    flux[q, r] -= low(q)
                    flux[q, 4 + r] += high(q)
                return 0

            lax.fori_loop(0, 4, outer_theta, 0)

            def finish(i, t, r):
                for q in fields:
                    moved = f[F_AT[q], t, r] - 0.025 * flux[q, i]
                    blended[q, i, pl.ds(0, CHUNKS), :] = moved
                    blended[q, i, pl.ds(CHUNKS, CHUNKS), :] = moved

            eight(finish, UNROLL)

            def rotate(i, t, r):
                w = frac_ref[half * 4 + r - 1]
                shift = shift_ref[half * 4 + r - 1]
                views = []
                for back_cells in (0, 1):
                    ahead = lax.rem(2 * CELLS - shift - back_cells, CELLS)
                    views.append((lax.div(ahead, 128), lax.rem(ahead, 128)))
                for q in fields:
                    for m in range(4):
                        parts = []
                        for whole, part in views:
                            near = blended[q, i, pl.ds(whole + 8 * m, 8), :]
                            far = blended[q, i, pl.ds(whole + 8 * m + 1, 8), :]
                            parts.append(pltpu.roll(jnp.where(lane8 < part, far, near), lax.rem(128 - part, 128), 1))
                        out = (1.0 - w) * parts[0] + w * parts[1]
                        if last:
                            ostage[q, pl.ds(64 * m + i, 8, stride=8), :] = out
                        elif q == DE:
                            f1[F_AT[DE], t, r, pl.ds(8 * m, 8), :] = out
                        else:
                            s1[S_AT[q], t + 1, r + 1, pl.ds(8 * m, 8), :] = out

            eight(rotate, UNROLL)
            if last:
                for k in ORDER:
                    to_blocks(k, g).start()
                own_blocks(g).start()
            elif EN in fields:
                each(olds_en[1], "start")
            elif VT in fields:
                each(olds_v[1], "start")
            else:
                begin(step + 1)

    for copies in halos:
        each(copies, "wait_send")
    for g in range(2):
        for k in range(1, AZ):
            to_rows(k, g).wait_send()
            to_blocks(k, g).wait_send()
    for g in range(2):
        pltpu.make_async_copy(back.at[:, SPANS[g]], back.at[:, SPANS[g]], b_recv.at[g]).wait()


def write_out(back, den_hbm, vel_hbm, ene_hbm, den_out, vel_out, ene_out, out_sem):
    targets = {
        VT: (vel_out.at[2], vel_hbm.at[2]), EN: (ene_out, ene_hbm), VR: (vel_out.at[1], vel_hbm.at[1]),
        DE: (den_out, den_hbm), VP: (vel_out.at[0], vel_hbm.at[0]),
    }
    writes = []
    for q in range(5):
        dst = targets[q][0]

        def one(tp, _):
            for h in range(2):
                src = owner(tp, h)
                for c in range(2):
                    for t in range(2):
                        dst[2 * tp + t, pl.ds(4 * h, 4), pl.ds(128 * c, 128)] = back[
                            src, q, pl.ds(c * 8 + t * 4, 4), :
                        ]
            return 0

        lax.fori_loop(0, 8, one, 0, unroll=8)
        writes.append(pltpu.make_async_copy(*targets[q], out_sem.at[q]))
        writes[-1].start()
    for copy in writes:
        copy.wait()


def shards(density, velocity, energy, shifts, fraction):
    hbm = pl.BlockSpec(memory_space=pl.ANY)
    f32 = jnp.float32
    limit = 40 * 1024 * 1024
    block = (AZ, 5, 16, 128)
    dma = pltpu.SemaphoreType.DMA
    fields = [pltpu.VMEM(v.shape, f32) for v in (density, velocity, energy)]
    back = pl.pallas_call(
        kernel,
        out_shape=pltpu.VMEM(block, f32),
        in_specs=[hbm] * 5,
        out_specs=hbm,
        scratch_shapes=fields + [
            pltpu.SMEM(shifts.shape, jnp.int32),
            pltpu.SMEM(fraction.shape, f32),
            pltpu.VMEM(block, f32),
            pltpu.VMEM((5, 256, 128), f32),
            pltpu.VMEM((4, 6, 8, CHUNKS, 128), f32),
            pltpu.VMEM((4, 6, 8, CHUNKS, 128), f32),
            pltpu.VMEM((5, 4, 6, CHUNKS, 128), f32),
            pltpu.VMEM((5, 4, 6, CHUNKS, 128), f32),
            pltpu.VMEM((8, CHUNKS, 128), f32),
            pltpu.VMEM((8, CHUNKS, 128), f32),
            pltpu.VMEM((8, CHUNKS, 128), f32),
            pltpu.VMEM((5, 8, CHUNKS, 128), f32),
            pltpu.VMEM((5, 8, 2 * CHUNKS, 128), f32),
            pltpu.VMEM((5, 256, 128), f32),
            dma((2, AZ)),
            dma((2,)),
            dma((10, 4)),
            dma((10, 4)),
            dma((2, AZ)),
            dma((2,)),
            dma((4,)),
            dma((5,)),
        ],
        compiler_params=pltpu.CompilerParams(collective_id=0, has_side_effects=True, vmem_limit_bytes=limit),
    )(*(pltpu.with_memory_space_constraint(v, pltpu.HBM) for v in (density, velocity, energy, shifts, fraction)))
    return pl.pallas_call(
        write_out,
        out_shape=tuple(jax.ShapeDtypeStruct(v.shape, f32) for v in (density, velocity, energy)),
        in_specs=[pl.BlockSpec(memory_space=pltpu.VMEM)],
        out_specs=(hbm,) * 3,
        scratch_shapes=fields + [dma((5,))],
        compiler_params=pltpu.CompilerParams(vmem_limit_bytes=16 * 1024 * 1024),
    )(pltpu.with_memory_space_constraint(back, pltpu.VMEM))


def solution(mesh):
    placed = (
        P(None, "rad", "az"),
        P(None, None, "rad", "az"),
        P(None, "rad", "az"),
        P("rad"),
        P("rad"),
    )
    return jax.shard_map(
        shards,
        mesh=mesh,
        in_specs=placed,
        out_specs=(P(None, "rad", "az"), P(None, None, "rad", "az"), P(None, "rad", "az")),
        check_vma=False,
    )
```

```python
import jax
import jax.numpy as jnp
from jax import lax
from jax.experimental import pallas as pl
from jax.experimental.pallas import tpu as pltpu
from jax.sharding import PartitionSpec as P

MESH = pl.DeviceIdType.MESH
AZ = 16
QUADS = 32
CHUNKS = 32
CELLS = 4096
PADDED = 264
STEPS = 2

EN, VT, VR, DE, VP = range(5)
EARLY, LATE = (EN, VT, VR), (DE, VP)
GROUPS = (EARLY, LATE)
SPANS = (pl.ds(0, 3), pl.ds(3, 2))
S_AT = {VR: 0, EN: 1, VT: 2, VP: 3}
F_AT = {DE: 0, VP: 1, VR: 2, EN: 3, VT: 4}
UNROLL = 8
ORDER = (10, 8, 6, 4, 14, 12, 2, 11, 9, 7, 5, 15, 13, 3, 1)


def owner(pair, half):
    return lax.div(pair, 2) * 4 + (1 - half) * 2 + lax.rem(pair, 2)


def prev_cell(x, lane):
    x1 = pltpu.roll(x, 1, 1)
    return jnp.where(lane == 0, pltpu.roll(x1, 1, 0), x1)


def next_cell(x, lane):
    x1 = pltpu.roll(x, 127, 1)
    return jnp.where(lane == 127, pltpu.roll(x1, CHUNKS - 1, 0), x1)


def kernel(
    den_hbm, vel_hbm, ene_hbm, shift_hbm, frac_hbm,
    back,
    den_ref, vel_ref, ene_ref, shift_ref, frac_ref,
    stage, rows, s0, s1, f0, f1, speed, factor, along, flux, blended, ostage,
    a_send, a_recv, h_send, h_recv, b_send, b_recv, l_sem, i_sem,
):
    a = lax.axis_index("az")
    rho = lax.axis_index("rad")
    x, y, core = lax.div(a, 4), lax.rem(lax.div(a, 2), 2), lax.rem(a, 2)
    half = 1 - y
    pair = 2 * x + core
    quad = 2 * rho + half
    states, fresh = (s0, s1), (f0, f1)

    loads = [
        pltpu.make_async_copy(src, dst, i_sem.at[n])
        for n, (src, dst) in enumerate((
            (ene_hbm, ene_ref), (vel_hbm, vel_ref), (den_hbm, den_ref), (shift_hbm, shift_ref), (frac_hbm, frac_ref)
        ))
    ]
    for copy in loads[:3]:
        copy.start()

    peers = []
    for k in range(AZ):
        dx, dy, dc = k // 4, (k // 2) % 2, k % 2
        peers.append(lax.rem(x + dx, 4) * 4 + lax.rem(y + dy, 2) * 2 + lax.rem(core + dc, 2))

    barrier = pltpu.get_barrier_semaphore()
    for k in range(1, AZ):
        pl.semaphore_signal(barrier, inc=1, device_id={"az": peers[k], "rad": rho}, device_id_type=MESH)
    cross = lax.rem(quad + 2 * half - 1 + QUADS, QUADS)
    has_cross = jnp.logical_and(quad > 0, quad < QUADS - 1)

    @pl.when(has_cross)
    def _():
        pl.semaphore_signal(
            barrier, inc=1, device_id={"az": owner(pair, lax.rem(cross, 2)), "rad": lax.div(cross, 2)},
            device_id_type=MESH,
        )

    for copy in loads[3:]:
        copy.start()

    inner_t, inner_r = pl.ds(1, 2), pl.ds(1, 4)
    own_t, own_r = pl.ds(2, 2), pl.ds(2, 4)
    low_two = pl.ds(0, 2)

    def clear(buf, where):
        buf[where] = jnp.zeros_like(buf[where])

    for buf in (f0, f1):
        pl.when(pair == 0)(lambda: clear(buf, (pl.ds(0, 5), 0, inner_r)))
        pl.when(pair == 7)(lambda: clear(buf, (pl.ds(0, 5), 3, inner_r)))
        pl.when(quad == 0)(lambda: clear(buf, (pl.ds(0, 5), inner_t, 0)))
        pl.when(quad == QUADS - 1)(lambda: clear(buf, (pl.ds(0, 5), inner_t, 5)))
    for buf in (s0, s1):
        pl.when(pair == 0)(lambda: clear(buf, (pl.ds(0, 3), low_two, own_r)))
        pl.when(pair == 7)(lambda: clear(buf, (pl.ds(0, 3), pl.ds(4, 2), own_r)))
        pl.when(quad == 0)(lambda: clear(buf, (pl.ds(0, 3), own_t, low_two)))
        pl.when(quad == QUADS - 1)(lambda: clear(buf, (pl.ds(0, 3), own_t, pl.ds(6, 2))))

    sources = {VT: vel_ref.at[2], EN: ene_ref, VR: vel_ref.at[1], DE: den_ref, VP: vel_ref.at[0]}

    def regroup(fields):
        def one(tp, _):
            for h in range(2):
                dest = owner(tp, h)
                for f in fields:
                    for c in range(2):
                        for t in range(2):
                            stage[dest, f, pl.ds(c * 8 + t * 4, 4), :] = sources[f][
                                2 * tp + t, pl.ds(4 * h, 4), pl.ds(128 * c, 128)
                            ]
            return 0

        lax.fori_loop(0, 8, one, 0, unroll=4)

    def to_rows(k, g):
        dest = peers[k]
        return pltpu.make_async_remote_copy(
            src_ref=stage.at[dest, SPANS[g]],
            dst_ref=rows.at[SPANS[g], pl.ds(pl.multiple_of(a * 16, 16), 16), :],
            send_sem=a_send.at[g, k],
            recv_sem=a_recv.at[g],
            device_id={"az": dest, "rad": rho},
            device_id_type=MESH,
        )

    def whole_rows(g):
        cells = rows.at[SPANS[g], pl.ds(0, 256), :]
        return pltpu.make_async_copy(cells, cells, a_recv.at[g])

    def own_rows(g):
        return pltpu.make_async_copy(
            stage.at[a, SPANS[g]], rows.at[SPANS[g], pl.ds(pl.multiple_of(a * 16, 16), 16), :], a_recv.at[g]
        )

    for copy in loads[:2]:
        copy.wait()
    regroup(EARLY)
    pl.semaphore_wait(barrier, AZ - 1 + has_cross.astype(jnp.int32))
    for k in ORDER:
        to_rows(k, 0).start()
    own_rows(0).start()
    for copy in loads[2:]:
        copy.wait()
    regroup(LATE)
    for k in ORDER:
        to_rows(k, 1).start()
    own_rows(1).start()

    lane = lax.broadcasted_iota(jnp.int32, (CHUNKS, 128), 1)
    lane8 = lax.broadcasted_iota(jnp.int32, (8, 128), 1)

    t_up, t_dn = lax.rem(pair + 1, 8), lax.rem(pair + 7, 8)
    r_up, r_dn = lax.rem(quad + 1, QUADS), lax.rem(quad + QUADS - 1, QUADS)
    has_tup, has_tdn = pair < 7, pair > 0
    has_rup, has_rdn = quad < QUADS - 1, quad > 0
    id_tup = {"az": owner(t_up, half), "rad": rho}
    id_tdn = {"az": owner(t_dn, half), "rad": rho}
    id_rup = {"az": owner(pair, lax.rem(r_up, 2)), "rad": lax.div(r_up, 2)}
    id_rdn = {"az": owner(pair, lax.rem(r_dn, 2)), "rad": lax.div(r_dn, 2)}

    def four(slot, r_up, r_dn, t_up, t_dn):
        def one(pair_of_refs, ident, d):
            return pltpu.make_async_remote_copy(
                src_ref=pair_of_refs[0], dst_ref=pair_of_refs[1], send_sem=h_send.at[slot, d],
                recv_sem=h_recv.at[slot, d], device_id=ident, device_id_type=MESH,
            )

        return (
            (one(r_up, id_rup, 2), has_rup, has_rdn),
            (one(r_dn, id_rdn, 3), has_rdn, has_rup),
            (one(t_up, id_tup, 0), has_tup, has_tdn),
            (one(t_dn, id_tdn, 1), has_tdn, has_tup),
        )

    def old_energy(step, slot):
        en = states[step].at[S_AT[EN]]
        return four(
            slot,
            (en.at[own_t, pl.ds(4, 2)], en.at[own_t, low_two]),
            (en.at[own_t, pl.ds(2, 2)], en.at[own_t, pl.ds(6, 2)]),
            (en.at[own_t, own_r], en.at[low_two, own_r]),
            (en.at[own_t, own_r], en.at[pl.ds(4, 2), own_r]),
        )

    def old_speeds(step, slot):
        vt, vr = states[step].at[S_AT[VT]], states[step].at[S_AT[VR]]
        return four(
            slot,
            (vr.at[own_t, 5], vr.at[own_t, 1]),
            (vr.at[own_t, 2], vr.at[own_t, 6]),
            (vt.at[3, own_r], vt.at[1, own_r]),
            (vt.at[2, own_r], vt.at[4, own_r]),
        )

    def halo(buf, t_fields, r_fields, slot):
        return four(
            slot,
            (buf.at[r_fields, inner_t, 4], buf.at[r_fields, inner_t, 0]),
            (buf.at[r_fields, inner_t, 1], buf.at[r_fields, inner_t, 5]),
            (buf.at[t_fields, 2, inner_r], buf.at[t_fields, 0, inner_r]),
            (buf.at[t_fields, 1, inner_r], buf.at[t_fields, 3, inner_r]),
        )

    def each(copies, what):
        for copy, sends, gets in copies:
            @pl.when(gets if what == "wait_recv" else sends)
            def _():
                getattr(copy, what)()

    def eight(body, unroll=1):
        def one(i, _):
            body(i, lax.div(i, 4) + 1, lax.rem(i, 4) + 1)
            return 0

        lax.fori_loop(0, 8, one, 0, unroll=unroll)

    def unpack(fields):
        def one(i, t, r):
            for q in fields:
                value = rows[q, pl.ds(i, CHUNKS, stride=8), :]
                if q == DE:
                    f0[F_AT[DE], t, r] = value
                else:
                    s0[S_AT[q], t + 1, r + 1] = value

        eight(one, UNROLL)

    def to_blocks(k, g):
        dest = peers[k]
        return pltpu.make_async_remote_copy(
            src_ref=ostage.at[SPANS[g], pl.ds(pl.multiple_of(dest * 16, 16), 16), :],
            dst_ref=back.at[a, SPANS[g]],
            send_sem=b_send.at[g, k],
            recv_sem=b_recv.at[g],
            device_id={"az": dest, "rad": rho},
            device_id_type=MESH,
        )

    def own_blocks(g):
        return pltpu.make_async_copy(
            ostage.at[SPANS[g], pl.ds(pl.multiple_of(a * 16, 16), 16), :], back.at[a, SPANS[g]], b_recv.at[g]
        )

    olds_en = (old_energy(0, 0), old_energy(1, 1))
    olds_v = (old_speeds(0, 2), old_speeds(1, 3))
    lates = tuple(halo(fresh[step], pl.ds(0, 2), pl.ds(0, 2), 4 + step) for step in range(STEPS))
    new_ens = tuple(halo(fresh[step], F_AT[EN], F_AT[EN], 6 + step) for step in range(STEPS))
    rests = tuple(halo(fresh[step], F_AT[VR], F_AT[VT], 8 + step) for step in range(STEPS))
    halos = olds_en + olds_v + lates + new_ens + rests

    def along_azimuth(f, i, t, r, fields):
        p_lo = speed[i]
        for q in fields:
            v = f[F_AT[q], t, r]
            low = p_lo * jnp.where(p_lo > 0, prev_cell(v, lane), v)
            flux[q, i] = next_cell(low, lane) - low

    def face(f, u, below, above):
        s = f[(F_AT[u],) + below] + f[(F_AT[u],) + above]
        up = s > 0
        return lambda q: s * jnp.where(up, f[(F_AT[q],) + below], f[(F_AT[q],) + above])

    def begin(step):
        s, f = states[step], fresh[step]

        def source_azimuth(i, t, r):
            den = f[F_AT[DE], t, r]
            k = 0.01 / jnp.where(den > 0, den, 1.0)
            e = s[S_AT[EN], t + 1, r + 1]
            vp = s[S_AT[VP], t + 1, r + 1]
            new = vp - k * (next_cell(e, lane) - prev_cell(e, lane))
            f[F_AT[VP], t, r] = new
            factor[i] = k
            along[i] = next_cell(vp, lane) - prev_cell(vp, lane)
            speed[i] = new + prev_cell(new, lane)

        eight(source_azimuth, UNROLL)
        each(lates[step], "start")

    for step in range(STEPS):
        s, f = states[step], fresh[step]
        last = step == STEPS - 1

        if step == 0:
            whole_rows(0).wait()
            unpack(EARLY)
            each(olds_en[0], "start")
            each(olds_v[0], "start")
            whole_rows(1).wait()
            unpack(LATE)
            begin(0)

        def azimuth_late(i, t, r):
            along_azimuth(f, i, t, r, LATE)

        eight(azimuth_late)

        def source_speeds(i, t, r):
            k = factor[i]
            f[F_AT[VR], t, r] = s[S_AT[VR], t + 1, r + 1] - k * (s[S_AT[EN], t + 1, r + 2] - s[S_AT[EN], t + 1, r])
            f[F_AT[VT], t, r] = s[S_AT[VT], t + 1, r + 1] - k * (s[S_AT[EN], t + 2, r + 1] - s[S_AT[EN], t, r + 1])

        def source_energy(i, t, r):
            e = s[S_AT[EN], t + 1, r + 1]
            div = (
                along[i]
                + (s[S_AT[VR], t + 1, r + 2] - s[S_AT[VR], t + 1, r])
                + (s[S_AT[VT], t + 2, r + 1] - s[S_AT[VT], t, r + 1])
            )
            f[F_AT[EN], t, r] = e - 0.01 * e * div

        def beyond(u, place, near, far, own):
            den = f[(F_AT[DE],) + place]
            k = 0.01 / jnp.where(den > 0, den, 1.0)
            low, high = (far, own) if near < own else (own, far)
            en = S_AT[EN]
            t, r = place
            if u == VT:
                new = s[S_AT[VT], near, r + 1] - k * (s[en, high, r + 1] - s[en, low, r + 1])
            else:
                new = s[S_AT[VR], t + 1, near] - k * (s[en, t + 1, high] - s[en, t + 1, low])
            f[(F_AT[u],) + place] = new

        def all_beyond():
            @pl.when(has_tdn)
            def _():
                for r in range(1, 5):
                    beyond(VT, (0, r), 1, 0, 2)

            @pl.when(has_tup)
            def _():
                for r in range(1, 5):
                    beyond(VT, (3, r), 4, 5, 3)

            @pl.when(has_rdn)
            def _():
                for t in range(1, 3):
                    beyond(VR, (t, 0), 1, 0, 2)

            @pl.when(has_rup)
            def _():
                for t in range(1, 3):
                    beyond(VR, (t, 5), 6, 7, 5)

        if last:
            each(olds_v[1], "wait_recv")
            eight(source_energy, UNROLL)
            each(new_ens[1], "start")
            each(olds_en[1], "wait_recv")
            eight(source_speeds, UNROLL)
            each(rests[1], "start")
        else:
            each(olds_en[0], "wait_recv")
            eight(source_speeds, UNROLL)
            each(rests[0], "start")
            each(olds_v[0], "wait_recv")
            eight(source_energy, UNROLL)
            each(new_ens[0], "start")

        def azimuth_early(i, t, r):
            along_azimuth(f, i, t, r, EARLY)

        def inner_faces(fields):
            def inner_radius(n, _):
                t, r = lax.div(n, 3), lax.rem(n, 3)
                one = face(f, VR, (t + 1, r + 1), (t + 1, r + 2))
                for q in fields:
                    v = one(q)
                    flux[q, 4 * t + r] += v
                    flux[q, 4 * t + r + 1] -= v
                return 0

            lax.fori_loop(0, 6, inner_radius, 0)

            def inner_theta(r, _):
                one = face(f, VT, (1, r + 1), (2, r + 1))
                for q in fields:
                    v = one(q)
                    flux[q, r] += v
                    flux[q, 4 + r] -= v
                return 0

            lax.fori_loop(0, 4, inner_theta, 0)

        inner_faces(LATE)
        if not last:
            eight(azimuth_early)
            inner_faces(EARLY)
        each(lates[step], "wait_recv")
        all_beyond()

        for g, fields in ((1, LATE), (0, EARLY)) if last else ((0, (VT, VR)), (0, (EN,)), (1, LATE)):
            if last and EN in fields:
                eight(azimuth_early)
                inner_faces(EARLY)
                each(rests[1], "wait_recv")
                each(new_ens[1], "wait_recv")
            elif not last and DE not in fields:
                each(new_ens[0] if EN in fields else rests[0], "wait_recv")

            def outer_radius(t, _):
                low = face(f, VR, (t + 1, 0), (t + 1, 1))
                high = face(f, VR, (t + 1, 4), (t + 1, 5))
                for q in fields:
                    flux[q, 4 * t] -= low(q)
                    flux[q, 4 * t + 3] += high(q)
                return 0

            lax.fori_loop(0, 2, outer_radius, 0)

            def outer_theta(r, _):
                low = face(f, VT, (0, r + 1), (1, r + 1))
                high = face(f, VT, (2, r + 1), (3, r + 1))
                for q in fields:
                    flux[q, r] -= low(q)
                    flux[q, 4 + r] += high(q)
                return 0

            lax.fori_loop(0, 4, outer_theta, 0)

            def finish(i, t, r):
                for q in fields:
                    moved = f[F_AT[q], t, r] - 0.025 * flux[q, i]
                    blended[q, i, pl.ds(0, CHUNKS), :] = moved
                    blended[q, i, pl.ds(CHUNKS, CHUNKS), :] = moved

            eight(finish, UNROLL)

            def rotate(i, t, r):
                w = frac_ref[half * 4 + r - 1]
                shift = shift_ref[half * 4 + r - 1]
                views = []
                for back_cells in (0, 1):
                    ahead = lax.rem(2 * CELLS - shift - back_cells, CELLS)
                    views.append((lax.div(ahead, 128), lax.rem(ahead, 128)))
                for q in fields:
                    for m in range(4):
                        parts = []
                        for whole, part in views:
                            near = blended[q, i, pl.ds(whole + 8 * m, 8), :]
                            far = blended[q, i, pl.ds(whole + 8 * m + 1, 8), :]
                            parts.append(pltpu.roll(jnp.where(lane8 < part, far, near), lax.rem(128 - part, 128), 1))
                        out = (1.0 - w) * parts[0] + w * parts[1]
                        if last:
                            ostage[q, pl.ds(64 * m + i, 8, stride=8), :] = out
                        elif q == DE:
                            f1[F_AT[DE], t, r, pl.ds(8 * m, 8), :] = out
                        else:
                            s1[S_AT[q], t + 1, r + 1, pl.ds(8 * m, 8), :] = out

            eight(rotate, UNROLL)
            if last:
                for k in ORDER:
                    to_blocks(k, g).start()
                own_blocks(g).start()
            elif EN in fields:
                each(olds_en[1], "start")
            elif VT in fields:
                each(olds_v[1], "start")
            else:
                begin(step + 1)

    for copies in halos:
        each(copies, "wait_send")
    for g in range(2):
        for k in range(1, AZ):
            to_rows(k, g).wait_send()
            to_blocks(k, g).wait_send()
    for g in range(2):
        pltpu.make_async_copy(back.at[:, SPANS[g]], back.at[:, SPANS[g]], b_recv.at[g]).wait()


def write_out(back, den_hbm, vel_hbm, ene_hbm, den_out, vel_out, ene_out, out_sem):
    targets = {
        VT: (vel_out.at[2], vel_hbm.at[2]), EN: (ene_out, ene_hbm), VR: (vel_out.at[1], vel_hbm.at[1]),
        DE: (den_out, den_hbm), VP: (vel_out.at[0], vel_hbm.at[0]),
    }
    writes = []
    for q in range(5):
        dst = targets[q][0]

        def one(tp, _):
            for h in range(2):
                src = owner(tp, h)
                for c in range(2):
                    for t in range(2):
                        dst[2 * tp + t, pl.ds(4 * h, 4), pl.ds(128 * c, 128)] = back[
                            src, q, pl.ds(c * 8 + t * 4, 4), :
                        ]
            return 0

        lax.fori_loop(0, 8, one, 0, unroll=8)
        writes.append(pltpu.make_async_copy(*targets[q], out_sem.at[q]))
        writes[-1].start()
    for copy in writes:
        copy.wait()


def shards(density, velocity, energy, shifts, fraction):
    hbm = pl.BlockSpec(memory_space=pl.ANY)
    f32 = jnp.float32
    limit = 40 * 1024 * 1024
    block = (AZ, 5, 16, 128)
    dma = pltpu.SemaphoreType.DMA
    fields = [pltpu.VMEM(v.shape, f32) for v in (density, velocity, energy)]
    back = pl.pallas_call(
        kernel,
        out_shape=pltpu.VMEM(block, f32),
        in_specs=[hbm] * 5,
        out_specs=hbm,
        scratch_shapes=fields + [
            pltpu.SMEM(shifts.shape, jnp.int32),
            pltpu.SMEM(fraction.shape, f32),
            pltpu.VMEM(block, f32),
            pltpu.VMEM((5, PADDED, 128), f32),
            pltpu.VMEM((4, 6, 8, CHUNKS, 128), f32),
            pltpu.VMEM((4, 6, 8, CHUNKS, 128), f32),
            pltpu.VMEM((5, 4, 6, CHUNKS, 128), f32),
            pltpu.VMEM((5, 4, 6, CHUNKS, 128), f32),
            pltpu.VMEM((8, CHUNKS, 128), f32),
            pltpu.VMEM((8, CHUNKS, 128), f32),
            pltpu.VMEM((8, CHUNKS, 128), f32),
            pltpu.VMEM((5, 8, CHUNKS, 128), f32),
            pltpu.VMEM((5, 8, 2 * CHUNKS, 128), f32),
            pltpu.VMEM((5, PADDED, 128), f32),
            dma((2, AZ)),
            dma((2,)),
            dma((10, 4)),
            dma((10, 4)),
            dma((2, AZ)),
            dma((2,)),
            dma((4,)),
            dma((5,)),
        ],
        compiler_params=pltpu.CompilerParams(collective_id=0, has_side_effects=True, vmem_limit_bytes=limit),
    )(*(pltpu.with_memory_space_constraint(v, pltpu.HBM) for v in (density, velocity, energy, shifts, fraction)))
    return pl.pallas_call(
        write_out,
        out_shape=tuple(jax.ShapeDtypeStruct(v.shape, f32) for v in (density, velocity, energy)),
        in_specs=[pl.BlockSpec(memory_space=pltpu.VMEM)],
        out_specs=(hbm,) * 3,
        scratch_shapes=fields + [dma((5,))],
        compiler_params=pltpu.CompilerParams(vmem_limit_bytes=16 * 1024 * 1024),
    )(pltpu.with_memory_space_constraint(back, pltpu.VMEM))


def solution(mesh):
    placed = (
        P(None, "rad", "az"),
        P(None, None, "rad", "az"),
        P(None, "rad", "az"),
        P("rad"),
        P("rad"),
    )
    return jax.shard_map(
        shards,
        mesh=mesh,
        in_specs=placed,
        out_specs=(P(None, "rad", "az"), P(None, None, "rad", "az"), P(None, "rad", "az")),
        check_vma=False,
    )
```

```python
import jax
import jax.numpy as jnp
from jax import lax
from jax.experimental import pallas as pl
from jax.experimental.pallas import tpu as pltpu
from jax.sharding import PartitionSpec as P

MESH = pl.DeviceIdType.MESH
AZ = 16
QUADS = 32
CHUNKS = 32
CELLS = 4096
PADDED = 264
STEPS = 2

EN, VT, VR, DE, VP = range(5)
EARLY, LATE = (EN, VT, VR), (DE, VP)
GROUPS = (EARLY, LATE)
SPANS = (pl.ds(0, 3), pl.ds(3, 2))
S_AT = {VR: 0, EN: 1, VT: 2, VP: 3}
F_AT = {DE: 0, VP: 1, VR: 2, EN: 3, VT: 4}
UNROLL = 8
ORDER = (10, 8, 6, 4, 14, 12, 2, 11, 9, 7, 5, 15, 13, 3, 1)


def owner(pair, half):
    return lax.div(pair, 2) * 4 + (1 - half) * 2 + lax.rem(pair, 2)


def prev_cell(x, lane):
    x1 = pltpu.roll(x, 1, 1)
    return jnp.where(lane == 0, pltpu.roll(x1, 1, 0), x1)


def next_cell(x, lane):
    x1 = pltpu.roll(x, 127, 1)
    return jnp.where(lane == 127, pltpu.roll(x1, CHUNKS - 1, 0), x1)


def kernel(
    den_hbm, vel_hbm, ene_hbm, shift_hbm, frac_hbm,
    back,
    den_ref, vel_ref, ene_ref, shift_ref, frac_ref,
    stage, rows, s0, s1, f0, f1, speed, factor, along, flux, blended, ostage,
    a_send, a_recv, h_send, h_recv, b_send, b_recv, l_sem, i_sem,
):
    a = lax.axis_index("az")
    rho = lax.axis_index("rad")
    x, y, core = lax.div(a, 4), lax.rem(lax.div(a, 2), 2), lax.rem(a, 2)
    half = 1 - y
    pair = 2 * x + core
    quad = 2 * rho + half
    states, fresh = (s0, s1), (f0, f1)

    loads = [
        pltpu.make_async_copy(src, dst, i_sem.at[n])
        for n, (src, dst) in enumerate((
            (ene_hbm, ene_ref), (vel_hbm, vel_ref), (den_hbm, den_ref), (shift_hbm, shift_ref), (frac_hbm, frac_ref)
        ))
    ]
    for copy in loads[:3]:
        copy.start()

    peers = []
    for k in range(AZ):
        dx, dy, dc = k // 4, (k // 2) % 2, k % 2
        peers.append(lax.rem(x + dx, 4) * 4 + lax.rem(y + dy, 2) * 2 + lax.rem(core + dc, 2))

    barrier = pltpu.get_barrier_semaphore()
    for k in range(1, AZ):
        pl.semaphore_signal(barrier, inc=1, device_id={"az": peers[k], "rad": rho}, device_id_type=MESH)
    cross = lax.rem(quad + 2 * half - 1 + QUADS, QUADS)
    has_cross = jnp.logical_and(quad > 0, quad < QUADS - 1)

    @pl.when(has_cross)
    def _():
        pl.semaphore_signal(
            barrier, inc=1, device_id={"az": owner(pair, lax.rem(cross, 2)), "rad": lax.div(cross, 2)},
            device_id_type=MESH,
        )

    for copy in loads[3:]:
        copy.start()

    inner_t, inner_r = pl.ds(1, 2), pl.ds(1, 4)
    own_t, own_r = pl.ds(2, 2), pl.ds(2, 4)
    low_two = pl.ds(0, 2)

    def clear(buf, where):
        buf[where] = jnp.zeros_like(buf[where])

    for buf in (f0, f1):
        pl.when(pair == 0)(lambda: clear(buf, (pl.ds(0, 5), 0, inner_r)))
        pl.when(pair == 7)(lambda: clear(buf, (pl.ds(0, 5), 3, inner_r)))
        pl.when(quad == 0)(lambda: clear(buf, (pl.ds(0, 5), inner_t, 0)))
        pl.when(quad == QUADS - 1)(lambda: clear(buf, (pl.ds(0, 5), inner_t, 5)))
    for buf in (s0, s1):
        pl.when(pair == 0)(lambda: clear(buf, (pl.ds(0, 3), low_two, own_r)))
        pl.when(pair == 7)(lambda: clear(buf, (pl.ds(0, 3), pl.ds(4, 2), own_r)))
        pl.when(quad == 0)(lambda: clear(buf, (pl.ds(0, 3), own_t, low_two)))
        pl.when(quad == QUADS - 1)(lambda: clear(buf, (pl.ds(0, 3), own_t, pl.ds(6, 2))))

    sources = {VT: vel_ref.at[2], EN: ene_ref, VR: vel_ref.at[1], DE: den_ref, VP: vel_ref.at[0]}

    def regroup(fields):
        def one(tp, _):
            for h in range(2):
                dest = owner(tp, h)
                for f in fields:
                    for c in range(2):
                        for t in range(2):
                            stage[dest, f, pl.ds(c * 8 + t * 4, 4), :] = sources[f][
                                2 * tp + t, pl.ds(4 * h, 4), pl.ds(128 * c, 128)
                            ]
            return 0

        lax.fori_loop(0, 8, one, 0, unroll=4)

    def to_rows(k, g):
        dest = peers[k]
        return pltpu.make_async_remote_copy(
            src_ref=stage.at[dest, SPANS[g]],
            dst_ref=rows.at[SPANS[g], pl.ds(pl.multiple_of(a * 16, 16), 16), :],
            send_sem=a_send.at[g, k],
            recv_sem=a_recv.at[g],
            device_id={"az": dest, "rad": rho},
            device_id_type=MESH,
        )

    def whole_rows(g):
        cells = rows.at[SPANS[g], pl.ds(0, 256), :]
        return pltpu.make_async_copy(cells, cells, a_recv.at[g])

    def own_rows(g):
        return pltpu.make_async_copy(
            stage.at[a, SPANS[g]], rows.at[SPANS[g], pl.ds(pl.multiple_of(a * 16, 16), 16), :], a_recv.at[g]
        )

    for copy in loads[:2]:
        copy.wait()
    regroup(EARLY)
    pl.semaphore_wait(barrier, AZ - 1 + has_cross.astype(jnp.int32))
    for k in ORDER:
        to_rows(k, 0).start()
    own_rows(0).start()
    for copy in loads[2:]:
        copy.wait()
    regroup(LATE)
    for k in ORDER:
        to_rows(k, 1).start()
    own_rows(1).start()

    lane = lax.broadcasted_iota(jnp.int32, (CHUNKS, 128), 1)
    lane8 = lax.broadcasted_iota(jnp.int32, (8, 128), 1)

    t_up, t_dn = lax.rem(pair + 1, 8), lax.rem(pair + 7, 8)
    r_up, r_dn = lax.rem(quad + 1, QUADS), lax.rem(quad + QUADS - 1, QUADS)
    has_tup, has_tdn = pair < 7, pair > 0
    has_rup, has_rdn = quad < QUADS - 1, quad > 0
    id_tup = {"az": owner(t_up, half), "rad": rho}
    id_tdn = {"az": owner(t_dn, half), "rad": rho}
    id_rup = {"az": owner(pair, lax.rem(r_up, 2)), "rad": lax.div(r_up, 2)}
    id_rdn = {"az": owner(pair, lax.rem(r_dn, 2)), "rad": lax.div(r_dn, 2)}

    def four(slot, r_up, r_dn, t_up, t_dn):
        def one(pair_of_refs, ident, d):
            return pltpu.make_async_remote_copy(
                src_ref=pair_of_refs[0], dst_ref=pair_of_refs[1], send_sem=h_send.at[slot, d],
                recv_sem=h_recv.at[slot, d], device_id=ident, device_id_type=MESH,
            )

        return (
            (one(r_up, id_rup, 2), has_rup, has_rdn),
            (one(r_dn, id_rdn, 3), has_rdn, has_rup),
            (one(t_up, id_tup, 0), has_tup, has_tdn),
            (one(t_dn, id_tdn, 1), has_tdn, has_tup),
        )

    def old_energy(step, slot):
        en = states[step].at[S_AT[EN]]
        return four(
            slot,
            (en.at[own_t, pl.ds(4, 2)], en.at[own_t, low_two]),
            (en.at[own_t, pl.ds(2, 2)], en.at[own_t, pl.ds(6, 2)]),
            (en.at[own_t, own_r], en.at[low_two, own_r]),
            (en.at[own_t, own_r], en.at[pl.ds(4, 2), own_r]),
        )

    def old_speeds(step, slot):
        vt, vr = states[step].at[S_AT[VT]], states[step].at[S_AT[VR]]
        return four(
            slot,
            (vr.at[own_t, 5], vr.at[own_t, 1]),
            (vr.at[own_t, 2], vr.at[own_t, 6]),
            (vt.at[3, own_r], vt.at[1, own_r]),
            (vt.at[2, own_r], vt.at[4, own_r]),
        )

    def halo(buf, t_fields, r_fields, slot):
        return four(
            slot,
            (buf.at[r_fields, inner_t, 4], buf.at[r_fields, inner_t, 0]),
            (buf.at[r_fields, inner_t, 1], buf.at[r_fields, inner_t, 5]),
            (buf.at[t_fields, 2, inner_r], buf.at[t_fields, 0, inner_r]),
            (buf.at[t_fields, 1, inner_r], buf.at[t_fields, 3, inner_r]),
        )

    def each(copies, what):
        for copy, sends, gets in copies:
            @pl.when(gets if what == "wait_recv" else sends)
            def _():
                getattr(copy, what)()

    def eight(body, unroll=1):
        def one(i, _):
            body(i, lax.div(i, 4) + 1, lax.rem(i, 4) + 1)
            return 0

        lax.fori_loop(0, 8, one, 0, unroll=unroll)

    def unpack(fields):
        def one(i, t, r):
            for q in fields:
                value = rows[q, pl.ds(i, CHUNKS, stride=8), :]
                if q == DE:
                    f0[F_AT[DE], t, r] = value
                else:
                    s0[S_AT[q], t + 1, r + 1] = value

        eight(one, UNROLL)

    def to_blocks(k, g):
        dest = peers[k]
        return pltpu.make_async_remote_copy(
            src_ref=ostage.at[SPANS[g], pl.ds(pl.multiple_of(dest * 16, 16), 16), :],
            dst_ref=back.at[a, SPANS[g]],
            send_sem=b_send.at[g, k],
            recv_sem=b_recv.at[g],
            device_id={"az": dest, "rad": rho},
            device_id_type=MESH,
        )

    def own_blocks(g):
        return pltpu.make_async_copy(
            ostage.at[SPANS[g], pl.ds(pl.multiple_of(a * 16, 16), 16), :], back.at[a, SPANS[g]], b_recv.at[g]
        )

    olds_en = (old_energy(0, 0), old_energy(1, 1))
    olds_v = (old_speeds(0, 2), old_speeds(1, 3))
    lates = tuple(halo(fresh[step], pl.ds(0, 2), pl.ds(0, 2), 4 + step) for step in range(STEPS))
    new_ens = tuple(halo(fresh[step], F_AT[EN], F_AT[EN], 6 + step) for step in range(STEPS))
    rests = tuple(halo(fresh[step], F_AT[VR], F_AT[VT], 8 + step) for step in range(STEPS))
    halos = olds_en + olds_v + lates + new_ens + rests

    def along_azimuth(f, i, t, r, fields):
        p_lo = speed[i]
        for q in fields:
            v = f[F_AT[q], t, r]
            low = p_lo * jnp.where(p_lo > 0, prev_cell(v, lane), v)
            flux[q, i] = next_cell(low, lane) - low

    def face(f, u, below, above):
        s = f[(F_AT[u],) + below] + f[(F_AT[u],) + above]
        up = s > 0
        return lambda q: s * jnp.where(up, f[(F_AT[q],) + below], f[(F_AT[q],) + above])

    def begin(step):
        s, f = states[step], fresh[step]

        def source_azimuth(i, t, r):
            den = f[F_AT[DE], t, r]
            k = 0.01 / jnp.where(den > 0, den, 1.0)
            e = s[S_AT[EN], t + 1, r + 1]
            vp = s[S_AT[VP], t + 1, r + 1]
            new = vp - k * (next_cell(e, lane) - prev_cell(e, lane))
            f[F_AT[VP], t, r] = new
            factor[i] = k
            along[i] = next_cell(vp, lane) - prev_cell(vp, lane)
            speed[i] = new + prev_cell(new, lane)

        eight(source_azimuth, UNROLL)
        each(lates[step], "start")

    for step in range(STEPS):
        s, f = states[step], fresh[step]
        last = step == STEPS - 1

        if step == 0:
            whole_rows(0).wait()
            unpack(EARLY)
            each(olds_en[0], "start")
            each(olds_v[0], "start")
            whole_rows(1).wait()
            unpack(LATE)
            begin(0)

        def azimuth_late(i, t, r):
            along_azimuth(f, i, t, r, LATE)

        eight(azimuth_late)

        def source_speeds(i, t, r):
            k = factor[i]
            f[F_AT[VR], t, r] = s[S_AT[VR], t + 1, r + 1] - k * (s[S_AT[EN], t + 1, r + 2] - s[S_AT[EN], t + 1, r])
            f[F_AT[VT], t, r] = s[S_AT[VT], t + 1, r + 1] - k * (s[S_AT[EN], t + 2, r + 1] - s[S_AT[EN], t, r + 1])

        def source_energy(i, t, r):
            e = s[S_AT[EN], t + 1, r + 1]
            div = (
                along[i]
                + (s[S_AT[VR], t + 1, r + 2] - s[S_AT[VR], t + 1, r])
                + (s[S_AT[VT], t + 2, r + 1] - s[S_AT[VT], t, r + 1])
            )
            f[F_AT[EN], t, r] = e - 0.01 * e * div

        def beyond(u, place, near, far, own):
            den = f[(F_AT[DE],) + place]
            k = 0.01 / jnp.where(den > 0, den, 1.0)
            low, high = (far, own) if near < own else (own, far)
            en = S_AT[EN]
            t, r = place
            if u == VT:
                new = s[S_AT[VT], near, r + 1] - k * (s[en, high, r + 1] - s[en, low, r + 1])
            else:
                new = s[S_AT[VR], t + 1, near] - k * (s[en, t + 1, high] - s[en, t + 1, low])
            f[(F_AT[u],) + place] = new

        def all_beyond():
            @pl.when(has_tdn)
            def _():
                for r in range(1, 5):
                    beyond(VT, (0, r), 1, 0, 2)

            @pl.when(has_tup)
            def _():
                for r in range(1, 5):
                    beyond(VT, (3, r), 4, 5, 3)

            @pl.when(has_rdn)
            def _():
                for t in range(1, 3):
                    beyond(VR, (t, 0), 1, 0, 2)

            @pl.when(has_rup)
            def _():
                for t in range(1, 3):
                    beyond(VR, (t, 5), 6, 7, 5)

        if last:
            each(olds_v[1], "wait_recv")
            eight(source_energy, UNROLL)
            each(new_ens[1], "start")
            each(olds_en[1], "wait_recv")
            eight(source_speeds, UNROLL)
            each(rests[1], "start")
        else:
            each(olds_en[0], "wait_recv")
            eight(source_speeds, UNROLL)
            each(rests[0], "start")
            each(olds_v[0], "wait_recv")
            eight(source_energy, UNROLL)
            each(new_ens[0], "start")

        def azimuth_early(i, t, r):
            along_azimuth(f, i, t, r, EARLY)

        def inner_faces(fields):
            def inner_radius(n, _):
                t, r = lax.div(n, 3), lax.rem(n, 3)
                one = face(f, VR, (t + 1, r + 1), (t + 1, r + 2))
                for q in fields:
                    v = one(q)
                    flux[q, 4 * t + r] += v
                    flux[q, 4 * t + r + 1] -= v
                return 0

            lax.fori_loop(0, 6, inner_radius, 0)

            def inner_theta(r, _):
                one = face(f, VT, (1, r + 1), (2, r + 1))
                for q in fields:
                    v = one(q)
                    flux[q, r] += v
                    flux[q, 4 + r] -= v
                return 0

            lax.fori_loop(0, 4, inner_theta, 0)

        inner_faces(LATE)
        if not last:
            eight(azimuth_early)
            inner_faces(EARLY)
        each(lates[step], "wait_recv")
        all_beyond()

        for g, fields in ((1, LATE), (-1, (VT, VR)), (0, (EN,))) if last else ((0, (VT, VR)), (0, (EN,)), (1, LATE)):
            if last and VT in fields:
                eight(azimuth_early)
                inner_faces(EARLY)
                each(rests[1], "wait_recv")
            elif last and EN in fields:
                each(new_ens[1], "wait_recv")
            elif not last and DE not in fields:
                each(new_ens[0] if EN in fields else rests[0], "wait_recv")

            def outer_radius(t, _):
                low = face(f, VR, (t + 1, 0), (t + 1, 1))
                high = face(f, VR, (t + 1, 4), (t + 1, 5))
                for q in fields:
                    flux[q, 4 * t] -= low(q)
                    flux[q, 4 * t + 3] += high(q)
                return 0

            lax.fori_loop(0, 2, outer_radius, 0, unroll=2)

            def outer_theta(r, _):
                low = face(f, VT, (0, r + 1), (1, r + 1))
                high = face(f, VT, (2, r + 1), (3, r + 1))
                for q in fields:
                    flux[q, r] -= low(q)
                    flux[q, 4 + r] += high(q)
                return 0

            lax.fori_loop(0, 4, outer_theta, 0, unroll=4)

            def finish(i, t, r):
                for q in fields:
                    moved = f[F_AT[q], t, r] - 0.025 * flux[q, i]
                    blended[q, i, pl.ds(0, CHUNKS), :] = moved
                    blended[q, i, pl.ds(CHUNKS, CHUNKS), :] = moved

            eight(finish, UNROLL)

            def rotate(i, t, r):
                w = frac_ref[half * 4 + r - 1]
                shift = shift_ref[half * 4 + r - 1]
                views = []
                for back_cells in (0, 1):
                    ahead = lax.rem(2 * CELLS - shift - back_cells, CELLS)
                    views.append((lax.div(ahead, 128), lax.rem(ahead, 128)))
                for q in fields:
                    for m in range(4):
                        parts = []
                        for whole, part in views:
                            near = blended[q, i, pl.ds(whole + 8 * m, 8), :]
                            far = blended[q, i, pl.ds(whole + 8 * m + 1, 8), :]
                            parts.append(pltpu.roll(jnp.where(lane8 < part, far, near), lax.rem(128 - part, 128), 1))
                        out = (1.0 - w) * parts[0] + w * parts[1]
                        if last:
                            ostage[q, pl.ds(64 * m + i, 8, stride=8), :] = out
                        elif q == DE:
                            f1[F_AT[DE], t, r, pl.ds(8 * m, 8), :] = out
                        else:
                            s1[S_AT[q], t + 1, r + 1, pl.ds(8 * m, 8), :] = out

            eight(rotate, UNROLL)
            if last and g >= 0:
                for k in ORDER:
                    to_blocks(k, g).start()
                own_blocks(g).start()
            elif last:
                pass
            elif EN in fields:
                each(olds_en[1], "start")
            elif VT in fields:
                each(olds_v[1], "start")
            else:
                begin(step + 1)

    for copies in halos:
        each(copies, "wait_send")
    for g in range(2):
        for k in range(1, AZ):
            to_rows(k, g).wait_send()
            to_blocks(k, g).wait_send()
    for g in range(2):
        pltpu.make_async_copy(back.at[:, SPANS[g]], back.at[:, SPANS[g]], b_recv.at[g]).wait()


def write_out(back, den_hbm, vel_hbm, ene_hbm, den_out, vel_out, ene_out, out_sem):
    targets = {
        VT: (vel_out.at[2], vel_hbm.at[2]), EN: (ene_out, ene_hbm), VR: (vel_out.at[1], vel_hbm.at[1]),
        DE: (den_out, den_hbm), VP: (vel_out.at[0], vel_hbm.at[0]),
    }
    writes = []
    for q in range(5):
        dst = targets[q][0]

        def one(tp, _):
            for h in range(2):
                src = owner(tp, h)
                for c in range(2):
                    for t in range(2):
                        dst[2 * tp + t, pl.ds(4 * h, 4), pl.ds(128 * c, 128)] = back[
                            src, q, pl.ds(c * 8 + t * 4, 4), :
                        ]
            return 0

        lax.fori_loop(0, 8, one, 0, unroll=8)
        writes.append(pltpu.make_async_copy(*targets[q], out_sem.at[q]))
        writes[-1].start()
    for copy in writes:
        copy.wait()


def shards(density, velocity, energy, shifts, fraction):
    hbm = pl.BlockSpec(memory_space=pl.ANY)
    f32 = jnp.float32
    limit = 40 * 1024 * 1024
    block = (AZ, 5, 16, 128)
    dma = pltpu.SemaphoreType.DMA
    fields = [pltpu.VMEM(v.shape, f32) for v in (density, velocity, energy)]
    back = pl.pallas_call(
        kernel,
        out_shape=pltpu.VMEM(block, f32),
        in_specs=[hbm] * 5,
        out_specs=hbm,
        scratch_shapes=fields + [
            pltpu.SMEM(shifts.shape, jnp.int32),
            pltpu.SMEM(fraction.shape, f32),
            pltpu.VMEM(block, f32),
            pltpu.VMEM((5, PADDED, 128), f32),
            pltpu.VMEM((4, 6, 8, CHUNKS, 128), f32),
            pltpu.VMEM((4, 6, 8, CHUNKS, 128), f32),
            pltpu.VMEM((5, 4, 6, CHUNKS, 128), f32),
            pltpu.VMEM((5, 4, 6, CHUNKS, 128), f32),
            pltpu.VMEM((8, CHUNKS, 128), f32),
            pltpu.VMEM((8, CHUNKS, 128), f32),
            pltpu.VMEM((8, CHUNKS, 128), f32),
            pltpu.VMEM((5, 8, CHUNKS, 128), f32),
            pltpu.VMEM((5, 8, 2 * CHUNKS, 128), f32),
            pltpu.VMEM((5, PADDED, 128), f32),
            dma((2, AZ)),
            dma((2,)),
            dma((10, 4)),
            dma((10, 4)),
            dma((2, AZ)),
            dma((2,)),
            dma((4,)),
            dma((5,)),
        ],
        compiler_params=pltpu.CompilerParams(collective_id=0, has_side_effects=True, vmem_limit_bytes=limit),
    )(*(pltpu.with_memory_space_constraint(v, pltpu.HBM) for v in (density, velocity, energy, shifts, fraction)))
    return pl.pallas_call(
        write_out,
        out_shape=tuple(jax.ShapeDtypeStruct(v.shape, f32) for v in (density, velocity, energy)),
        in_specs=[pl.BlockSpec(memory_space=pltpu.VMEM)],
        out_specs=(hbm,) * 3,
        scratch_shapes=fields + [dma((5,))],
        compiler_params=pltpu.CompilerParams(vmem_limit_bytes=16 * 1024 * 1024),
    )(pltpu.with_memory_space_constraint(back, pltpu.VMEM))


def solution(mesh):
    placed = (
        P(None, "rad", "az"),
        P(None, None, "rad", "az"),
        P(None, "rad", "az"),
        P("rad"),
        P("rad"),
    )
    return jax.shard_map(
        shards,
        mesh=mesh,
        in_specs=placed,
        out_specs=(P(None, "rad", "az"), P(None, None, "rad", "az"), P(None, "rad", "az")),
        check_vma=False,
    )
```
